128 devices in a mesh: dp: 32 (over x, z, core), row: 2 (over y_hi), col: 2 (over y_lo).
Axes of the slice: x: 4, y: 4 (y_hi: 2, y_lo: 2; y = y_hi * 2 + y_lo), z: 4, core: 2. Of those that a mesh axis runs over, the one named last changes fastest.
Arguments:
- tokens: bfloat16 [32768, 768], P(('dp', 'row'), 'col'), may hold values from -1.796875 to 1.796875
- ln1_gain: float32 [2, 768], P(None, 'col'), may hold values from 0.25 to 3.5
- ln1_shift: float32 [2, 768], P(None, 'col'), may hold values from -3 to 3
- w_query: bfloat16 [2, 768, 768], P(None, 'col', 'row'), may hold values from -0.21875 to 0.21875
- w_key: bfloat16 [2, 768, 768], P(None, 'col', 'row'), may hold values from -0.21875 to 0.21875
- w_value: bfloat16 [2, 768, 768], P(None, 'col', 'row'), may hold values from -0.21875 to 0.21875
- query_gain: float32 [2, 64], replicated, may hold values from 0.25 to 1.75
- key_gain: float32 [2, 64], replicated, may hold values from 0.25 to 1.75
- w_out: bfloat16 [2, 768, 768], P(None, 'row', 'col'), may hold values from -0.875 to 0.875
- ln2_gain: float32 [2, 768], P(None, 'col'), may hold values from 0.25 to 3.5
- ln2_shift: float32 [2, 768], P(None, 'col'), may hold values from -3 to 3
- w_up: bfloat16 [2, 768, 3072], P(None, 'col', 'row'), may hold values from -0.21875 to 0.21875
- up_bias: float32 [2, 3072], P(None, 'row'), may hold values from -3 to 3
- w_down: bfloat16 [2, 3072, 768], P(None, 'row', 'col'), may hold values from -0.109375 to 0.109375
- down_bias: float32 [2, 768], P(None, 'col'), may hold values from -3 to 3
- cotangent: bfloat16 [32768, 768], P(('dp', 'row'), 'col'), may hold values from -6 to 6
Outputs:
- out: bfloat16 [32768, 768], P(('dp', 'row'), 'col')
- grad_tokens: float32 [32768, 768], P(('dp', 'row'), 'col')
- grad_ln1_gain: float32 [2, 768], P(None, 'col')
- grad_ln1_shift: float32 [2, 768], P(None, 'col')
- grad_w_query: float32 [2, 768, 768], P(None, 'col', 'row')
- grad_w_key: float32 [2, 768, 768], P(None, 'col', 'row')
- grad_w_value: float32 [2, 768, 768], P(None, 'col', 'row')
- grad_query_gain: float32 [2, 64], replicated
- grad_key_gain: float32 [2, 64], replicated
- grad_w_out: float32 [2, 768, 768], P(None, 'row', 'col')
- grad_ln2_gain: float32 [2, 768], P(None, 'col')
- grad_ln2_shift: float32 [2, 768], P(None, 'col')
- grad_w_up: float32 [2, 768, 3072], P(None, 'col', 'row')
- grad_up_bias: float32 [2, 3072], P(None, 'row')
- grad_w_down: float32 [2, 3072, 768], P(None, 'row', 'col')
- grad_down_bias: float32 [2, 768], P(None, 'col')
The draws below stay inside these ranges and needn't reach their ends.
All inputs are finite; a program needn't handle non-finite values.
Results may differ from the reference program's by a relative error of at most 0.04.
Values may be sent and summed in bfloat16 or wider, within the bound.
A program may use at most 256 MiB of HBM per device.

```python
import jax
import jax.numpy as jnp
from jax import lax

D = 768
HEADS = 12
HEAD_DIM = 64
FF = 3072
LAYERS = 2
PATCHES = 1024
TOKENS = 32768
N_DP = 32


def ramp_gain(key, start, finish, rough):
    place = jnp.arange(D, dtype=jnp.float32) / (D - 1)
    base = start * jnp.exp(place * jnp.log(finish / start))
    return base[None, :] * rough


def draw_ln1_gain(key, part):
    key = jax.random.fold_in(key, 11)
    rough = 1.0 + 0.08 * jnp.clip(jax.random.normal(key, (LAYERS, D), jnp.float32), -3.0, 3.0)
    return ramp_gain(key, 0.4, 2.0, rough)


def draw_ln2_gain(key, part):
    key = jax.random.fold_in(key, 12)
    rough = 1.0 + 0.08 * jnp.clip(jax.random.normal(key, (LAYERS, D), jnp.float32), -3.0, 3.0)
    return ramp_gain(key, 0.4, 2.0, rough)


def steps_of(own_key, dims, shards, smallest, high):
    def one(axis_at, blocks):
        heights = jax.random.uniform(jax.random.fold_in(jax.random.fold_in(own_key, 6), axis_at), (blocks,), jnp.float32, smallest / len(shards), high / len(shards))
        return jnp.repeat(jnp.exp(heights), dims[axis_at] // blocks).reshape((-1,) + (1,) * (len(dims) - axis_at - 1))

    level = one(*shards[0])
    for cut in shards[1:]:
        level = level * one(*cut)
    return level


def normal_values(stream_key, extent, scale, most, pieces=(), kind=jnp.bfloat16):
    values = scale * jax.random.normal(stream_key, extent, jnp.float32)
    if pieces:
        values = values * steps_of(stream_key, extent, pieces, -0.22, 0.18)
    return jnp.clip(values, -most, most).astype(kind)


def setup_inputs(seed: int = 0) -> dict:
    key_of = jax.random.split(jax.random.key(seed), 17)
    return {
        "tokens": normal_values(key_of[0], (TOKENS, D), 0.3, 1.796875, ((0, 64), (1, 2))),
        "ln1_gain": draw_ln1_gain(jax.random.fold_in(key_of[16], 71), 0),
        "ln1_shift": normal_values(key_of[2], (LAYERS, D), 0.3, 3.0, ((1, 2),), jnp.float32),
        "w_query": normal_values(key_of[3], (LAYERS, D, D), D ** -0.5, 0.21875, ((1, 2), (2, 2))),
        "w_key": normal_values(key_of[4], (LAYERS, D, D), D ** -0.5, 0.21875, ((1, 2), (2, 2))),
        "w_value": normal_values(key_of[5], (LAYERS, D, D), D ** -0.5, 0.21875, ((1, 2), (2, 2))),
        "query_gain": jnp.clip(1.0 + 0.15 * jax.random.normal(key_of[6], (LAYERS, HEAD_DIM), jnp.float32), 0.25, 1.75),
        "key_gain": jnp.clip(1.0 + 0.15 * jax.random.normal(key_of[7], (LAYERS, HEAD_DIM), jnp.float32), 0.25, 1.75),
        "w_out": normal_values(key_of[8], (LAYERS, D, D), (D // 16) ** -0.5, 0.875, ((1, 2), (2, 2))),
        "ln2_gain": draw_ln2_gain(jax.random.fold_in(key_of[16], 71), 0),
        "ln2_shift": normal_values(key_of[10], (LAYERS, D), 0.3, 3.0, ((1, 2),), jnp.float32),
        "w_up": normal_values(key_of[11], (LAYERS, D, FF), D ** -0.5, 0.21875, ((1, 2), (2, 2))),
        "up_bias": normal_values(key_of[12], (LAYERS, FF), 0.5, 3.0, ((1, 2),), jnp.float32),
        "w_down": normal_values(key_of[13], (LAYERS, FF, D), FF ** -0.5, 0.109375, ((1, 2), (2, 2))),
        "down_bias": normal_values(key_of[14], (LAYERS, D), 0.5, 3.0, ((1, 2),), jnp.float32),
        "cotangent": normal_values(key_of[15], (TOKENS, D), 1.0, 6.0, ((0, 64), (1, 2))),
    }


EPS = 1e-06
HIGHEST = lax.Precision.HIGHEST

@jax.custom_vjp
def low(v):
    return lax.optimization_barrier(v.astype(jnp.bfloat16)).astype(jnp.float32)

@jax.custom_vjp
def low_back(v):
    return v

def low_keep(v):
    return (low(v), None)

def low_pass(kept, grad):
    return (grad,)

def back_keep(v):
    return (v, None)

def back_low(kept, grad):
    return (low(grad),)
low.defvjp(low_keep, low_pass)
low_back.defvjp(back_keep, back_low)

def mult(left, right):
    return jnp.dot(left, right, precision=HIGHEST)

def layer_norm(resid, gain, shift):
    mean = lax.optimization_barrier(jnp.mean(resid, axis=-1, keepdims=True))
    centred = resid - mean
    spread = lax.optimization_barrier(jnp.mean(centred * centred, axis=-1, keepdims=True))
    return centred * lax.rsqrt(spread + EPS) * gain + shift

def one_block(query_block, key_all, value_all):
    factor = HEAD_DIM ** (-0.5)
    scores = low_back(jnp.einsum('qhd,khd->hqk', query_block, key_all, precision=HIGHEST) * factor)
    probs = low(jax.nn.softmax(scores, axis=-1))
    return jnp.einsum('hqk,khd->qhd', probs, value_all, precision=HIGHEST)

def attend(queries, keys, values):
    length = queries.shape[0]
    block = min(512, length)
    checked = jax.checkpoint(one_block)
    blocks = queries.reshape(length // block, block, HEADS, HEAD_DIM)
    mixed = lax.map(lambda query_block: checked(query_block, keys, values), blocks)
    return mixed.reshape(length, HEADS * HEAD_DIM)

def layer(resid, weights):
    gain_one, shift_one, w_query, w_key, w_value, query_gain, key_gain, w_out, gain_two, shift_two, w_up, up_bias, w_down, down_bias = weights
    length = resid.shape[0]
    normed = low(layer_norm(resid, gain_one, shift_one))
    query_raw = low_back(mult(normed, w_query)).reshape(length, HEADS, HEAD_DIM)
    key_raw = low_back(mult(normed, w_key)).reshape(length, HEADS, HEAD_DIM)
    value_raw = low_back(mult(normed, w_value))
    queries = low(layer_norm(query_raw, query_gain, 0.0))
    keys = low(layer_norm(key_raw, key_gain, 0.0))
    values = low(value_raw).reshape(length, HEADS, HEAD_DIM)
    mixed = low(low_back(attend(queries, keys, values)))
    resid_two = resid + low_back(mult(mixed, w_out))
    normed_two = low(layer_norm(resid_two, gain_two, shift_two))
    hidden = low_back(mult(normed_two, w_up) + up_bias)
    active = low(jax.nn.gelu(hidden, approximate=True))
    return resid_two + low_back(mult(active, w_down) + down_bias)

def reference(tokens, ln1_gain, ln1_shift, w_query, w_key, w_value, query_gain, key_gain, w_out, ln2_gain, ln2_shift, w_up, up_bias, w_down, down_bias, cotangent):
    params = tuple((item.astype(jnp.float32) for item in (ln1_gain, ln1_shift, w_query, w_key, w_value, query_gain, key_gain, w_out, ln2_gain, ln2_shift, w_up, up_bias, w_down, down_bias)))
    images = tokens.astype(jnp.float32).reshape(N_DP, PATCHES, D)
    seeds = cotangent.astype(jnp.float32).reshape(N_DP, PATCHES, D)

    def forward(image_all, weights_all):

        def per_image(carry, image):
            resid = image
            for layer_at in range(LAYERS):
                resid = layer(resid, tuple((item[layer_at] for item in weights_all)))
            return (carry, resid)
        return lax.scan(jax.checkpoint(per_image), jnp.zeros((), jnp.float32), image_all)[1]
    result, pull = jax.vjp(forward, images, params)
    grad_images, grads = pull(seeds)
    return (result.reshape(TOKENS, D).astype(jnp.bfloat16), grad_images.reshape(TOKENS, D), grads[0], grads[1], grads[2], grads[3], grads[4], grads[5], grads[6], grads[7], grads[8], grads[9], grads[10], grads[11], grads[12], grads[13])
```

```python
import functools

import jax
import jax.numpy as jnp
from jax import lax
from jax.experimental import pallas as pl
from jax.experimental.pallas import tpu as pltpu
from jax.sharding import Mesh, PartitionSpec as P

HEAD_DIM = 64
EPS = 1e-06
LOG2E = 1.4426950408889634
BF = jnp.bfloat16
F32 = jnp.float32
GROUP = ("core", "row", "col")
BLOCK = 256


def place(core, row, col):
    return core * 4 + row * 2 + col


SPOTS = [(c, r, q) for c in range(2) for r in range(2) for q in range(2)]
OWN_IN = [(place(c, r, q), place(r, q ^ c, q)) for c, r, q in SPOTS]
OTHER_IN = [(place(c, r, q), place(r, 1 ^ q ^ c, 1 ^ q)) for c, r, q in SPOTS]
OWN_OUT = [(b, a) for a, b in OWN_IN]
CROSS = [(0, 3), (3, 0), (1, 2), (2, 1)]


def swap_core(value):
    return lax.ppermute(value, "core", [(0, 1), (1, 0)])


def swap_col(value):
    return lax.ppermute(value, "col", [(0, 1), (1, 0)])


def swap_cross(value):
    return lax.ppermute(value, ("row", "col"), CROSS)


def flip(value, axis):
    first, second = jnp.split(value, 2, axis=axis)
    return jnp.concatenate((second, first), axis=axis)


def dot(left, right, left_axis=1, right_axis=0):
    return lax.dot_general(
        left, right, (((left_axis,), (right_axis,)), ((), ())), preferred_element_type=F32
    )


def gather_core(value):
    return jnp.concatenate((value, swap_core(value)), axis=0)


def total_group(partial):
    rows = partial.shape[0] // 2
    chip = partial[:rows] + swap_core(partial[rows:].astype(BF)).astype(F32)
    return chip + flip(swap_cross(chip.astype(BF)), 1).astype(F32)


def norm(resid, gain, shift):
    mean = jnp.mean(resid, axis=1, keepdims=True)
    centred = resid - mean
    factor = lax.rsqrt(jnp.mean(centred * centred, axis=1, keepdims=True) + EPS)
    normal = centred * factor
    return normal, factor, (normal * gain + shift).astype(BF)


def norm_back(grad, normal, factor, gain):
    scaled = grad * gain
    first = jnp.mean(scaled, axis=1, keepdims=True)
    second = jnp.mean(scaled * normal, axis=1, keepdims=True)
    return factor * (scaled - first - normal * second)


def head_norm(values):
    mean = jnp.mean(values, axis=0, keepdims=True)
    centred = values - mean
    factor = lax.rsqrt(jnp.mean(centred * centred, axis=0, keepdims=True) + EPS)
    return centred * factor, factor


def head_norm_back(grad, normal, factor, gain):
    scaled = grad * gain
    first = jnp.mean(scaled, axis=0, keepdims=True)
    second = jnp.mean(scaled * normal, axis=0, keepdims=True)
    return factor * (scaled - first - normal * second)


SCALE2 = LOG2E * HEAD_DIM ** (-0.5)


def attend_kernel(qkv_ref, gain_ref, mixed_ref, total_ref):
    gains = gain_ref[...]
    query = (head_norm(qkv_ref[0, 0])[0] * gains[:, 0:1]).astype(BF)
    key_rows = (head_norm(qkv_ref[1, 0])[0] * gains[:, 1:2]).T.astype(BF)
    value = qkv_ref[2, 0].astype(BF)
    for at in range(0, query.shape[1], BLOCK):
        expo = jnp.exp2(dot(key_rows, query[:, at : at + BLOCK]) * SCALE2)
        total = jnp.sum(expo, axis=0, keepdims=True)
        mixed = dot(value, expo.astype(BF))
        mixed_ref[0, :, at : at + BLOCK] = (mixed * (1.0 / total)).astype(BF)
        total_ref[0, :, at : at + BLOCK] = jnp.log2(total)


def attend(qkv, gains):
    heads, rows = qkv.shape[1], qkv.shape[3]
    return pl.pallas_call(
        attend_kernel,
        grid=(heads,),
        in_specs=[
            pl.BlockSpec((3, 1, HEAD_DIM, rows), lambda h: (0, h, 0, 0)),
            pl.BlockSpec((HEAD_DIM, 2), lambda h: (0, 0)),
        ],
        out_specs=[
            pl.BlockSpec((1, HEAD_DIM, rows), lambda h: (h, 0, 0)),
            pl.BlockSpec((1, 1, rows), lambda h: (h, 0, 0)),
        ],
        out_shape=[
            jax.ShapeDtypeStruct((heads, HEAD_DIM, rows), BF),
            jax.ShapeDtypeStruct((heads, 1, rows), F32),
        ],
        compiler_params=pltpu.CompilerParams(vmem_limit_bytes=40 * 2**20),
        cost_estimate=pl.CostEstimate(
            flops=16 * heads * rows * rows * HEAD_DIM,
            bytes_accessed=heads * rows * HEAD_DIM * 16,
            transcendentals=heads * rows * rows,
        ),
        name="attend",
    )(qkv, gains)


def attend_back_kernel(qkv_ref, gain_ref, total_ref, grad_ref, out_ref, gain_out_ref):
    gains = gain_ref[...]
    query_normal, query_factor = head_norm(qkv_ref[0, 0])
    key_normal, key_factor = head_norm(qkv_ref[1, 0])
    query = (query_normal * gains[:, 0:1]).astype(BF)
    key_full = key_normal * gains[:, 1:2]
    key = key_full.astype(BF)
    key_rows = key_full.T.astype(BF)
    value_rows = qkv_ref[2, 0].T.astype(BF)
    key_sum = jnp.zeros(key.shape, F32)
    value_sum = jnp.zeros(key.shape, F32)
    query_parts = []
    for at in range(0, query.shape[1], BLOCK):
        here = slice(at, at + BLOCK)
        grad = grad_ref[0, :, here]
        probs = jnp.exp2(dot(key_rows, query[:, here]) * SCALE2 - total_ref[0, :, here])
        pulled = dot(value_rows, grad)
        delta = jnp.sum(probs * pulled, axis=0, keepdims=True)
        score_grad = (probs * (pulled - delta)).astype(BF)
        query_parts.append(dot(key, score_grad))
        key_sum = key_sum + dot(query[:, here], score_grad, 1, 1)
        value_sum = value_sum + dot(grad, probs.astype(BF), 1, 1)
    scale = HEAD_DIM ** (-0.5)
    query_sum = jnp.concatenate(query_parts, axis=1) * scale
    key_sum = key_sum * scale
    out_ref[0, 0] = head_norm_back(query_sum, query_normal, query_factor, gains[:, 0:1]).astype(BF)
    out_ref[1, 0] = head_norm_back(key_sum, key_normal, key_factor, gains[:, 1:2]).astype(BF)
    out_ref[2, 0] = value_sum.astype(BF)
    gain_out_ref[0] = jnp.concatenate(
        (
            jnp.sum(query_sum * query_normal, axis=1, keepdims=True),
            jnp.sum(key_sum * key_normal, axis=1, keepdims=True),
        ),
        axis=1,
    )


def attend_back(qkv, gains, total, grad):
    heads, rows = qkv.shape[1], qkv.shape[3]
    return pl.pallas_call(
        attend_back_kernel,
        grid=(heads,),
        in_specs=[
            pl.BlockSpec((3, 1, HEAD_DIM, rows), lambda h: (0, h, 0, 0)),
            pl.BlockSpec((HEAD_DIM, 2), lambda h: (0, 0)),
            pl.BlockSpec((1, 1, rows), lambda h: (h, 0, 0)),
            pl.BlockSpec((1, HEAD_DIM, rows), lambda h: (h, 0, 0)),
        ],
        out_specs=[
            pl.BlockSpec((3, 1, HEAD_DIM, rows), lambda h: (0, h, 0, 0)),
            pl.BlockSpec((1, HEAD_DIM, 2), lambda h: (h, 0, 0)),
        ],
        out_shape=[
            jax.ShapeDtypeStruct((3, heads, HEAD_DIM, rows), BF),
            jax.ShapeDtypeStruct((heads, HEAD_DIM, 2), F32),
        ],
        compiler_params=pltpu.CompilerParams(vmem_limit_bytes=48 * 2**20),
        cost_estimate=pl.CostEstimate(
            flops=40 * heads * rows * rows * HEAD_DIM,
            bytes_accessed=heads * rows * HEAD_DIM * 24,
            transcendentals=heads * rows * rows,
        ),
        name="attend_back",
    )(qkv, gains, total, grad)


def gelu_parts(hidden):
    square = hidden * hidden
    bent = jnp.tanh(0.7978845608 * hidden * (1.0 + 0.044715 * square))
    active = 0.5 * hidden * (1.0 + bent)
    slope = 0.5 * (1.0 + bent) + 0.5 * hidden * (1.0 - bent * bent) * (
        0.7978845608 * (1.0 + 3.0 * 0.044715 * square)
    )
    return active, slope


def layer_forward(resid, weights):
    w_qkv, gains, w_out, w_up, up_bias, w_down, vectors = weights
    rows = resid.shape[0]
    normal_one, factor_one, normed_one = norm(resid, vectors[0], vectors[1])
    seen_one = gather_core(normed_one)
    qkv = dot(w_qkv, seen_one, 1, 1).reshape(3, -1, HEAD_DIM, 2 * rows)
    mixed, total = attend(qkv, gains)
    mine = mixed.reshape(-1, 2 * rows)
    chip = jnp.concatenate((mine[:, :rows], swap_core(mine[:, rows:])), axis=0)
    joined = jnp.concatenate((chip, swap_cross(chip)), axis=0)
    resid_two = resid + dot(joined, w_out, 0, 0)
    normal_two, factor_two, normed_two = norm(resid_two, vectors[2], vectors[3])
    seen_two = gather_core(normed_two)
    hidden = dot(seen_two, w_up) + up_bias
    active = gelu_parts(hidden)[0].astype(BF)
    result = (resid_two + vectors[4]) + total_group(dot(active, w_down))
    cache = (
        normal_one, factor_one, seen_one, qkv, mixed, total,
        normal_two, factor_two, seen_two, hidden, active,
    )
    return result, cache


def layer_backward(grad, cache, weights, w_out_mine):
    w_qkv, gains, w_out, w_up, up_bias, w_down, vectors = weights
    (
        normal_one, factor_one, seen_one, qkv, mixed, total,
        normal_two, factor_two, seen_two, hidden, active,
    ) = cache
    rows = grad.shape[0]
    branch = grad.astype(BF)
    seen_branch = gather_core(branch)
    active_grad = dot(seen_branch, w_down, 1, 1)
    hidden_grad = (active_grad * gelu_parts(hidden)[1]).astype(BF)
    normed_two_grad = total_group(dot(hidden_grad, w_up, 1, 1))
    grad_down = dot(active, seen_branch, 0, 0)
    grad_up = dot(hidden_grad, seen_two, 0, 0)
    bias_up = jnp.sum(hidden_grad.astype(F32), axis=0)
    bias_down = jnp.sum(branch.astype(F32), axis=0)
    gain_two = jnp.sum(normed_two_grad * normal_two, axis=0)
    shift_two = jnp.sum(normed_two_grad, axis=0)
    resid_two_grad = grad + norm_back(normed_two_grad, normal_two, factor_two, vectors[2])
    seen_proj = gather_core(resid_two_grad.astype(BF))
    mine = mixed.reshape(-1, 2 * rows)
    mixed_grad = dot(w_out_mine, seen_proj, 1, 1).astype(BF).reshape(mixed.shape)
    grad_out = dot(mine, seen_proj)
    qkv_grad, gains_grad = attend_back(qkv, gains, total, mixed_grad)
    qkv_grad = qkv_grad.reshape(-1, 2 * rows)
    normed_one_grad = total_group(dot(qkv_grad, w_qkv, 0, 0))
    grad_qkv = dot(qkv_grad, seen_one)
    gain_one = jnp.sum(normed_one_grad * normal_one, axis=0)
    shift_one = jnp.sum(normed_one_grad, axis=0)
    resid_grad = resid_two_grad + norm_back(normed_one_grad, normal_one, factor_one, vectors[0])
    gains_grad = jnp.sum(gains_grad, axis=0).T.reshape(-1)
    small = jnp.stack((gain_one, shift_one, gain_two, shift_two, bias_down))
    return resid_grad, (grad_up, grad_down, grad_qkv, grad_out, small, bias_up, gains_grad)


def reduce_grads(grads):
    grad_up, grad_down, grad_qkv, grad_out, small, bias_up, gains_grad = grads
    half = grad_up.shape[1] // 2
    gains_low = gains_grad.astype(BF)
    gains_sum = gains_low.astype(F32) + swap_cross(gains_low).astype(F32)
    shared = jnp.concatenate(
        (
            bias_up.reshape(2, half),
            jnp.pad(gains_sum, (0, half - gains_sum.shape[0]))[None],
            jnp.zeros((8, half), F32),
        ),
        axis=0,
    )
    whole = jnp.concatenate((grad_up, grad_down, grad_qkv, grad_out, small), axis=0).astype(BF)
    shared = shared.astype(BF)
    other = jnp.concatenate((whole[:, half:], shared), axis=0)
    own = jnp.concatenate((whole[:, :half], shared), axis=0)
    summed = own.astype(F32) + swap_col(other).astype(F32)
    return summed.astype(BF)


def shards(
    tokens, ln1_gain, ln1_shift, w_query, w_key, w_value, query_gain, key_gain, w_out,
    ln2_gain, ln2_shift, w_up, up_bias, w_down, down_bias, cotangent,
):
    core = lax.axis_index("core")
    layers = w_query.shape[0]
    heads_here = w_query.shape[2] // 2
    units_here = w_up.shape[2] // 2

    def take(value, size, axis):
        return lax.dynamic_slice_in_dim(value, core * size, size, axis)

    def both(own, axis):
        return jnp.concatenate((own, swap_col(own)), axis=axis)

    def arrive(value):
        return jnp.concatenate(
            (lax.ppermute(value, GROUP, OWN_IN), lax.ppermute(value, GROUP, OTHER_IN)), axis=1
        ).astype(F32)

    resid = arrive(tokens)
    vectors = both(jnp.stack((ln1_gain, ln1_shift, ln2_gain, ln2_shift, down_bias), axis=1), 2)
    up_bias_here = take(up_bias, units_here, 1)
    weights, mine_out = [], []
    for at in range(layers):
        qkv_here = jnp.concatenate(
            [take(w[at], heads_here, 1).T for w in (w_query, w_key, w_value)], axis=0
        )
        out_here = both(take(w_out[at], heads_here, 0), 1)
        out_chip = jnp.concatenate((out_here, swap_core(out_here)), axis=0)
        out_all = jnp.concatenate((out_chip, flip(swap_cross(out_chip), 1)), axis=0)
        weights.append(
            (
                both(qkv_here, 1),
                jnp.stack((query_gain[at], key_gain[at]), axis=1),
                out_all,
                both(take(w_up[at], units_here, 1), 0),
                up_bias_here[at],
                both(take(w_down[at], units_here, 0), 1),
                vectors[at],
            )
        )
        mine_out.append(out_here)
    caches = []
    for at in range(layers):
        resid, cache = layer_forward(resid, weights[at])
        caches.append(cache)
    half = resid.shape[1] // 2
    result = lax.ppermute(resid[:, :half].astype(BF), GROUP, OWN_OUT)
    grad = arrive(cotangent)
    summed = [None] * layers
    for at in reversed(range(layers)):
        grad, grads = layer_backward(grad, caches[at], weights[at], mine_out[at])
        summed[at] = lax.psum(reduce_grads(grads), ("x", "z"))
    grad_tokens = lax.ppermute(grad[:, :half].astype(BF), GROUP, OWN_OUT).astype(F32)
    total = jnp.stack(summed)
    partner = swap_core(total)
    first = jnp.where(core == 0, total, partner).astype(F32)
    second = jnp.where(core == 0, partner, total).astype(F32)
    at_up, at_down = 0, units_here
    at_qkv = 2 * units_here
    at_out = at_qkv + 3 * heads_here
    at_small = at_out + heads_here

    def pair(start, size, axis):
        return jnp.concatenate(
            (first[:, start : start + size], second[:, start : start + size]), axis=axis
        )

    grad_up = jnp.swapaxes(pair(at_up, units_here, 1), 1, 2)
    grad_down = pair(at_down, units_here, 1)
    grad_q, grad_k, grad_v = (
        jnp.swapaxes(pair(at_qkv + i * heads_here, heads_here, 1), 1, 2) for i in range(3)
    )
    grad_out = pair(at_out, heads_here, 1)
    both_small = first[:, at_small : at_small + 8] + second[:, at_small : at_small + 8]
    bias_up = pair(at_small + 5, 2, 1).reshape(layers, -1)
    return (
        result,
        grad_tokens,
        both_small[:, 0],
        both_small[:, 1],
        grad_q,
        grad_k,
        grad_v,
        both_small[:, 7, :HEAD_DIM],
        both_small[:, 7, HEAD_DIM : 2 * HEAD_DIM],
        grad_out,
        both_small[:, 2],
        both_small[:, 3],
        grad_up,
        bias_up,
        grad_down,
        both_small[:, 4],
    )


def solution(mesh):
    fine = Mesh(mesh.devices.reshape(4, 4, 2, 2, 2), ("x", "z", "core", "row", "col"))
    rows = ("x", "z", "core", "row")
    in_specs = (
        P(rows, "col"),
        P(None, "col"),
        P(None, "col"),
        P(None, "col", "row"),
        P(None, "col", "row"),
        P(None, "col", "row"),
        P(),
        P(),
        P(None, "row", "col"),
        P(None, "col"),
        P(None, "col"),
        P(None, "col", "row"),
        P(None, "row"),
        P(None, "row", "col"),
        P(None, "col"),
        P(rows, "col"),
    )
    out_specs = (P(rows, "col"),) * 2 + in_specs[1:15]
    return jax.shard_map(shards, mesh=fine, in_specs=in_specs, out_specs=out_specs, check_vma=False)
```

```python
import functools

import jax
import jax.numpy as jnp
from jax import lax
from jax.experimental import pallas as pl
from jax.experimental.pallas import tpu as pltpu
from jax.sharding import Mesh, PartitionSpec as P

HEAD_DIM = 64
EPS = 1e-06
LOG2E = 1.4426950408889634
BF = jnp.bfloat16
F32 = jnp.float32
GROUP = ("core", "row", "col")
BLOCK = 256


def place(core, row, col):
    return core * 4 + row * 2 + col


SPOTS = [(c, r, q) for c in range(2) for r in range(2) for q in range(2)]
OWN_IN = [(place(c, r, q), place(r, q ^ c, q)) for c, r, q in SPOTS]
OTHER_IN = [(place(c, r, q), place(r, 1 ^ q ^ c, 1 ^ q)) for c, r, q in SPOTS]
OWN_OUT = [(b, a) for a, b in OWN_IN]
CROSS = [(0, 3), (3, 0), (1, 2), (2, 1)]


def swap_core(value):
    return lax.ppermute(value, "core", [(0, 1), (1, 0)])


def swap_col(value):
    return lax.ppermute(value, "col", [(0, 1), (1, 0)])


def swap_cross(value):
    return lax.ppermute(value, ("row", "col"), CROSS)


def flip(value, axis):
    first, second = jnp.split(value, 2, axis=axis)
    return jnp.concatenate((second, first), axis=axis)


def dot(left, right, left_axis=1, right_axis=0):
    return lax.dot_general(
        left, right, (((left_axis,), (right_axis,)), ((), ())), preferred_element_type=F32
    )


def gather_core(value):
    return jnp.concatenate((value, swap_core(value)), axis=0)


def total_group(partial):
    rows = partial.shape[0] // 2
    chip = partial[:rows] + swap_core(partial[rows:].astype(BF)).astype(F32)
    return chip + flip(swap_cross(chip.astype(BF)), 1).astype(F32)


def norm(resid, gain, shift):
    mean = jnp.mean(resid, axis=1, keepdims=True)
    centred = resid - mean
    factor = lax.rsqrt(jnp.mean(centred * centred, axis=1, keepdims=True) + EPS)
    normal = centred * factor
    return normal, factor, (normal * gain + shift).astype(BF)


def norm_back(grad, normal, factor, gain):
    scaled = grad * gain
    first = jnp.mean(scaled, axis=1, keepdims=True)
    second = jnp.mean(scaled * normal, axis=1, keepdims=True)
    return factor * (scaled - first - normal * second)


def head_norm(values):
    mean = jnp.mean(values, axis=0, keepdims=True)
    centred = values - mean
    factor = lax.rsqrt(jnp.mean(centred * centred, axis=0, keepdims=True) + EPS)
    return centred * factor, factor


def head_norm_back(grad, normal, factor, gain):
    scaled = grad * gain
    first = jnp.mean(scaled, axis=0, keepdims=True)
    second = jnp.mean(scaled * normal, axis=0, keepdims=True)
    return factor * (scaled - first - normal * second)


SCALE2 = LOG2E * HEAD_DIM ** (-0.5)


def attend_kernel(qkv_ref, gain_ref, mixed_ref, total_ref):
    gains = gain_ref[...]
    query = (head_norm(qkv_ref[0, 0])[0] * gains[:, 0:1]).astype(BF)
    key_rows = (head_norm(qkv_ref[1, 0])[0] * gains[:, 1:2]).T.astype(BF)
    value = qkv_ref[2, 0].astype(BF)
    for at in range(0, query.shape[1], BLOCK):
        expo = jnp.exp2(dot(key_rows, query[:, at : at + BLOCK]) * SCALE2)
        total = jnp.sum(expo, axis=0, keepdims=True)
        mixed = dot(value, expo.astype(BF))
        mixed_ref[0, :, at : at + BLOCK] = (mixed * (1.0 / total)).astype(BF)
        total_ref[0, :, at : at + BLOCK] = jnp.log2(total)


def attend(qkv, gains):
    heads, rows = qkv.shape[1], qkv.shape[3]
    return pl.pallas_call(
        attend_kernel,
        grid=(heads,),
        in_specs=[
            pl.BlockSpec((3, 1, HEAD_DIM, rows), lambda h: (0, h, 0, 0)),
            pl.BlockSpec((HEAD_DIM, 2), lambda h: (0, 0)),
        ],
        out_specs=[
            pl.BlockSpec((1, HEAD_DIM, rows), lambda h: (h, 0, 0)),
            pl.BlockSpec((1, 1, rows), lambda h: (h, 0, 0)),
        ],
        out_shape=[
            jax.ShapeDtypeStruct((heads, HEAD_DIM, rows), BF),
            jax.ShapeDtypeStruct((heads, 1, rows), F32),
        ],
        compiler_params=pltpu.CompilerParams(vmem_limit_bytes=40 * 2**20),
        cost_estimate=pl.CostEstimate(
            flops=16 * heads * rows * rows * HEAD_DIM,
            bytes_accessed=heads * rows * HEAD_DIM * 16,
            transcendentals=heads * rows * rows,
        ),
        name="attend",
    )(qkv, gains)


def attend_back_kernel(qkv_ref, gain_ref, total_ref, grad_ref, out_ref, gain_out_ref):
    gains = gain_ref[...]
    query_normal, query_factor = head_norm(qkv_ref[0, 0])
    key_normal, key_factor = head_norm(qkv_ref[1, 0])
    query = (query_normal * gains[:, 0:1]).astype(BF)
    key_full = key_normal * gains[:, 1:2]
    key = key_full.astype(BF)
    key_rows = key_full.T.astype(BF)
    value_rows = qkv_ref[2, 0].T.astype(BF)
    key_sum = jnp.zeros(key.shape, F32)
    value_sum = jnp.zeros(key.shape, F32)
    query_parts = []
    for at in range(0, query.shape[1], BLOCK):
        here = slice(at, at + BLOCK)
        grad = grad_ref[0, :, here]
        probs = jnp.exp2(dot(key_rows, query[:, here]) * SCALE2 - total_ref[0, :, here])
        pulled = dot(value_rows, grad)
        delta = jnp.sum(probs * pulled, axis=0, keepdims=True)
        score_grad = (probs * (pulled - delta)).astype(BF)
        query_parts.append(dot(key, score_grad))
        key_sum = key_sum + dot(query[:, here], score_grad, 1, 1)
        value_sum = value_sum + dot(grad, probs.astype(BF), 1, 1)
    scale = HEAD_DIM ** (-0.5)
    query_sum = jnp.concatenate(query_parts, axis=1) * scale
    key_sum = key_sum * scale
    out_ref[0, 0] = head_norm_back(query_sum, query_normal, query_factor, gains[:, 0:1]).astype(BF)
    out_ref[1, 0] = head_norm_back(key_sum, key_normal, key_factor, gains[:, 1:2]).astype(BF)
    out_ref[2, 0] = value_sum.astype(BF)
    gain_out_ref[0] = jnp.concatenate(
        (
            jnp.sum(query_sum * query_normal, axis=1, keepdims=True),
            jnp.sum(key_sum * key_normal, axis=1, keepdims=True),
        ),
        axis=1,
    )


def attend_back(qkv, gains, total, grad):
    heads, rows = qkv.shape[1], qkv.shape[3]
    return pl.pallas_call(
        attend_back_kernel,
        grid=(heads,),
        in_specs=[
            pl.BlockSpec((3, 1, HEAD_DIM, rows), lambda h: (0, h, 0, 0)),
            pl.BlockSpec((HEAD_DIM, 2), lambda h: (0, 0)),
            pl.BlockSpec((1, 1, rows), lambda h: (h, 0, 0)),
            pl.BlockSpec((1, HEAD_DIM, rows), lambda h: (h, 0, 0)),
        ],
        out_specs=[
            pl.BlockSpec((3, 1, HEAD_DIM, rows), lambda h: (0, h, 0, 0)),
            pl.BlockSpec((1, HEAD_DIM, 2), lambda h: (h, 0, 0)),
        ],
        out_shape=[
            jax.ShapeDtypeStruct((3, heads, HEAD_DIM, rows), BF),
            jax.ShapeDtypeStruct((heads, HEAD_DIM, 2), F32),
        ],
        compiler_params=pltpu.CompilerParams(vmem_limit_bytes=48 * 2**20),
        cost_estimate=pl.CostEstimate(
            flops=40 * heads * rows * rows * HEAD_DIM,
            bytes_accessed=heads * rows * HEAD_DIM * 24,
            transcendentals=heads * rows * rows,
        ),
        name="attend_back",
    )(qkv, gains, total, grad)


def gelu_parts(hidden):
    square = hidden * hidden
    bent = jnp.tanh(0.7978845608 * hidden * (1.0 + 0.044715 * square))
    active = 0.5 * hidden * (1.0 + bent)
    slope = 0.5 * (1.0 + bent) + 0.5 * hidden * (1.0 - bent * bent) * (
        0.7978845608 * (1.0 + 3.0 * 0.044715 * square)
    )
    return active, slope


def layer_forward(resid, weights):
    w_qkv, gains, w_out, w_up, up_bias, w_down, vectors = weights
    rows = resid.shape[0]
    normal_one, factor_one, normed_one = norm(resid, vectors[0], vectors[1])
    seen_one = gather_core(normed_one)
    qkv = dot(w_qkv, seen_one, 1, 1).reshape(3, -1, HEAD_DIM, 2 * rows)
    mixed, total = attend(qkv, gains)
    mine = mixed.reshape(-1, 2 * rows)
    chip = jnp.concatenate((mine[:, :rows], swap_core(mine[:, rows:])), axis=0)
    joined = jnp.concatenate((chip, swap_cross(chip)), axis=0)
    resid_two = resid + dot(joined, w_out, 0, 0)
    normal_two, factor_two, normed_two = norm(resid_two, vectors[2], vectors[3])
    seen_two = gather_core(normed_two)
    hidden = dot(seen_two, w_up) + up_bias
    active = gelu_parts(hidden)[0].astype(BF)
    result = (resid_two + vectors[4]) + total_group(dot(active, w_down))
    cache = (
        normal_one, factor_one, seen_one, qkv, mixed, total,
        normal_two, factor_two, seen_two, hidden, active,
    )
    return result, cache


def layer_backward(grad, cache, weights, w_out_mine):
    w_qkv, gains, w_out, w_up, up_bias, w_down, vectors = weights
    (
        normal_one, factor_one, seen_one, qkv, mixed, total,
        normal_two, factor_two, seen_two, hidden, active,
    ) = cache
    rows = grad.shape[0]
    branch = grad.astype(BF)
    seen_branch = gather_core(branch)
    active_grad = dot(seen_branch, w_down, 1, 1)
    hidden_grad = (active_grad * gelu_parts(hidden)[1]).astype(BF)
    normed_two_grad = total_group(dot(hidden_grad, w_up, 1, 1))
    grad_down = dot(active, seen_branch, 0, 0)
    grad_up = dot(seen_two, hidden_grad, 0, 0)
    bias_up = jnp.sum(hidden_grad.astype(F32), axis=0)
    bias_down = jnp.sum(branch.astype(F32), axis=0)
    gain_two = jnp.sum(normed_two_grad * normal_two, axis=0)
    shift_two = jnp.sum(normed_two_grad, axis=0)
    resid_two_grad = grad + norm_back(normed_two_grad, normal_two, factor_two, vectors[2])
    seen_proj = gather_core(resid_two_grad.astype(BF))
    mine = mixed.reshape(-1, 2 * rows)
    mixed_grad = dot(w_out_mine, seen_proj, 1, 1).astype(BF).reshape(mixed.shape)
    grad_out = dot(mine, seen_proj)
    qkv_grad, gains_grad = attend_back(qkv, gains, total, mixed_grad)
    qkv_grad = qkv_grad.reshape(-1, 2 * rows)
    normed_one_grad = total_group(dot(qkv_grad, w_qkv, 0, 0))
    grad_qkv = dot(qkv_grad, seen_one)
    gain_one = jnp.sum(normed_one_grad * normal_one, axis=0)
    shift_one = jnp.sum(normed_one_grad, axis=0)
    resid_grad = resid_two_grad + norm_back(normed_one_grad, normal_one, factor_one, vectors[0])
    gains_grad = jnp.sum(gains_grad, axis=0).T.reshape(-1)
    small = jnp.stack((gain_one, shift_one, gain_two, shift_two, bias_down))
    return resid_grad, (grad_up, grad_down, grad_qkv, grad_out, small, bias_up, gains_grad)


def link_bits():
    x, z = lax.axis_index("x"), lax.axis_index("z")
    col = lax.axis_index("col")
    return {
        "x1": ({"x": x + 1 - 2 * (x % 2)}, ((x + 1) // 2) % 2),
        "x2": ({"x": 3 - x}, x // 2),
        "z1": ({"z": z + 1 - 2 * (z % 2)}, ((z + 1) // 2) % 2),
        "z2": ({"z": 3 - z}, z // 2),
        "col": ({"col": 1 - col}, None),
    }


ORDERS = (
    ("x1", "z1", "x2", "z2", "col"),
    ("z1", "x2", "z2", "col", "x1"),
    ("x2", "z2", "col", "x1", "z1"),
    ("z2", "col", "x1", "z1", "x2"),
    ("col", "x1", "z1", "x2", "z2"),
    ("x1", "z1", "x2", "z2", "col"),
    ("z1", "x2", "z2", "col", "x1"),
    ("x2", "z2", "col", "x1", "z1"),
    ("z2", "col", "x1", "z1", "x2"),
    ("col", "x2", "z2", "x1", "z1"),
)
UNIT = 256


def plan_chunks(rows):
    units = rows // UNIT
    count = min(units, len(ORDERS))
    sizes = [units // count + (1 if i < units % count else 0) for i in range(count)]
    chunks, start = [], 0
    for size, order in zip(sizes, ORDERS):
        chunks.append((start, size * UNIT, order))
        start += size * UNIT
    return chunks


def step_shapes(rows, order, width):
    shapes = []
    for link in order:
        if link == "col":
            width //= 2
        else:
            rows //= 2
        shapes.append((rows, width))
    return shapes


def add_into(target, other, row, col_size):
    rows = target.shape[0]
    block = min(rows, 64)

    @pl.loop(0, rows // block)
    def _(at):
        here = pl.ds(pl.multiple_of(at * block, block), block)
        there = pl.ds(pl.multiple_of(row + at * block, 16), block)
        target[here, :] = (
            target[here, :].astype(F32) + other[there, :col_size].astype(F32)
        ).astype(BF)


def reduce_kernel(chunks, copies, *refs):
    inputs = refs[: copies["inputs"]]
    both = refs[copies["inputs"]]
    scratch = list(refs[copies["inputs"] + 1 :])
    work = scratch.pop(0)
    load_sem, send_sem, recv_sem, gather_send, gather_recv, core_send, core_recv = scratch[-7:]
    landing = scratch[:-7]
    core = lax.axis_index("core")
    links = link_bits()
    partner = {"core": 1 - core}

    loads = []
    for at, (source, rows, cols, row, col) in enumerate(copies["list"]):
        load = pltpu.make_async_copy(
            inputs[source].at[pl.ds(rows[0], rows[1]), pl.ds(cols[0], cols[1])],
            work.at[pl.ds(row, rows[1]), pl.ds(col, cols[1])],
            load_sem.at[at],
        )
        load.start()
        loads.append(load)
    barrier = pltpu.get_barrier_semaphore()
    for device in [links[name][0] for name in ("x1", "x2", "z1", "z2", "col")] + [partner]:
        pl.semaphore_signal(barrier, inc=1, device_id=device, device_id_type=pl.DeviceIdType.MESH)
    for load in loads:
        load.wait()
    pl.semaphore_wait(barrier, 6)

    sent = []
    state, flight = [], []
    for at, (start, rows, order) in enumerate(chunks):
        state.append(work.at[pl.ds(start, rows), :])
        flight.append(None)
    for step in range(5):
        for at, (start, rows, order) in enumerate(chunks):
            if step > 0:
                copy, keep_row, width = flight[at]
                copy.wait_recv()
                target = landing[at * 5 + step - 1]
                add_into(target, state[at], keep_row, width)
                state[at] = target
            link = order[step]
            device, bit = links[link]
            landed = landing[at * 5 + step]
            size, width = landed.shape
            if link == "col":
                source = state[at].at[:, pl.ds(width, width)]
                keep_row = 0
            else:
                keep_row = bit * size
                source = state[at].at[pl.ds(pl.multiple_of((1 - bit) * size, size), size), :]
            copy = pltpu.make_async_remote_copy(
                src_ref=source,
                dst_ref=landed,
                send_sem=send_sem.at[at, step],
                recv_sem=recv_sem.at[at, step],
                device_id=device,
                device_id_type=pl.DeviceIdType.MESH,
            )
            copy.start()
            sent.append(copy)
            flight[at] = (copy, keep_row, width)
    region = []
    for at, (start, rows, order) in enumerate(chunks):
        copy, keep_row, width = flight[at]
        copy.wait_recv()
        target = landing[at * 5 + 4]
        add_into(target, state[at], keep_row, width)
        offset, size = 0, rows
        for link in order:
            if link != "col":
                size //= 2
                offset = offset + links[link][1] * size
        both[core, pl.ds(pl.multiple_of(start + offset, 16), size), :] = target[...]
        region.append((start + offset, size))
    back = [[link for link in reversed(order) if link != "col"] for _, _, order in chunks]
    waiting = [None] * len(chunks)

    def settle(at):
        copy, bit, size = waiting[at]
        copy.wait_recv()
        lo, _ = region[at]
        region[at] = (lo - bit * size, 2 * size)

    for step in range(4):
        for at in range(len(chunks)):
            if step > 0:
                settle(at)
            lo, size = region[at]
            device, bit = links[back[at][step]]
            place_here = both.at[core, pl.ds(pl.multiple_of(lo, 16), size), :]
            copy = pltpu.make_async_remote_copy(
                src_ref=place_here,
                dst_ref=place_here,
                send_sem=gather_send.at[at, step],
                recv_sem=gather_recv.at[at, step],
                device_id=device,
                device_id_type=pl.DeviceIdType.MESH,
            )
            copy.start()
            sent.append(copy)
            waiting[at] = (copy, bit, size)
    last = []
    for at, (start, rows, order) in enumerate(chunks):
        settle(at)
        place_here = both.at[core, pl.ds(start, rows), :]
        copy = pltpu.make_async_remote_copy(
            src_ref=place_here,
            dst_ref=place_here,
            send_sem=core_send.at[at],
            recv_sem=core_recv.at[at],
            device_id=partner,
            device_id_type=pl.DeviceIdType.MESH,
        )
        copy.start()
        last.append(copy)
    for copy in last:
        copy.wait_recv()
    for copy in sent + last:
        copy.wait_send()


def reduce_all(parts, copies, rows, collective_id):
    width = parts[0].shape[1]
    chunks = plan_chunks(rows)
    landing = [
        pltpu.VMEM(shape, BF)
        for _, size, order in chunks
        for shape in step_shapes(size, order, width)
    ]
    count = len(chunks)
    return pl.pallas_call(
        functools.partial(reduce_kernel, chunks, {"inputs": len(parts), "list": copies}),
        in_specs=[pl.BlockSpec(memory_space=pl.ANY)] * len(parts),
        out_specs=pl.BlockSpec(memory_space=pltpu.VMEM),
        out_shape=jax.ShapeDtypeStruct((2, rows, width // 2), BF),
        scratch_shapes=[pltpu.VMEM((rows, width), BF)]
        + landing
        + [
            pltpu.SemaphoreType.DMA((len(copies),)),
            pltpu.SemaphoreType.DMA((count, 5)),
            pltpu.SemaphoreType.DMA((count, 5)),
            pltpu.SemaphoreType.DMA((count, 4)),
            pltpu.SemaphoreType.DMA((count, 4)),
            pltpu.SemaphoreType.DMA((count,)),
            pltpu.SemaphoreType.DMA((count,)),
        ],
        compiler_params=pltpu.CompilerParams(
            collective_id=collective_id, has_side_effects=True, vmem_limit_bytes=48 * 2**20
        ),
        cost_estimate=pl.CostEstimate(
            flops=rows * width * 400, bytes_accessed=rows * width * 40, transcendentals=0
        ),
        name="reduce_all",
    )(*parts)


def finish_kernel(both_ref, up_ref, down_ref, q_ref, k_ref, v_ref, out_ref, small_ref):
    units = down_ref.shape[1] // 2
    half = up_ref.shape[1]
    heads = out_ref.shape[1] // 2
    for core in range(2):
        for part in range(units // half):
            up_ref[0, :, pl.ds(core * units + part * half, half)] = both_ref[
                core, 0, pl.ds(part * half, half), :
            ].astype(F32)
        down_ref[0, pl.ds(core * units, units), :] = both_ref[core, 0, pl.ds(units, units), :].astype(F32)
        out_ref[0, pl.ds(core * heads, heads), :] = both_ref[
            core, 0, pl.ds(2 * units + 3 * heads, heads), :
        ].astype(F32)
        small_ref[0, core] = both_ref[core, 0, pl.ds(2 * units + 4 * heads, 16), :].astype(F32)
    for at, ref in enumerate((q_ref, k_ref, v_ref)):
        here = pl.ds(2 * units + at * heads, heads)
        ref[0] = jnp.concatenate((both_ref[0, 0, here, :], both_ref[1, 0, here, :]), axis=0).astype(F32).T


def finish(both, units, heads):
    _, layers, rows, half = both.shape
    shapes = [(half, 2 * units), (2 * units, half)] + [(half, 2 * heads)] * 3 + [(2 * heads, half)]

    def spec(shape):
        return pl.BlockSpec((1,) + shape, lambda l: (l,) + (0,) * len(shape))

    small = (2, 16, half)
    return pl.pallas_call(
        finish_kernel,
        grid=(layers,),
        in_specs=[pl.BlockSpec((2, 1, rows, half), lambda l: (0, l, 0, 0))],
        out_specs=[spec(shape) for shape in shapes] + [spec(small)],
        out_shape=[jax.ShapeDtypeStruct((layers,) + s, F32) for s in shapes + [small]],
        compiler_params=pltpu.CompilerParams(vmem_limit_bytes=48 * 2**20),
        name="finish",
    )(both)


def pack_grads(grads):
    grad_up, grad_down, grad_qkv, grad_out, small, bias_up, gains_grad = grads
    half = grad_up.shape[1] // 2
    gains_low = gains_grad.astype(BF)
    gains_sum = gains_low.astype(F32) + swap_cross(gains_low).astype(F32)
    bias_rows = jnp.concatenate((bias_up.reshape(2, half),) * 2, axis=1)
    gains_row = jnp.concatenate((jnp.pad(gains_sum, (0, half - gains_sum.shape[0])),) * 2)[None]
    small = jnp.concatenate((small, bias_rows, gains_row, jnp.zeros((8, 2 * half), F32)), axis=0)
    return [value.astype(BF) for value in (grad_up, grad_down, grad_qkv, grad_out, small)]


LAYER_ROWS = 2432


def pack_copies(first, base, units, heads, width):
    half = width // 2
    copies = []
    for i in range(2):
        for j in range(2):
            copies.append((first, (i * half, half), (j * half, half), base + j * half, i * half))
    row = base + units
    for at, size in ((1, units), (2, 3 * heads), (3, heads), (4, 16)):
        copies.append((first + at, (0, size), (0, width), row, 0))
        row += size
    return copies


def shards(
    tokens, ln1_gain, ln1_shift, w_query, w_key, w_value, query_gain, key_gain, w_out,
    ln2_gain, ln2_shift, w_up, up_bias, w_down, down_bias, cotangent,
):
    core = lax.axis_index("core")
    layers = w_query.shape[0]
    heads_here = w_query.shape[2] // 2
    units_here = w_up.shape[2] // 2

    def take(value, size, axis):
        return lax.dynamic_slice_in_dim(value, core * size, size, axis)

    def both(own, axis):
        return jnp.concatenate((own, swap_col(own)), axis=axis)

    def arrive(value):
        return jnp.concatenate(
            (lax.ppermute(value, GROUP, OWN_IN), lax.ppermute(value, GROUP, OTHER_IN)), axis=1
        ).astype(F32)

    resid = arrive(tokens)
    vectors = both(jnp.stack((ln1_gain, ln1_shift, ln2_gain, ln2_shift, down_bias), axis=1), 2)
    up_bias_here = take(up_bias, units_here, 1)
    weights, mine_out = [], []
    for at in range(layers):
        qkv_here = jnp.concatenate(
            [take(w[at], heads_here, 1).T for w in (w_query, w_key, w_value)], axis=0
        )
        out_here = both(take(w_out[at], heads_here, 0), 1)
        out_chip = jnp.concatenate((out_here, swap_core(out_here)), axis=0)
        out_all = jnp.concatenate((out_chip, flip(swap_cross(out_chip), 1)), axis=0)
        weights.append(
            (
                both(qkv_here, 1),
                jnp.stack((query_gain[at], key_gain[at]), axis=1),
                out_all,
                both(take(w_up[at], units_here, 1), 0),
                up_bias_here[at],
                both(take(w_down[at], units_here, 0), 1),
                vectors[at],
            )
        )
        mine_out.append(out_here)
    caches = []
    for at in range(layers):
        resid, cache = layer_forward(resid, weights[at])
        caches.append(cache)
    half = resid.shape[1] // 2
    result = lax.ppermute(resid[:, :half].astype(BF), GROUP, OWN_OUT)
    grad = arrive(cotangent)
    parts, copies = [], []
    for at in reversed(range(layers)):
        grad, grads = layer_backward(grad, caches[at], weights[at], mine_out[at])
        if at == layers - 1:
            grad, result = lax.optimization_barrier((grad, result))
        copies += pack_copies(len(parts), at * LAYER_ROWS, units_here, heads_here, 2 * half)
        parts += pack_grads(grads)
    grad_tokens = lax.ppermute(grad[:, :half].astype(BF), GROUP, OWN_OUT).astype(F32)
    both_cores = reduce_all(parts, copies, layers * LAYER_ROWS, 1)
    both_cores = both_cores.reshape(2, layers, LAYER_ROWS, half)
    grad_up, grad_down, grad_q, grad_k, grad_v, grad_out, small = finish(
        both_cores, units_here, heads_here
    )
    both_small = small[:, 0] + small[:, 1]
    bias_up = small[:, :, 5:7].reshape(layers, -1)
    return (
        result,
        grad_tokens,
        both_small[:, 0],
        both_small[:, 1],
        grad_q,
        grad_k,
        grad_v,
        both_small[:, 7, :HEAD_DIM],
        both_small[:, 7, HEAD_DIM : 2 * HEAD_DIM],
        grad_out,
        both_small[:, 2],
        both_small[:, 3],
        grad_up,
        bias_up,
        grad_down,
        both_small[:, 4],
    )


def solution(mesh):
    fine = Mesh(mesh.devices.reshape(4, 4, 2, 2, 2), ("x", "z", "core", "row", "col"))
    rows = ("x", "z", "core", "row")
    in_specs = (
        P(rows, "col"),
        P(None, "col"),
        P(None, "col"),
        P(None, "col", "row"),
        P(None, "col", "row"),
        P(None, "col", "row"),
        P(),
        P(),
        P(None, "row", "col"),
        P(None, "col"),
        P(None, "col"),
        P(None, "col", "row"),
        P(None, "row"),
        P(None, "row", "col"),
        P(None, "col"),
        P(rows, "col"),
    )
    out_specs = (P(rows, "col"),) * 2 + in_specs[1:15]
    return jax.shard_map(shards, mesh=fine, in_specs=in_specs, out_specs=out_specs, check_vma=False)
```

```python
import functools

import jax
import jax.numpy as jnp
from jax import lax
from jax.experimental import pallas as pl
from jax.experimental.pallas import tpu as pltpu
from jax.sharding import Mesh, PartitionSpec as P

HEAD_DIM = 64
EPS = 1e-06
LOG2E = 1.4426950408889634
BF = jnp.bfloat16
F32 = jnp.float32
GROUP = ("core", "row", "col")
BLOCK = 256


def place(core, row, col):
    return core * 4 + row * 2 + col


SPOTS = [(c, r, q) for c in range(2) for r in range(2) for q in range(2)]
OWN_IN = [(place(c, r, q), place(r, q ^ c, q)) for c, r, q in SPOTS]
OTHER_IN = [(place(c, r, q), place(r, 1 ^ q ^ c, 1 ^ q)) for c, r, q in SPOTS]
OWN_OUT = [(b, a) for a, b in OWN_IN]
CROSS = [(0, 3), (3, 0), (1, 2), (2, 1)]


def swap_core(value):
    return lax.ppermute(value, "core", [(0, 1), (1, 0)])


def swap_col(value):
    return lax.ppermute(value, "col", [(0, 1), (1, 0)])


def swap_cross(value):
    return lax.ppermute(value, ("row", "col"), CROSS)


def flip(value, axis):
    first, second = jnp.split(value, 2, axis=axis)
    return jnp.concatenate((second, first), axis=axis)


def dot(left, right, left_axis=1, right_axis=0):
    return lax.dot_general(
        left, right, (((left_axis,), (right_axis,)), ((), ())), preferred_element_type=F32
    )


MESH = pl.DeviceIdType.MESH
ROWS = 256


def norm(resid):
    mean = jnp.mean(resid, axis=1, keepdims=True)
    centred = resid - mean
    factor = lax.rsqrt(jnp.mean(centred * centred, axis=1, keepdims=True) + EPS)
    return centred * factor, factor


def norm_back(grad, normal, factor, gain):
    scaled = grad * gain
    first = jnp.mean(scaled, axis=1, keepdims=True)
    second = jnp.mean(scaled * normal, axis=1, keepdims=True)
    return factor * (scaled - first - normal * second)


def head_norm(values):
    mean = jnp.mean(values, axis=0, keepdims=True)
    centred = values - mean
    factor = lax.rsqrt(jnp.mean(centred * centred, axis=0, keepdims=True) + EPS)
    return centred * factor, factor


def head_norm_back(grad, normal, factor, gain):
    scaled = grad * gain
    first = jnp.mean(scaled, axis=0, keepdims=True)
    second = jnp.mean(scaled * normal, axis=0, keepdims=True)
    return factor * (scaled - first - normal * second)


SCALE2 = LOG2E * HEAD_DIM ** (-0.5)


def gelu_parts(hidden):
    square = hidden * hidden
    bent = jnp.tanh(0.7978845608 * hidden * (1.0 + 0.044715 * square))
    active = 0.5 * hidden * (1.0 + bent)
    slope = 0.5 * (1.0 + bent) + 0.5 * hidden * (1.0 - bent * bent) * (
        0.7978845608 * (1.0 + 3.0 * 0.044715 * square)
    )
    return active, slope


def partners():
    core, row, col = (lax.axis_index(name) for name in GROUP)
    return (
        {"core": 1 - core},
        {"row": 1 - row, "col": 1 - col},
        {"core": 1 - core, "row": 1 - row, "col": 1 - col},
    )


def greet(devices):
    barrier = pltpu.get_barrier_semaphore()
    for device in devices:
        pl.semaphore_signal(barrier, inc=1, device_id=device, device_id_type=MESH)


def meet(devices):
    pl.semaphore_wait(pltpu.get_barrier_semaphore(), len(devices))


def send(source, target, sems, at, device):
    copy = pltpu.make_async_remote_copy(
        src_ref=source,
        dst_ref=target,
        send_sem=sems.at[0, at],
        recv_sem=sems.at[1, at],
        device_id=device,
        device_id_type=MESH,
    )
    copy.start()
    return copy


class Totals:
    def __init__(self, chip, core_out, core_in, cross_out, cross_in, sems, partner, cross):
        self.refs = (chip, core_out, core_in, cross_out, cross_in)
        self.sems, self.partner, self.cross = sems, partner, cross
        self.copies = []

    def run(self, compute, ready):
        chip, core_out, core_in, cross_out, cross_in = self.refs
        rows = chip.shape[0]
        count = rows // ROWS
        core_copies, cross_copies = [], []

        def pass_on(at):
            here = pl.ds(at * ROWS, ROWS)
            core_copies[at].wait_recv()
            total = chip[here, :] + core_in[here, :].astype(F32)
            chip[here, :] = total
            if cross_out is not None:
                cross_out[here, :] = total.astype(BF)
                cross_copies.append(
                    send(cross_out.at[here, :], cross_in.at[here, :], self.sems, count + at, self.cross)
                )

        for at in range(count):
            here = pl.ds(at * ROWS, ROWS)
            chip[here, :] = compute(at * ROWS)
            if at > 0:
                pass_on(at - 1)
            ready(at)
            core_out[here, :] = compute(rows + at * ROWS).astype(BF)
            core_copies.append(
                send(core_out.at[here, :], core_in.at[here, :], self.sems, at, self.partner)
            )
        pass_on(count - 1)
        self.cross_copies = cross_copies
        self.copies = core_copies + cross_copies

    def chunk(self, at):
        chip, _, _, _, cross_in = self.refs
        here = pl.ds(at * ROWS, ROWS)
        self.cross_copies[at].wait_recv()
        half = chip.shape[1] // 2
        other = cross_in[here, :].astype(F32)
        return chip[here, :] + jnp.concatenate((other[:, half:], other[:, :half]), axis=1)

    def close(self):
        for copy in self.copies:
            copy.wait_send()


def spread(fill, whole, sems, partner):
    rows = whole.shape[0] // 2
    copies = []
    for at in range(rows // ROWS):
        here = pl.ds(at * ROWS, ROWS)
        whole[here, :] = fill(at * ROWS)
        if at == 0:
            yield None
        copies.append(
            send(whole.at[here, :], whole.at[pl.ds(rows + at * ROWS, ROWS), :], sems, at, partner)
        )
    yield copies


def fill_and_send(fill, whole, sems, devices):
    steps = spread(fill, whole, sems, devices[0])
    next(steps)
    meet(devices)
    return next(steps)


def attend_forward_kernel(
    resid_ref, w_qkv_ref, gain_ref, w_out_ref, vector_ref,
    out_ref, seen_ref, qkv_ref, mixed_ref, total_ref,
    joined, seen_sems, head_sems,
):
    near, cross, far = partners()
    devices = (near, cross, far)
    greet(devices)
    rows = resid_ref.shape[0]
    heads = mixed_ref.shape[0] // HEAD_DIM
    span = heads * HEAD_DIM

    def fill(row):
        normal, _ = norm(resid_ref[pl.ds(row, ROWS), :])
        return (normal * vector_ref[0:1, :] + vector_ref[1:2, :]).astype(BF)

    copies = fill_and_send(fill, seen_ref, seen_sems, devices)
    for at in range(2 * rows // ROWS):
        if at * ROWS >= rows:
            copies[at - rows // ROWS].wait_recv()
        here = pl.ds(at * ROWS, ROWS)
        qkv_ref[:, here] = dot(w_qkv_ref[...], seen_ref[here, :], 1, 1)
    gains = gain_ref[...]
    for head in range(heads):
        own = pl.ds(head * HEAD_DIM, HEAD_DIM)
        query = (head_norm(qkv_ref[own, :])[0] * gains[:, 0:1]).astype(BF)
        key = head_norm(qkv_ref[pl.ds(span + head * HEAD_DIM, HEAD_DIM), :])[0] * gains[:, 1:2]
        key_rows = key.T.astype(BF)
        value = qkv_ref[pl.ds(2 * span + head * HEAD_DIM, HEAD_DIM), :].astype(BF)
        for at in range(0, 2 * rows, BLOCK):
            expo = jnp.exp2(dot(key_rows, query[:, at : at + BLOCK]) * SCALE2)
            total = jnp.sum(expo, axis=0, keepdims=True)
            mixed = (dot(value, expo.astype(BF)) * (1.0 / total)).astype(BF)
            mixed_ref[own, at : at + BLOCK] = mixed
            if at < rows:
                joined[own, at : at + BLOCK] = mixed
            total_ref[head : head + 1, at : at + BLOCK] = jnp.log2(total)
        mine, others = pl.ds(0, rows), pl.ds(rows, rows)
        for spot, (device, columns) in enumerate(((near, others), (cross, mine), (far, others))):
            copies.append(
                send(
                    mixed_ref.at[own, columns],
                    joined.at[pl.ds((spot + 1) * span + head * HEAD_DIM, HEAD_DIM), :],
                    head_sems,
                    head * 3 + spot,
                    device,
                )
            )
    for copy in copies[-3 * heads :]:
        copy.wait_recv()
    for at in range(rows // ROWS):
        here = pl.ds(at * ROWS, ROWS)
        out_ref[here, :] = resid_ref[here, :] + dot(joined[:, here], w_out_ref[...], 0, 0)
    for copy in copies:
        copy.wait_send()


def feed_forward_kernel(last, resid_ref, w_up_ref, bias_ref, w_down_ref, vector_ref, *refs):
    out_ref, seen_ref, active_ref, slope_ref = refs[:4]
    chip, core_out, core_in = refs[4:7]
    cross_out, cross_in = (None, None) if last else refs[7:9]
    seen_sems, total_sems = refs[-2:]
    near, cross, _ = partners()
    devices = (near,) if last else (near, cross)
    greet(devices)

    def fill(row):
        normal, _ = norm(resid_ref[pl.ds(row, ROWS), :])
        return (normal * vector_ref[2:3, :] + vector_ref[3:4, :]).astype(BF)

    copies = fill_and_send(fill, seen_ref, seen_sems, devices)

    def compute(row):
        here = pl.ds(row, ROWS)
        hidden = dot(seen_ref[here, :], w_up_ref[...]) + bias_ref[...]
        active, slope = gelu_parts(hidden)
        active = active.astype(BF)
        active_ref[here, :] = active
        slope_ref[here, :] = slope.astype(BF)
        return dot(active, w_down_ref[...])

    totals = Totals(chip, core_out, core_in, cross_out, cross_in, total_sems, near, cross)
    totals.run(compute, lambda at: copies[at].wait_recv())
    for at in range(resid_ref.shape[0] // ROWS):
        here = pl.ds(at * ROWS, ROWS)
        total = chip[here, :] if last else totals.chunk(at)
        out_ref[here, :] = total if last else resid_ref[here, :] + (total + vector_ref[4:5, :])
    for copy in copies:
        copy.wait_send()
    totals.close()


def feed_backward_kernel(
    grad_ref, resid_ref, seen_ref, active_ref, slope_ref, w_up_ref, w_down_ref, vector_ref,
    out_ref, up_ref, down_ref, small_ref,
    branch, hidden, chip, core_out, core_in, cross_out, cross_in, seen_sems, total_sems,
):
    near, cross, _ = partners()
    devices = (near, cross)
    greet(devices)
    width = grad_ref.shape[1]
    copies = fill_and_send(
        lambda row: grad_ref[pl.ds(row, ROWS), :].astype(BF), branch, seen_sems, devices
    )

    def compute(row):
        here = pl.ds(row, ROWS)
        active_grad = dot(branch[here, :], w_down_ref[...], 1, 1)
        low = (active_grad * slope_ref[here, :].astype(F32)).astype(BF)
        hidden[here, :] = low
        return dot(low, w_up_ref[...], 1, 1)

    totals = Totals(chip, core_out, core_in, cross_out, cross_in, total_sems, near, cross)
    totals.run(compute, lambda at: copies[at].wait_recv())
    rows = grad_ref.shape[0]
    for at in range(0, width, ROWS):
        down_ref[at : at + ROWS, :] = dot(active_ref[:, at : at + ROWS], branch[...], 0, 0).astype(BF)
        up_ref[at : at + ROWS, :] = dot(seen_ref[:, at : at + ROWS], hidden[...], 0, 0).astype(BF)
    small_ref[2:3, :] = jnp.sum(branch[0:rows, :].astype(F32), axis=0, keepdims=True)
    small_ref[3:4, :] = jnp.sum(hidden[...].astype(F32), axis=0, keepdims=True)
    gain_sum = jnp.zeros((1, width), F32)
    shift_sum = jnp.zeros((1, width), F32)
    for at in range(rows // ROWS):
        here = pl.ds(at * ROWS, ROWS)
        grad = totals.chunk(at)
        normal, factor = norm(resid_ref[here, :])
        gain_sum = gain_sum + jnp.sum(grad * normal, axis=0, keepdims=True)
        shift_sum = shift_sum + jnp.sum(grad, axis=0, keepdims=True)
        out_ref[here, :] = grad_ref[here, :] + norm_back(grad, normal, factor, vector_ref[2:3, :])
    small_ref[0:1, :] = gain_sum
    small_ref[1:2, :] = shift_sum
    for copy in copies:
        copy.wait_send()
    totals.close()


def attend_backward_kernel(
    grad_ref, resid_ref, seen_ref, qkv_ref, mixed_ref, total_ref, w_qkv_ref, w_out_ref, gain_ref,
    vector_ref, out_ref, grad_qkv_ref, grad_out_ref, small_ref, gains_ref,
    proj, mixed_grad, qkv_grad, chip, core_out, core_in, cross_out, cross_in, seen_sems, total_sems,
):
    near, cross, _ = partners()
    devices = (near, cross)
    greet(devices)
    rows, width = grad_ref.shape
    copies = fill_and_send(
        lambda row: grad_ref[pl.ds(row, ROWS), :].astype(BF), proj, seen_sems, devices
    )
    for at in range(2 * rows // ROWS):
        if at * ROWS >= rows:
            copies[at - rows // ROWS].wait_recv()
        here = pl.ds(at * ROWS, ROWS)
        mixed_grad[:, here] = dot(w_out_ref[...], proj[here, :], 1, 1).astype(BF)
    gains = gain_ref[...]
    span = mixed_ref.shape[0]
    scale = HEAD_DIM ** (-0.5)
    gains_sum = jnp.zeros((HEAD_DIM, 2), F32)
    for head in range(span // HEAD_DIM):
        own = pl.ds(head * HEAD_DIM, HEAD_DIM)
        key_at = pl.ds(span + head * HEAD_DIM, HEAD_DIM)
        value_at = pl.ds(2 * span + head * HEAD_DIM, HEAD_DIM)
        query_normal, query_factor = head_norm(qkv_ref[own, :])
        key_normal, key_factor = head_norm(qkv_ref[key_at, :])
        query = (query_normal * gains[:, 0:1]).astype(BF)
        key_full = key_normal * gains[:, 1:2]
        key = key_full.astype(BF)
        key_rows = key_full.T.astype(BF)
        value_rows = qkv_ref[value_at, :].T.astype(BF)
        key_sum = jnp.zeros(key.shape, F32)
        value_sum = jnp.zeros(key.shape, F32)
        query_parts = []
        for at in range(0, 2 * rows, BLOCK):
            grad = mixed_grad[own, at : at + BLOCK]
            logits = dot(key_rows, query[:, at : at + BLOCK]) * SCALE2
            probs = jnp.exp2(logits - total_ref[head : head + 1, at : at + BLOCK])
            pulled = dot(value_rows, grad)
            delta = jnp.sum(probs * pulled, axis=0, keepdims=True)
            score_grad = (probs * (pulled - delta)).astype(BF)
            query_parts.append(dot(key, score_grad))
            key_sum = key_sum + dot(query[:, at : at + BLOCK], score_grad, 1, 1)
            value_sum = value_sum + dot(grad, probs.astype(BF), 1, 1)
        query_sum = jnp.concatenate(query_parts, axis=1) * scale
        key_sum = key_sum * scale
        qkv_grad[own, :] = head_norm_back(query_sum, query_normal, query_factor, gains[:, 0:1]).astype(BF)
        qkv_grad[key_at, :] = head_norm_back(key_sum, key_normal, key_factor, gains[:, 1:2]).astype(BF)
        qkv_grad[value_at, :] = value_sum.astype(BF)
        gains_sum = gains_sum + jnp.concatenate(
            (
                jnp.sum(query_sum * query_normal, axis=1, keepdims=True),
                jnp.sum(key_sum * key_normal, axis=1, keepdims=True),
            ),
            axis=1,
        )
    gains_ref[...] = gains_sum

    def compute(row):
        return dot(qkv_grad[:, pl.ds(row, ROWS)], w_qkv_ref[...], 0, 0)

    totals = Totals(chip, core_out, core_in, cross_out, cross_in, total_sems, near, cross)
    totals.run(compute, lambda at: None)
    for at in range(0, 3 * span, span):
        here = pl.ds(at, span)
        grad_qkv_ref[here, :] = dot(qkv_grad[here, :], seen_ref[...]).astype(BF)
    grad_out_ref[...] = dot(mixed_ref[...], proj[...]).astype(BF)
    gain_sum = jnp.zeros((1, width), F32)
    shift_sum = jnp.zeros((1, width), F32)
    for at in range(rows // ROWS):
        here = pl.ds(at * ROWS, ROWS)
        grad = totals.chunk(at)
        normal, factor = norm(resid_ref[here, :])
        gain_sum = gain_sum + jnp.sum(grad * normal, axis=0, keepdims=True)
        shift_sum = shift_sum + jnp.sum(grad, axis=0, keepdims=True)
        out_ref[here, :] = grad_ref[here, :] + norm_back(grad, normal, factor, vector_ref[0:1, :])
    small_ref[0:1, :] = gain_sum
    small_ref[1:2, :] = shift_sum
    for copy in copies:
        copy.wait_send()
    totals.close()


def call(kernel, name, collective_id, inputs, outs, scratch):
    vmem = pl.BlockSpec(memory_space=pltpu.VMEM)
    return pl.pallas_call(
        kernel,
        in_specs=[vmem] * len(inputs),
        out_specs=[vmem] * len(outs),
        out_shape=[jax.ShapeDtypeStruct(*out) for out in outs],
        scratch_shapes=scratch,
        compiler_params=pltpu.CompilerParams(
            collective_id=collective_id, has_side_effects=True, vmem_limit_bytes=48 * 2**20
        ),
        name=name,
    )(*inputs)


def pair_sems(count):
    return pltpu.SemaphoreType.DMA((2, count))


def total_scratch(rows, width, last=False):
    low = pltpu.VMEM((rows, width), BF)
    count = rows // ROWS
    return [pltpu.VMEM((rows, width), F32)] + [low] * (2 if last else 4) + [
        pair_sems(count),
        pair_sems(2 * count),
    ]


def layer_forward(resid, weights, last):
    w_qkv, gains, w_out, w_up, up_bias, w_down, vectors = weights
    rows, width = resid.shape
    span = w_qkv.shape[0] // 3
    units = w_up.shape[1]
    resid_two, seen_one, qkv, mixed, total = call(
        attend_forward_kernel,
        "attend_forward",
        2,
        (resid, w_qkv, gains, w_out, vectors),
        [
            ((rows, width), F32),
            ((2 * rows, width), BF),
            ((3 * span, 2 * rows), F32),
            ((span, 2 * rows), BF),
            ((span // HEAD_DIM, 2 * rows), F32),
        ],
        [pltpu.VMEM((4 * span, rows), BF), pair_sems(rows // ROWS), pair_sems(3 * span // HEAD_DIM)],
    )
    result, seen_two, active, slope = call(
        functools.partial(feed_forward_kernel, last),
        "feed_forward",
        4 if last else 3,
        (resid_two, w_up, up_bias[None], w_down, vectors),
        [((rows, width), F32), ((2 * rows, width), BF)] + [((2 * rows, units), BF)] * 2,
        total_scratch(rows, width, last),
    )
    cache = (resid, seen_one, qkv, mixed, total, resid_two, seen_two, active, slope)
    return result, cache


def layer_backward(grad, cache, weights, w_out_mine):
    w_qkv, gains, w_out, w_up, up_bias, w_down, vectors = weights
    resid, seen_one, qkv, mixed, total, resid_two, seen_two, active, slope = cache
    rows, width = grad.shape
    units = w_up.shape[1]
    span = mixed.shape[0]
    low = pltpu.VMEM((2 * rows, width), BF)
    resid_two_grad, grad_up, grad_down, small_two = call(
        feed_backward_kernel,
        "feed_backward",
        5,
        (grad, resid_two, seen_two, active, slope, w_up, w_down, vectors),
        [((rows, width), F32), ((width, units), BF), ((units, width), BF), ((4, width), F32)],
        [low, pltpu.VMEM((2 * rows, units), BF)] + total_scratch(rows, width),
    )
    resid_grad, grad_qkv, grad_out, small_one, gains_grad = call(
        attend_backward_kernel,
        "attend_backward",
        6,
        (resid_two_grad, resid, seen_one, qkv, mixed, total, w_qkv, w_out_mine, gains, vectors),
        [
            ((rows, width), F32),
            ((3 * span, width), BF),
            ((span, width), BF),
            ((2, width), F32),
            ((HEAD_DIM, 2), F32),
        ],
        [low, pltpu.VMEM((span, 2 * rows), BF), pltpu.VMEM((3 * span, 2 * rows), BF)]
        + total_scratch(rows, width),
    )
    small = jnp.concatenate((small_one, small_two[:3]), axis=0)
    return resid_grad, (
        grad_up, grad_down, grad_qkv, grad_out, small, small_two[3], gains_grad.T.reshape(-1),
    )


def link_bits():
    x, z = lax.axis_index("x"), lax.axis_index("z")
    col = lax.axis_index("col")
    return {
        "x1": ({"x": x + 1 - 2 * (x % 2)}, ((x + 1) // 2) % 2),
        "x2": ({"x": 3 - x}, x // 2),
        "z1": ({"z": z + 1 - 2 * (z % 2)}, ((z + 1) // 2) % 2),
        "z2": ({"z": 3 - z}, z // 2),
        "col": ({"col": 1 - col}, None),
    }


ORDERS = (
    ("x1", "z1", "x2", "z2", "col"),
    ("z1", "x2", "z2", "col", "x1"),
    ("x2", "z2", "col", "x1", "z1"),
    ("z2", "col", "x1", "z1", "x2"),
    ("col", "x1", "z1", "x2", "z2"),
    ("x1", "z1", "x2", "z2", "col"),
    ("z1", "x2", "z2", "col", "x1"),
    ("x2", "z2", "col", "x1", "z1"),
    ("z2", "col", "x1", "z1", "x2"),
    ("col", "x2", "z2", "x1", "z1"),
)
UNIT = 256


def plan_chunks(rows):
    units = rows // UNIT
    count = min(units, len(ORDERS))
    sizes = [units // count + (1 if i < units % count else 0) for i in range(count)]
    chunks, start = [], 0
    for size, order in zip(sizes, ORDERS):
        chunks.append((start, size * UNIT, order))
        start += size * UNIT
    return chunks


def step_shapes(rows, order, width):
    shapes = []
    for link in order:
        if link == "col":
            width //= 2
        else:
            rows //= 2
        shapes.append((rows, width))
    return shapes


def add_into(target, other, row, col_size):
    rows = target.shape[0]
    block = min(rows, 64)

    @pl.loop(0, rows // block)
    def _(at):
        here = pl.ds(pl.multiple_of(at * block, block), block)
        there = pl.ds(pl.multiple_of(row + at * block, 16), block)
        target[here, :] = (
            target[here, :].astype(F32) + other[there, :col_size].astype(F32)
        ).astype(BF)


def reduce_kernel(chunks, copies, *refs):
    inputs = refs[: copies["inputs"]]
    both = refs[copies["inputs"]]
    scratch = list(refs[copies["inputs"] + 1 :])
    work = scratch.pop(0)
    load_sem, send_sem, recv_sem, gather_send, gather_recv, core_send, core_recv = scratch[-7:]
    landing = scratch[:-7]
    core = lax.axis_index("core")
    links = link_bits()
    partner = {"core": 1 - core}

    loads = []
    for at, (source, rows, cols, row, col) in enumerate(copies["list"]):
        load = pltpu.make_async_copy(
            inputs[source].at[pl.ds(rows[0], rows[1]), pl.ds(cols[0], cols[1])],
            work.at[pl.ds(row, rows[1]), pl.ds(col, cols[1])],
            load_sem.at[at],
        )
        load.start()
        loads.append(load)
    barrier = pltpu.get_barrier_semaphore()
    for device in [links[name][0] for name in ("x1", "x2", "z1", "z2", "col")] + [partner]:
        pl.semaphore_signal(barrier, inc=1, device_id=device, device_id_type=pl.DeviceIdType.MESH)
    for load in loads:
        load.wait()
    pl.semaphore_wait(barrier, 6)

    sent = []
    state, flight = [], []
    for at, (start, rows, order) in enumerate(chunks):
        state.append(work.at[pl.ds(start, rows), :])
        flight.append(None)
    for step in range(5):
        for at, (start, rows, order) in enumerate(chunks):
            if step > 0:
                copy, keep_row, width = flight[at]
                copy.wait_recv()
                target = landing[at * 5 + step - 1]
                add_into(target, state[at], keep_row, width)
                state[at] = target
            link = order[step]
            device, bit = links[link]
            landed = landing[at * 5 + step]
            size, width = landed.shape
            if link == "col":
                source = state[at].at[:, pl.ds(width, width)]
                keep_row = 0
            else:
                keep_row = bit * size
                source = state[at].at[pl.ds(pl.multiple_of((1 - bit) * size, size), size), :]
            copy = pltpu.make_async_remote_copy(
                src_ref=source,
                dst_ref=landed,
                send_sem=send_sem.at[at, step],
                recv_sem=recv_sem.at[at, step],
                device_id=device,
                device_id_type=pl.DeviceIdType.MESH,
            )
            copy.start()
            sent.append(copy)
            flight[at] = (copy, keep_row, width)
    region = []
    for at, (start, rows, order) in enumerate(chunks):
        copy, keep_row, width = flight[at]
        copy.wait_recv()
        target = landing[at * 5 + 4]
        add_into(target, state[at], keep_row, width)
        offset, size = 0, rows
        for link in order:
            if link != "col":
                size //= 2
                offset = offset + links[link][1] * size
        both[core, pl.ds(pl.multiple_of(start + offset, 16), size), :] = target[...]
        region.append((start + offset, size))
    back = [[link for link in reversed(order) if link != "col"] for _, _, order in chunks]
    waiting = [None] * len(chunks)

    def settle(at):
        copy, bit, size = waiting[at]
        copy.wait_recv()
        lo, _ = region[at]
        region[at] = (lo - bit * size, 2 * size)

    for step in range(4):
        for at in range(len(chunks)):
            if step > 0:
                settle(at)
            lo, size = region[at]
            device, bit = links[back[at][step]]
            place_here = both.at[core, pl.ds(pl.multiple_of(lo, 16), size), :]
            copy = pltpu.make_async_remote_copy(
                src_ref=place_here,
                dst_ref=place_here,
                send_sem=gather_send.at[at, step],
                recv_sem=gather_recv.at[at, step],
                device_id=device,
                device_id_type=pl.DeviceIdType.MESH,
            )
            copy.start()
            sent.append(copy)
            waiting[at] = (copy, bit, size)
    last = []
    for at, (start, rows, order) in enumerate(chunks):
        settle(at)
        place_here = both.at[core, pl.ds(start, rows), :]
        copy = pltpu.make_async_remote_copy(
            src_ref=place_here,
            dst_ref=place_here,
            send_sem=core_send.at[at],
            recv_sem=core_recv.at[at],
            device_id=partner,
            device_id_type=pl.DeviceIdType.MESH,
        )
        copy.start()
        last.append(copy)
    for copy in last:
        copy.wait_recv()
    for copy in sent + last:
        copy.wait_send()


def reduce_all(parts, copies, rows, collective_id):
    width = parts[0].shape[1]
    chunks = plan_chunks(rows)
    landing = [
        pltpu.VMEM(shape, BF)
        for _, size, order in chunks
        for shape in step_shapes(size, order, width)
    ]
    count = len(chunks)
    return pl.pallas_call(
        functools.partial(reduce_kernel, chunks, {"inputs": len(parts), "list": copies}),
        in_specs=[pl.BlockSpec(memory_space=pl.ANY)] * len(parts),
        out_specs=pl.BlockSpec(memory_space=pltpu.VMEM),
        out_shape=jax.ShapeDtypeStruct((2, rows, width // 2), BF),
        scratch_shapes=[pltpu.VMEM((rows, width), BF)]
        + landing
        + [
            pltpu.SemaphoreType.DMA((len(copies),)),
            pltpu.SemaphoreType.DMA((count, 5)),
            pltpu.SemaphoreType.DMA((count, 5)),
            pltpu.SemaphoreType.DMA((count, 4)),
            pltpu.SemaphoreType.DMA((count, 4)),
            pltpu.SemaphoreType.DMA((count,)),
            pltpu.SemaphoreType.DMA((count,)),
        ],
        compiler_params=pltpu.CompilerParams(
            collective_id=collective_id, has_side_effects=True, vmem_limit_bytes=48 * 2**20
        ),
        cost_estimate=pl.CostEstimate(
            flops=rows * width * 400, bytes_accessed=rows * width * 40, transcendentals=0
        ),
        name="reduce_all",
    )(*parts)


def finish_kernel(both_ref, up_ref, down_ref, q_ref, k_ref, v_ref, out_ref, small_ref):
    units = down_ref.shape[1] // 2
    half = up_ref.shape[1]
    heads = out_ref.shape[1] // 2
    for core in range(2):
        for part in range(units // half):
            up_ref[0, :, pl.ds(core * units + part * half, half)] = both_ref[
                core, 0, pl.ds(part * half, half), :
            ].astype(F32)
        down_ref[0, pl.ds(core * units, units), :] = both_ref[core, 0, pl.ds(units, units), :].astype(F32)
        out_ref[0, pl.ds(core * heads, heads), :] = both_ref[
            core, 0, pl.ds(2 * units + 3 * heads, heads), :
        ].astype(F32)
        small_ref[0, core] = both_ref[core, 0, pl.ds(2 * units + 4 * heads, 16), :].astype(F32)
    for at, ref in enumerate((q_ref, k_ref, v_ref)):
        here = pl.ds(2 * units + at * heads, heads)
        ref[0] = jnp.concatenate((both_ref[0, 0, here, :], both_ref[1, 0, here, :]), axis=0).astype(F32).T


def finish(both, units, heads):
    _, layers, rows, half = both.shape
    shapes = [(half, 2 * units), (2 * units, half)] + [(half, 2 * heads)] * 3 + [(2 * heads, half)]

    def spec(shape):
        return pl.BlockSpec((1,) + shape, lambda l: (l,) + (0,) * len(shape))

    small = (2, 16, half)
    return pl.pallas_call(
        finish_kernel,
        grid=(layers,),
        in_specs=[pl.BlockSpec((2, 1, rows, half), lambda l: (0, l, 0, 0))],
        out_specs=[spec(shape) for shape in shapes] + [spec(small)],
        out_shape=[jax.ShapeDtypeStruct((layers,) + s, F32) for s in shapes + [small]],
        compiler_params=pltpu.CompilerParams(vmem_limit_bytes=48 * 2**20),
        name="finish",
    )(both)


def pack_grads(grads):
    grad_up, grad_down, grad_qkv, grad_out, small, bias_up, gains_grad = grads
    half = grad_up.shape[1] // 2
    gains_low = gains_grad.astype(BF)
    gains_sum = gains_low.astype(F32) + swap_cross(gains_low).astype(F32)
    bias_rows = jnp.concatenate((bias_up.reshape(2, half),) * 2, axis=1)
    gains_row = jnp.concatenate((jnp.pad(gains_sum, (0, half - gains_sum.shape[0])),) * 2)[None]
    small = jnp.concatenate((small, bias_rows, gains_row, jnp.zeros((8, 2 * half), F32)), axis=0)
    return [value.astype(BF) for value in (grad_up, grad_down, grad_qkv, grad_out, small)]


LAYER_ROWS = 2432


def pack_copies(first, base, units, heads, width):
    half = width // 2
    copies = []
    for i in range(2):
        for j in range(2):
            copies.append((first, (i * half, half), (j * half, half), base + j * half, i * half))
    row = base + units
    for at, size in ((1, units), (2, 3 * heads), (3, heads), (4, 16)):
        copies.append((first + at, (0, size), (0, width), row, 0))
        row += size
    return copies


def shards(
    tokens, ln1_gain, ln1_shift, w_query, w_key, w_value, query_gain, key_gain, w_out,
    ln2_gain, ln2_shift, w_up, up_bias, w_down, down_bias, cotangent,
):
    core = lax.axis_index("core")
    layers = w_query.shape[0]
    heads_here = w_query.shape[2] // 2
    units_here = w_up.shape[2] // 2

    def take(value, size, axis):
        return lax.dynamic_slice_in_dim(value, core * size, size, axis)

    def both(own, axis):
        return jnp.concatenate((own, swap_col(own)), axis=axis)

    def arrive(value):
        return jnp.concatenate(
            (lax.ppermute(value, GROUP, OWN_IN), lax.ppermute(value, GROUP, OTHER_IN)), axis=1
        ).astype(F32)

    resid = arrive(tokens)
    vectors = both(jnp.stack((ln1_gain, ln1_shift, ln2_gain, ln2_shift, down_bias), axis=1), 2)
    up_bias_here = take(up_bias, units_here, 1)
    weights, mine_out = [], []
    for at in range(layers):
        qkv_here = jnp.concatenate(
            [take(w[at], heads_here, 1).T for w in (w_query, w_key, w_value)], axis=0
        )
        out_here = both(take(w_out[at], heads_here, 0), 1)
        out_chip = jnp.concatenate((out_here, swap_core(out_here)), axis=0)
        out_all = jnp.concatenate((out_chip, flip(swap_cross(out_chip), 1)), axis=0)
        weights.append(
            (
                both(qkv_here, 1),
                jnp.stack((query_gain[at], key_gain[at]), axis=1),
                out_all,
                both(take(w_up[at], units_here, 1), 0),
                up_bias_here[at],
                both(take(w_down[at], units_here, 0), 1),
                vectors[at],
            )
        )
        mine_out.append(out_here)
    caches = []
    for at in range(layers):
        last = at == layers - 1
        total, cache = layer_forward(resid, weights[at], last)
        caches.append(cache)
        resid = None if last else total
    half = total.shape[1] // 2
    resid = caches[-1][5][:, :half] + vectors[-1][4:5, :half] + total[:, :half]
    resid = resid + swap_cross(total[:, half:].astype(BF)).astype(F32)
    result = lax.ppermute(resid.astype(BF), GROUP, OWN_OUT)
    grad = arrive(cotangent)
    parts, copies = [], []
    for at in reversed(range(layers)):
        grad, grads = layer_backward(grad, caches[at], weights[at], mine_out[at])
        copies += pack_copies(len(parts), at * LAYER_ROWS, units_here, heads_here, 2 * half)
        parts += pack_grads(grads)
    grad_tokens = lax.ppermute(grad[:, :half].astype(BF), GROUP, OWN_OUT).astype(F32)
    both_cores = reduce_all(parts, copies, layers * LAYER_ROWS, 1)
    both_cores = both_cores.reshape(2, layers, LAYER_ROWS, half)
    grad_up, grad_down, grad_q, grad_k, grad_v, grad_out, small = finish(
        both_cores, units_here, heads_here
    )
    both_small = small[:, 0] + small[:, 1]
    bias_up = small[:, :, 5:7].reshape(layers, -1)
    return (
        result,
        grad_tokens,
        both_small[:, 0],
        both_small[:, 1],
        grad_q,
        grad_k,
        grad_v,
        both_small[:, 7, :HEAD_DIM],
        both_small[:, 7, HEAD_DIM : 2 * HEAD_DIM],
        grad_out,
        both_small[:, 2],
        both_small[:, 3],
        grad_up,
        bias_up,
        grad_down,
        both_small[:, 4],
    )


def solution(mesh):
    fine = Mesh(mesh.devices.reshape(4, 4, 2, 2, 2), ("x", "z", "core", "row", "col"))
    rows = ("x", "z", "core", "row")
    in_specs = (
        P(rows, "col"),
        P(None, "col"),
        P(None, "col"),
        P(None, "col", "row"),
        P(None, "col", "row"),
        P(None, "col", "row"),
        P(),
        P(),
        P(None, "row", "col"),
        P(None, "col"),
        P(None, "col"),
        P(None, "col", "row"),
        P(None, "row"),
        P(None, "row", "col"),
        P(None, "col"),
        P(rows, "col"),
    )
    out_specs = (P(rows, "col"),) * 2 + in_specs[1:15]
    return jax.shard_map(shards, mesh=fine, in_specs=in_specs, out_specs=out_specs, check_vma=False)
```

```python
import functools

import jax
import jax.numpy as jnp
from jax import lax
from jax.experimental import pallas as pl
from jax.experimental.pallas import tpu as pltpu
from jax.sharding import Mesh, PartitionSpec as P

HEAD_DIM = 64
EPS = 1e-06
LOG2E = 1.4426950408889634
BF = jnp.bfloat16
F32 = jnp.float32
GROUP = ("core", "row", "col")
BLOCK = 256


def dot(left, right, left_axis=1, right_axis=0):
    return lax.dot_general(
        left, right, (((left_axis,), (right_axis,)), ((), ())), preferred_element_type=F32
    )


MESH = pl.DeviceIdType.MESH
ROWS = 256


def norm(resid):
    mean = jnp.mean(resid, axis=1, keepdims=True)
    centred = resid - mean
    factor = lax.rsqrt(jnp.mean(centred * centred, axis=1, keepdims=True) + EPS)
    return centred * factor, factor


def norm_back(grad, normal, factor, gain):
    scaled = grad * gain
    first = jnp.mean(scaled, axis=1, keepdims=True)
    second = jnp.mean(scaled * normal, axis=1, keepdims=True)
    return factor * (scaled - first - normal * second)


def head_norm(values):
    mean = jnp.mean(values, axis=0, keepdims=True)
    centred = values - mean
    factor = lax.rsqrt(jnp.mean(centred * centred, axis=0, keepdims=True) + EPS)
    return centred * factor, factor


def head_norm_back(grad, normal, factor, gain):
    scaled = grad * gain
    first = jnp.mean(scaled, axis=0, keepdims=True)
    second = jnp.mean(scaled * normal, axis=0, keepdims=True)
    return factor * (scaled - first - normal * second)


SCALE2 = LOG2E * HEAD_DIM ** (-0.5)


def gelu_parts(hidden):
    square = hidden * hidden
    bent = jnp.tanh(0.7978845608 * hidden * (1.0 + 0.044715 * square))
    active = 0.5 * hidden * (1.0 + bent)
    slope = 0.5 * (1.0 + bent) + 0.5 * hidden * (1.0 - bent * bent) * (
        0.7978845608 * (1.0 + 3.0 * 0.044715 * square)
    )
    return active, slope


def group_device(core_flip, row_flip, col_flip):
    device = {}
    for name, flipped in zip(GROUP, (core_flip, row_flip, col_flip)):
        if flipped:
            device[name] = 1 - lax.axis_index(name)
    return device


def partners():
    return group_device(1, 0, 0), group_device(0, 1, 1), group_device(1, 1, 1)


def whole_group():
    return [group_device(i & 1, (i >> 1) & 1, i >> 2) for i in range(1, 8)]


def plane_neighbours():
    x, z = lax.axis_index("x"), lax.axis_index("z")
    around = ({"x": (x + 1) % 4}, {"x": (x + 3) % 4}, {"z": (z + 1) % 4}, {"z": (z + 3) % 4})
    return around, (x + 2 * z) % 4


class Quarters:
    def __init__(self, pieces, sems):
        self.sems, self.pieces = sems, pieces
        self.around, self.quarter = plane_neighbours()

    def cut(self, ref):
        size = ref.shape[0] // 4
        return ref.at[pl.ds(pl.multiple_of(self.quarter * size, 16), size), :]

    def fetch(self):
        self.first = [
            send(self.cut(source), self.cut(target), self.sems, 4 * at, device)
            for at, (source, target, device) in enumerate(self.pieces)
        ]

    def share(self):
        self.second = []
        for at, (_, target, _) in enumerate(self.pieces):
            self.first[at].wait_recv()
            here = self.cut(target)
            for spot in range(3):
                self.second.append(send(here, here, self.sems, 4 * at + 1 + spot, self.around[spot]))

    def arrive(self):
        for copy in self.second:
            copy.wait_recv()

    def close(self):
        for copy in self.first + self.second:
            copy.wait_send()


def image_spots():
    core, row, col = (lax.axis_index(name) for name in GROUP)
    flip = (col + core) % 2
    own = {"core": row, "row": flip, "col": col}
    other = {"core": row, "row": 1 - flip, "col": 1 - col}
    back = {"core": (row + col) % 2, "row": core, "col": col}
    stays = jnp.logical_and(core == row, col == 0)
    return own, other, back, stays


def move(source, target, sems, at, device, stays):
    def remote():
        return pltpu.make_async_remote_copy(
            src_ref=source,
            dst_ref=target,
            send_sem=sems.at[0, at],
            recv_sem=sems.at[1, at],
            device_id=device,
            device_id_type=MESH,
        )

    @pl.when(jnp.logical_not(stays))
    def _():
        remote().start()

    @pl.when(stays)
    def _():
        pltpu.make_async_copy(source, target, sems.at[0, at]).start()

    def finish():
        @pl.when(jnp.logical_not(stays))
        def _():
            remote().wait()

        @pl.when(stays)
        def _():
            pltpu.make_async_copy(source, target, sems.at[0, at]).wait()

    return finish


def local(source, target, sems, at):
    copy = pltpu.make_async_copy(source, target, sems.at[0, at])
    copy.start()
    return copy


def greet(devices):
    barrier = pltpu.get_barrier_semaphore()
    for device in devices:
        pl.semaphore_signal(barrier, inc=1, device_id=device, device_id_type=MESH)


def meet(devices):
    pl.semaphore_wait(pltpu.get_barrier_semaphore(), len(devices))


def send(source, target, sems, at, device):
    copy = pltpu.make_async_remote_copy(
        src_ref=source,
        dst_ref=target,
        send_sem=sems.at[0, at],
        recv_sem=sems.at[1, at],
        device_id=device,
        device_id_type=MESH,
    )
    copy.start()
    return copy


class Totals:
    def __init__(self, chip, core_out, core_in, cross_out, cross_in, sems, partner, cross):
        self.refs = (chip, core_out, core_in, cross_out, cross_in)
        self.sems, self.partner, self.cross = sems, partner, cross
        self.copies = []

    def run(self, compute, ready):
        chip, core_out, core_in, cross_out, cross_in = self.refs
        rows = chip.shape[0]
        count = rows // ROWS
        core_copies, cross_copies = [], []

        def pass_on(at):
            here = pl.ds(at * ROWS, ROWS)
            core_copies[at].wait_recv()
            total = chip[here, :] + core_in[here, :].astype(F32)
            chip[here, :] = total
            if cross_out is not None:
                cross_out[here, :] = total.astype(BF)
                cross_copies.append(
                    send(cross_out.at[here, :], cross_in.at[here, :], self.sems, count + at, self.cross)
                )

        for at in range(count):
            here = pl.ds(at * ROWS, ROWS)
            chip[here, :] = compute(at * ROWS)
            if at > 0:
                pass_on(at - 1)
            ready(at)
            core_out[here, :] = compute(rows + at * ROWS).astype(BF)
            core_copies.append(
                send(core_out.at[here, :], core_in.at[here, :], self.sems, at, self.partner)
            )
        pass_on(count - 1)
        self.cross_copies = cross_copies
        self.copies = core_copies + cross_copies

    def chunk(self, at):
        chip, _, _, _, cross_in = self.refs
        here = pl.ds(at * ROWS, ROWS)
        self.cross_copies[at].wait_recv()
        half = chip.shape[1] // 2
        other = cross_in[here, :].astype(F32)
        return chip[here, :] + jnp.concatenate((other[:, half:], other[:, :half]), axis=1)

    def close(self):
        for copy in self.copies:
            copy.wait_send()


def spread(fill, whole, sems, partner):
    rows = whole.shape[0] // 2
    copies = []
    for at in range(rows // ROWS):
        here = pl.ds(at * ROWS, ROWS)
        whole[here, :] = fill(at * ROWS)
        if at == 0:
            yield None
        copies.append(
            send(whole.at[here, :], whole.at[pl.ds(rows + at * ROWS, ROWS), :], sems, at, partner)
        )
    yield copies


def fill_and_send(fill, whole, sems, devices):
    steps = spread(fill, whole, sems, devices[0])
    next(steps)
    meet(devices)
    return next(steps)


def arrive_kernel(
    token_ref, wq_load, wk_load, wv_load, one_gain, one_shift, two_gain, two_shift, bias_load,
    out_ref, w_qkv_ref, later_ref, vector_ref,
    landed, sems, share_sems,
):
    around, _ = plane_neighbours()
    devices = whole_group() + list(around)
    greet(devices)
    core = lax.axis_index("core")
    own, other, _, stays = image_spots()
    beside = group_device(0, 0, 1)
    half = token_ref.shape[1]
    meet(devices)
    finish = move(token_ref, landed.at[:, pl.ds(0, half)], sems, 0, own, stays)
    copies = [send(token_ref, landed.at[:, pl.ds(half, half)], sems, 1, other)]
    span = w_qkv_ref.shape[0] // 3

    def turned(ref, layer):
        whole = ref[layer].astype(F32).T
        return jnp.where(core == 0, whole[:span], whole[span:]).astype(BF)

    loads = (wq_load, wk_load, wv_load)
    for at, load in enumerate(loads):
        w_qkv_ref[pl.ds(at * span, span), 0:half] = turned(load(), 0)
    shared = Quarters(
        [(w_qkv_ref.at[:, pl.ds(0, half)], w_qkv_ref.at[:, pl.ds(half, half)], beside)], share_sems
    )
    shared.fetch()
    refs = [load() for load in (one_gain, one_shift, two_gain, two_shift, bias_load)]
    for layer in range(vector_ref.shape[0]):
        rows = [ref[layer : layer + 1, :] for ref in refs]
        vector_ref[layer, :, 0:half] = jnp.concatenate(rows + [jnp.zeros((3, half), F32)], axis=0)
    copies.append(
        send(vector_ref.at[:, :, pl.ds(0, half)], vector_ref.at[:, :, pl.ds(half, half)], sems, 2, beside)
    )
    for at, load in enumerate(loads):
        later_ref[pl.ds(at * span, span), :] = turned(load(), 1)
    shared.share()
    finish()
    copies[0].wait()
    out_ref[...] = landed[...].astype(F32)
    copies[1].wait()
    shared.arrive()
    shared.close()


def attend_forward_kernel(
    layer, resid_load, w_qkv_load, gain_load, vector_load, raw_out_ref, raw_up_ref, raw_down_ref,
    out_ref, seen_ref, qkv_ref, mixed_ref, total_ref, w_out_ref, w_up_ref, w_down_ref,
    joined, seen_sems, head_sems, keep_sems, share_sems,
):
    near, cross, far = partners()
    beside, across = group_device(0, 0, 1), group_device(0, 1, 0)
    around, _ = plane_neighbours()
    devices = (near, cross, far, beside, across) + around
    greet(devices)
    core = lax.axis_index("core")
    resid_ref, vector_ref = resid_load(), vector_load()
    rows, width = resid_ref.shape
    half = width // 2
    units = w_up_ref.shape[1]
    heads = mixed_ref.shape[0] // HEAD_DIM
    span = heads * HEAD_DIM

    def fill(row):
        normal, _ = norm(resid_ref[pl.ds(row, ROWS), :])
        return (normal * vector_ref[0:1, :] + vector_ref[1:2, :]).astype(BF)

    copies = fill_and_send(fill, seen_ref, seen_sems, devices)
    pieces, kept = [], []
    up_raw = raw_up_ref.at[layer, :, pl.ds(pl.multiple_of(core * units, units), units)]
    down_raw = raw_down_ref.at[layer, pl.ds(pl.multiple_of(core * units, units), units), :]
    pieces.append((up_raw, w_up_ref.at[pl.ds(half, half), :], beside))
    pieces.append((down_raw, w_down_ref.at[:, pl.ds(half, half)], beside))
    for at in range(2):
        source = raw_out_ref.at[layer, pl.ds((core + at - 2 * at * core) * span, span), :]
        for device, row, col in ((beside, 0, half), (cross, half, half), (across, half, 0)):
            pieces.append((source, w_out_ref.at[pl.ds(row + at * span, span), pl.ds(col, half)], device))
        kept.append(local(source, w_out_ref.at[pl.ds(at * span, span), pl.ds(0, half)], keep_sems, at))
    kept.append(local(up_raw, w_up_ref.at[pl.ds(0, half), :], keep_sems, 2))
    kept.append(local(down_raw, w_down_ref.at[:, pl.ds(0, half)], keep_sems, 3))
    shared = Quarters(pieces, share_sems)
    shared.fetch()
    w_qkv_ref = w_qkv_load()
    for at in range(2 * rows // ROWS):
        if at * ROWS >= rows:
            copies[at - rows // ROWS].wait_recv()
        here = pl.ds(at * ROWS, ROWS)
        qkv_ref[:, here] = dot(w_qkv_ref[...], seen_ref[here, :], 1, 1)
    gains = gain_load()[...]
    for head in range(heads):
        if head == 1:
            shared.share()
        own = pl.ds(head * HEAD_DIM, HEAD_DIM)
        query = (head_norm(qkv_ref[own, :])[0] * gains[:, 0:1]).astype(BF)
        key = head_norm(qkv_ref[pl.ds(span + head * HEAD_DIM, HEAD_DIM), :])[0] * gains[:, 1:2]
        key_rows = key.T.astype(BF)
        value = qkv_ref[pl.ds(2 * span + head * HEAD_DIM, HEAD_DIM), :].astype(BF)
        for at in range(0, 2 * rows, BLOCK):
            expo = jnp.exp2(dot(key_rows, query[:, at : at + BLOCK]) * SCALE2)
            total = jnp.sum(expo, axis=0, keepdims=True)
            mixed = (dot(value, expo.astype(BF)) * (1.0 / total)).astype(BF)
            mixed_ref[own, at : at + BLOCK] = mixed
            if at < rows:
                joined[own, at : at + BLOCK] = mixed
            total_ref[head : head + 1, at : at + BLOCK] = jnp.log2(total)
        mine, others = pl.ds(0, rows), pl.ds(rows, rows)
        for spot, (device, columns) in enumerate(((near, others), (cross, mine), (far, others))):
            copies.append(
                send(
                    mixed_ref.at[own, columns],
                    joined.at[pl.ds((spot + 1) * span + head * HEAD_DIM, HEAD_DIM), :],
                    head_sems,
                    head * 3 + spot,
                    device,
                )
            )
    shared.arrive()
    for copy in kept:
        copy.wait()
    for copy in copies[-3 * heads :]:
        copy.wait_recv()
    for at in range(rows // ROWS):
        here = pl.ds(at * ROWS, ROWS)
        out_ref[here, :] = resid_ref[here, :] + dot(joined[:, here], w_out_ref[...], 0, 0)
    for copy in copies:
        copy.wait_send()
    shared.close()


def feed_forward_kernel(layer, last, resid_load, w_up_load, bias_load, w_down_load, vector_load, side_ref, *refs):
    out_ref, seen_ref, active_ref, slope_ref, side_out = refs[:5]
    if last:
        low_ref, chip, core_out, core_in, landed = refs[5:10]
        cross_out, cross_in = None, None
    else:
        chip, core_out, core_in, cross_out, cross_in = refs[5:10]
    seen_sems, total_sems, side_sems = refs[-3:]
    near, cross, _ = partners()
    beside = group_device(0, 0, 1)
    devices = whole_group() if last else (near, cross, beside)
    greet(devices)
    core = lax.axis_index("core")
    resid_ref, vector_ref = resid_load(), vector_load()
    half = resid_ref.shape[1] // 2

    def fill(row):
        normal, _ = norm(resid_ref[pl.ds(row, ROWS), :])
        return (normal * vector_ref[2:3, :] + vector_ref[3:4, :]).astype(BF)

    if last:
        steps = spread(fill, seen_ref, seen_sems, near)
        next(steps)
        meet(devices)
        copies = next(steps)
        own, other, _, stays = image_spots()
        arrived = move(side_ref, landed.at[:, pl.ds(0, half)], side_sems, 0, own, stays)
        side = send(side_ref, landed.at[:, pl.ds(half, half)], side_sems, 1, other)
    else:
        copies = fill_and_send(fill, seen_ref, seen_sems, devices)
        kept = local(side_ref, side_out.at[:, pl.ds(0, half)], side_sems, 0)
        side = send(side_ref, side_out.at[:, pl.ds(half, half)], side_sems, 1, beside)

    w_up_ref, w_down_ref, bias_ref = w_up_load(), w_down_load(), bias_load()
    units = w_up_ref.shape[1]
    bias = bias_ref[layer : layer + 1, pl.ds(pl.multiple_of(core * units, units), units)]

    def compute(row):
        here = pl.ds(row, ROWS)
        hidden = dot(seen_ref[here, :], w_up_ref[...]) + bias
        active, slope = gelu_parts(hidden)
        active = active.astype(BF)
        active_ref[here, :] = active
        slope_ref[here, :] = slope.astype(BF)
        return dot(active, w_down_ref[...])

    totals = Totals(chip, core_out, core_in, cross_out, cross_in, total_sems, near, cross)
    totals.run(compute, lambda at: copies[at].wait_recv())
    for at in range(resid_ref.shape[0] // ROWS):
        here = pl.ds(at * ROWS, ROWS)
        total = chip[here, :] if last else totals.chunk(at)
        out_ref[here, :] = resid_ref[here, :] + (total + vector_ref[4:5, :])
        if last:
            low_ref[here, :] = total[:, half:].astype(BF)
    for copy in copies:
        copy.wait_send()
    totals.close()
    side.wait()
    if last:
        arrived()
        side_out[...] = landed[...].astype(F32)
    else:
        kept.wait()


def feed_backward_kernel(
    grad_load, resid_load, seen_load, active_load, slope_load, w_up_load, w_down_load, vector_load,
    out_ref, up_ref, down_ref, small_ref,
    branch, hidden, chip, core_out, core_in, cross_out, cross_in, seen_sems, total_sems,
):
    near, cross, _ = partners()
    devices = (near, cross)
    greet(devices)
    grad_ref = grad_load()
    width = grad_ref.shape[1]
    copies = fill_and_send(
        lambda row: grad_ref[pl.ds(row, ROWS), :].astype(BF), branch, seen_sems, devices
    )
    w_down_ref, slope_ref, w_up_ref = w_down_load(), slope_load(), w_up_load()

    def compute(row):
        here = pl.ds(row, ROWS)
        active_grad = dot(branch[here, :], w_down_ref[...], 1, 1)
        low = (active_grad * slope_ref[here, :].astype(F32)).astype(BF)
        hidden[here, :] = low
        return dot(low, w_up_ref[...], 1, 1)

    totals = Totals(chip, core_out, core_in, cross_out, cross_in, total_sems, near, cross)
    totals.run(compute, lambda at: copies[at].wait_recv())
    rows = grad_ref.shape[0]
    active_ref, seen_ref, resid_ref, vector_ref = active_load(), seen_load(), resid_load(), vector_load()
    for at in range(0, width, ROWS):
        down_ref[at : at + ROWS, :] = dot(active_ref[:, at : at + ROWS], branch[...], 0, 0).astype(BF)
        up_ref[at : at + ROWS, :] = dot(seen_ref[:, at : at + ROWS], hidden[...], 0, 0).astype(BF)
    bias_down = jnp.sum(branch[0:rows, :].astype(F32), axis=0, keepdims=True)
    bias_up = jnp.sum(hidden[...].astype(F32), axis=0, keepdims=True)
    half = width // 2
    gain_sum = jnp.zeros((1, width), F32)
    shift_sum = jnp.zeros((1, width), F32)
    for at in range(rows // ROWS):
        here = pl.ds(at * ROWS, ROWS)
        grad = totals.chunk(at)
        normal, factor = norm(resid_ref[here, :])
        gain_sum = gain_sum + jnp.sum(grad * normal, axis=0, keepdims=True)
        shift_sum = shift_sum + jnp.sum(grad, axis=0, keepdims=True)
        out_ref[here, :] = grad_ref[here, :] + norm_back(grad, normal, factor, vector_ref[2:3, :])
    small_ref[...] = jnp.concatenate(
        [gain_sum, shift_sum, bias_down]
        + [jnp.concatenate((bias_up[:, i * half : (i + 1) * half],) * 2, axis=1) for i in range(2)]
        + [jnp.zeros((11, width), F32)],
        axis=0,
    ).astype(BF)
    for copy in copies:
        copy.wait_send()
    totals.close()


def attend_backward_kernel(
    grad_load, resid_load, seen_load, qkv_load, mixed_load, total_load, w_qkv_load, w_out_load, gain_load,
    vector_load, out_ref, grad_qkv_ref, grad_out_ref, small_ref,
    proj, mixed_grad, qkv_grad, gains_own, gains_in,
    chip, core_out, core_in, cross_out, cross_in, seen_sems, total_sems, gain_sems,
):
    near, cross, _ = partners()
    devices = (near, cross)
    greet(devices)
    grad_ref = grad_load()
    rows, width = grad_ref.shape
    copies = fill_and_send(
        lambda row: grad_ref[pl.ds(row, ROWS), :].astype(BF), proj, seen_sems, devices
    )
    w_out_ref = w_out_load()
    span = mixed_grad.shape[0]
    for at in range(2 * rows // ROWS):
        if at * ROWS >= rows:
            copies[at - rows // ROWS].wait_recv()
        here = pl.ds(at * ROWS, ROWS)
        mixed_grad[:, here] = dot(w_out_ref[pl.ds(0, span), :], proj[here, :], 1, 1).astype(BF)
    gains, qkv_ref, total_ref = gain_load()[...], qkv_load(), total_load()
    scale = HEAD_DIM ** (-0.5)
    gains_sum = jnp.zeros((HEAD_DIM, 2), F32)
    for head in range(span // HEAD_DIM):
        own = pl.ds(head * HEAD_DIM, HEAD_DIM)
        key_at = pl.ds(span + head * HEAD_DIM, HEAD_DIM)
        value_at = pl.ds(2 * span + head * HEAD_DIM, HEAD_DIM)
        query_normal, query_factor = head_norm(qkv_ref[own, :])
        key_normal, key_factor = head_norm(qkv_ref[key_at, :])
        query = (query_normal * gains[:, 0:1]).astype(BF)
        key_full = key_normal * gains[:, 1:2]
        key = key_full.astype(BF)
        key_rows = key_full.T.astype(BF)
        value_rows = qkv_ref[value_at, :].T.astype(BF)
        key_sum = jnp.zeros(key.shape, F32)
        value_sum = jnp.zeros(key.shape, F32)
        query_parts = []
        for at in range(0, 2 * rows, BLOCK):
            grad = mixed_grad[own, at : at + BLOCK]
            logits = dot(key_rows, query[:, at : at + BLOCK]) * SCALE2
            probs = jnp.exp2(logits - total_ref[head : head + 1, at : at + BLOCK])
            pulled = dot(value_rows, grad)
            delta = jnp.sum(probs * pulled, axis=0, keepdims=True)
            score_grad = (probs * (pulled - delta)).astype(BF)
            query_parts.append(dot(key, score_grad))
            key_sum = key_sum + dot(query[:, at : at + BLOCK], score_grad, 1, 1)
            value_sum = value_sum + dot(grad, probs.astype(BF), 1, 1)
        query_sum = jnp.concatenate(query_parts, axis=1) * scale
        key_sum = key_sum * scale
        qkv_grad[own, :] = head_norm_back(query_sum, query_normal, query_factor, gains[:, 0:1]).astype(BF)
        qkv_grad[key_at, :] = head_norm_back(key_sum, key_normal, key_factor, gains[:, 1:2]).astype(BF)
        qkv_grad[value_at, :] = value_sum.astype(BF)
        gains_sum = gains_sum + jnp.concatenate(
            (
                jnp.sum(query_sum * query_normal, axis=1, keepdims=True),
                jnp.sum(key_sum * key_normal, axis=1, keepdims=True),
            ),
            axis=1,
        )
    square = jnp.concatenate((gains_sum, jnp.zeros((HEAD_DIM, 126), F32)), axis=1)
    gains_own[...] = jnp.concatenate((square, jnp.zeros((128 - HEAD_DIM, 128), F32)), axis=0).T[0:8]
    gains_copy = send(gains_own, gains_in, gain_sems, 0, cross)

    w_qkv_ref = w_qkv_load()

    def compute(row):
        return dot(qkv_grad[:, pl.ds(row, ROWS)], w_qkv_ref[...], 0, 0)

    totals = Totals(chip, core_out, core_in, cross_out, cross_in, total_sems, near, cross)
    totals.run(compute, lambda at: None)
    seen_ref, mixed_ref, resid_ref, vector_ref = seen_load(), mixed_load(), resid_load(), vector_load()
    for at in range(0, 3 * span, span):
        here = pl.ds(at, span)
        grad_qkv_ref[here, :] = dot(qkv_grad[here, :], seen_ref[...]).astype(BF)
    grad_out_ref[...] = dot(mixed_ref[...], proj[...]).astype(BF)
    gain_sum = jnp.zeros((1, width), F32)
    shift_sum = jnp.zeros((1, width), F32)
    for at in range(rows // ROWS):
        here = pl.ds(at * ROWS, ROWS)
        grad = totals.chunk(at)
        normal, factor = norm(resid_ref[here, :])
        gain_sum = gain_sum + jnp.sum(grad * normal, axis=0, keepdims=True)
        shift_sum = shift_sum + jnp.sum(grad, axis=0, keepdims=True)
        out_ref[here, :] = grad_ref[here, :] + norm_back(grad, normal, factor, vector_ref[0:1, :])
    gains_copy.wait()
    shared = gains_own[0:2, :] + gains_in[0:2, :]
    blank = jnp.zeros((2, width // 2 - 128), F32)
    small_ref[...] = jnp.concatenate(
        [gain_sum, shift_sum]
        + [jnp.concatenate((shared, blank, shared, blank), axis=1), jnp.zeros((12, width), F32)],
        axis=0,
    ).astype(BF)
    for copy in copies:
        copy.wait_send()
    totals.close()


class Load:
    def __init__(self, source, target, sem):
        self.copy = pltpu.make_async_copy(source, target, sem)
        self.copy.start()
        self.target, self.waited = target, False

    def __call__(self):
        if not self.waited:
            self.copy.wait()
            self.waited = True
        return self.target


def call(kernel, name, collective_id, inputs, outs, scratch):
    vmem = pl.BlockSpec(memory_space=pltpu.VMEM)
    hbm = pl.BlockSpec(memory_space=pl.ANY)

    def kind(spec):
        return spec[0] if isinstance(spec, tuple) and isinstance(spec[0], str) else "block"

    def bare(spec):
        return spec if kind(spec) == "block" else spec[1]

    kinds = [kind(spec) for spec in inputs]
    values = [bare(spec) for spec in inputs]
    loaded = [at for at, k in enumerate(kinds) if k == "load"]

    def body(*refs):
        refs = list(refs)
        staged, sems = refs[-1 - len(loaded) : -1], refs[-1]
        given = refs[: len(inputs)]
        loads = [Load(given[at], staged[i], sems.at[i]) for i, at in enumerate(loaded)]
        for at, load in zip(loaded, loads):
            given[at] = load
        kernel(*given, *refs[len(inputs) : -1 - len(loaded)])
        for load in loads:
            load()

    return pl.pallas_call(
        body,
        in_specs=[vmem if k == "block" else hbm for k in kinds],
        out_specs=[vmem if kind(spec) == "block" else hbm for spec in outs],
        out_shape=[jax.ShapeDtypeStruct(*bare(spec)) for spec in outs],
        scratch_shapes=scratch
        + [pltpu.VMEM(values[at].shape, values[at].dtype) for at in loaded]
        + [pltpu.SemaphoreType.DMA((max(1, len(loaded)),))],
        compiler_params=pltpu.CompilerParams(
            collective_id=collective_id, has_side_effects=True, vmem_limit_bytes=56 * 2**20
        ),
        name=name,
    )(*values)


def pair_sems(count):
    return pltpu.SemaphoreType.DMA((2, count))


def total_scratch(rows, width):
    return [pltpu.VMEM((rows, width), F32)] + [pltpu.VMEM((rows, width), BF)] * 4


def total_sems(rows):
    return [pair_sems(rows // ROWS), pair_sems(2 * rows // ROWS)]


def arrive(tokens, w_query, w_key, w_value, vectors):
    rows, half = tokens.shape
    span = w_query.shape[2] // 2
    layers = w_query.shape[0]
    return call(
        arrive_kernel,
        "arrive",
        7,
        [("hbm", tokens)] + [("load", value) for value in (w_query, w_key, w_value) + vectors],
        [
            ((rows, 2 * half), F32),
            ((3 * span, 2 * half), BF),
            ((3 * span, half), BF),
            ((layers, 8, 2 * half), F32),
        ],
        [pltpu.VMEM((rows, 2 * half), BF), pair_sems(3), pair_sems(4)],
    )


def attend_forward(layer, resid, w_qkv, gains, vectors, raw_out, raw_up, raw_down):
    rows, width = resid.shape
    span = w_qkv.shape[0] // 3
    units = raw_up.shape[2] // 2
    return call(
        functools.partial(attend_forward_kernel, layer),
        "attend_forward_%d" % layer,
        8 + layer,
        [("load", value) for value in (resid, w_qkv, gains, vectors)]
        + [("hbm", value) for value in (raw_out, raw_up, raw_down)],
        [
            ((rows, width), F32),
            ((2 * rows, width), BF),
            ((3 * span, 2 * rows), F32),
            ((span, 2 * rows), BF),
            ((span // HEAD_DIM, 2 * rows), F32),
            ((width, width), BF),
            ((width, units), BF),
            ((units, width), BF),
        ],
        [
            pltpu.VMEM((4 * span, rows), BF),
            pair_sems(rows // ROWS),
            pair_sems(3 * span // HEAD_DIM),
            pair_sems(4),
            pair_sems(32),
        ],
    )


def feed_forward(layer, last, resid, w_up, up_bias, w_down, vectors, side):
    rows, width = resid.shape
    units = w_up.shape[1]
    outs = [((rows, width), F32), ((2 * rows, width), BF)] + [((2 * rows, units), BF)] * 2
    low = pltpu.VMEM((rows, width), BF)
    if last:
        outs += [((rows, width), F32), ((rows, width // 2), BF)]
        scratch = [pltpu.VMEM((rows, width), F32), low, low, low]
    else:
        outs += [((side.shape[0], width), BF)]
        scratch = total_scratch(rows, width)
    return call(
        functools.partial(feed_forward_kernel, layer, last),
        "feed_forward_%d" % layer,
        4 if last else 3,
        [("load", value) for value in (resid, w_up, up_bias, w_down, vectors)] + [("hbm", side)],
        outs,
        scratch + total_sems(rows) + [pair_sems(2)],
    )


def feed_backward(grad, resid, seen, active, slope, w_up, w_down, vectors):
    rows, width = grad.shape
    units = w_up.shape[1]
    return call(
        feed_backward_kernel,
        "feed_backward",
        5,
        [("load", value) for value in (grad, resid, seen, active, slope, w_up, w_down, vectors)],
        [((rows, width), F32), ((width, units), BF), ((units, width), BF), ((16, width), BF)],
        [pltpu.VMEM((2 * rows, width), BF), pltpu.VMEM((2 * rows, units), BF)]
        + total_scratch(rows, width)
        + total_sems(rows),
    )


def attend_backward(grad, resid, seen, qkv, mixed, total, w_qkv, w_out, gains, vectors):
    rows, width = grad.shape
    span = mixed.shape[0]
    return call(
        attend_backward_kernel,
        "attend_backward",
        6,
        [
            ("load", value)
            for value in (grad, resid, seen, qkv, mixed, total, w_qkv, w_out, gains, vectors)
        ],
        [((rows, width), F32), ((3 * span, width), BF), ((span, width), BF), ((16, width), BF)],
        [
            pltpu.VMEM((2 * rows, width), BF),
            pltpu.VMEM((span, 2 * rows), BF),
            pltpu.VMEM((3 * span, 2 * rows), BF),
            pltpu.VMEM((8, 128), F32),
            pltpu.VMEM((8, 128), F32),
        ]
        + total_scratch(rows, width)
        + total_sems(rows)
        + [pair_sems(1)],
    )


def link_bits():
    x, z = lax.axis_index("x"), lax.axis_index("z")
    col = lax.axis_index("col")
    return {
        "x1": ({"x": x + 1 - 2 * (x % 2)}, ((x + 1) // 2) % 2),
        "x2": ({"x": 3 - x}, x // 2),
        "z1": ({"z": z + 1 - 2 * (z % 2)}, ((z + 1) // 2) % 2),
        "z2": ({"z": 3 - z}, z // 2),
        "col": ({"col": 1 - col}, None),
    }


ORDERS = (
    ("x1", "z1", "x2", "z2", "col"),
    ("z1", "x2", "z2", "col", "x1"),
    ("x2", "z2", "col", "x1", "z1"),
    ("z2", "col", "x1", "z1", "x2"),
    ("col", "x1", "z1", "x2", "z2"),
    ("x1", "z1", "x2", "z2", "col"),
    ("z1", "x2", "z2", "col", "x1"),
    ("x2", "z2", "col", "x1", "z1"),
    ("z2", "col", "x1", "z1", "x2"),
    ("col", "x2", "z2", "x1", "z1"),
)
UNIT = 256


def plan_chunks(rows):
    units = rows // UNIT
    count = min(units, len(ORDERS))
    sizes = [units // count + (1 if i < units % count else 0) for i in range(count)]
    chunks, start = [], 0
    for size, order in zip(sizes, ORDERS):
        chunks.append((start, size * UNIT, order))
        start += size * UNIT
    return chunks


def step_shapes(rows, order, width):
    shapes = []
    for link in order:
        if link == "col":
            width //= 2
        else:
            rows //= 2
        shapes.append((rows, width))
    return shapes


def add_into(target, other, row, col_size):
    rows = target.shape[0]
    block = min(rows, 64)

    @pl.loop(0, rows // block)
    def _(at):
        here = pl.ds(pl.multiple_of(at * block, block), block)
        there = pl.ds(pl.multiple_of(row + at * block, 16), block)
        target[here, :] = (
            target[here, :].astype(F32) + other[there, :col_size].astype(F32)
        ).astype(BF)


def reduce_kernel(chunks, copies, *refs):
    last_ref, low_ref, grad_ref = refs[:3]
    refs = refs[3:]
    inputs = refs[: copies["inputs"]]
    both, result_ref, token_ref = refs[copies["inputs"] : copies["inputs"] + 3]
    scratch = list(refs[copies["inputs"] + 3 :])
    work, low_in, result_low, token_low, token_in, home_sems = scratch[:6]
    scratch = scratch[6:]
    load_sem, send_sem, recv_sem, gather_send, gather_recv, core_send, core_recv = scratch[-7:]
    landing = scratch[:-7]
    core = lax.axis_index("core")
    links = link_bits()
    partner = {"core": 1 - core}

    loads = []
    for at, (source, rows, cols, row, col) in enumerate(copies["list"]):
        load = pltpu.make_async_copy(
            inputs[source].at[pl.ds(rows[0], rows[1]), pl.ds(cols[0], cols[1])],
            work.at[pl.ds(row, rows[1]), pl.ds(col, cols[1])],
            load_sem.at[at],
        )
        load.start()
        loads.append(load)
    devices = [links[name][0] for name in ("x1", "x2", "z1", "z2")] + whole_group()
    greet(devices)
    half = both.shape[2]
    token_low[...] = grad_ref[:, 0:half].astype(BF)
    for load in loads:
        load.wait()
    meet(devices)
    _, _, home, stays = image_spots()
    low_copy = send(low_ref, low_in, home_sems, 0, partners()[1])

    sent = []
    state, flight = [], []
    for at, (start, rows, order) in enumerate(chunks):
        state.append(work.at[pl.ds(start, rows), :])
        flight.append(None)
    for step in range(5):
        for at, (start, rows, order) in enumerate(chunks):
            if step > 0:
                copy, keep_row, width = flight[at]
                copy.wait_recv()
                target = landing[at * 5 + step - 1]
                add_into(target, state[at], keep_row, width)
                state[at] = target
            link = order[step]
            device, bit = links[link]
            landed = landing[at * 5 + step]
            size, width = landed.shape
            if link == "col":
                source = state[at].at[:, pl.ds(width, width)]
                keep_row = 0
            else:
                keep_row = bit * size
                source = state[at].at[pl.ds(pl.multiple_of((1 - bit) * size, size), size), :]
            copy = pltpu.make_async_remote_copy(
                src_ref=source,
                dst_ref=landed,
                send_sem=send_sem.at[at, step],
                recv_sem=recv_sem.at[at, step],
                device_id=device,
                device_id_type=pl.DeviceIdType.MESH,
            )
            copy.start()
            sent.append(copy)
            flight[at] = (copy, keep_row, width)
    token_done = move(token_low, token_in, home_sems, 1, home, stays)
    low_copy.wait()
    result_low[...] = (last_ref[:, 0:half] + low_in[...].astype(F32)).astype(BF)
    result_done = move(result_low, result_ref, home_sems, 2, home, stays)
    region = []
    for at, (start, rows, order) in enumerate(chunks):
        copy, keep_row, width = flight[at]
        copy.wait_recv()
        target = landing[at * 5 + 4]
        add_into(target, state[at], keep_row, width)
        offset, size = 0, rows
        for link in order:
            if link != "col":
                size //= 2
                offset = offset + links[link][1] * size
        both[core, pl.ds(pl.multiple_of(start + offset, 16), size), :] = target[...]
        region.append((start + offset, size))
    back = [[link for link in reversed(order) if link != "col"] for _, _, order in chunks]
    waiting = [None] * len(chunks)

    def settle(at):
        copy, bit, size = waiting[at]
        copy.wait_recv()
        lo, _ = region[at]
        region[at] = (lo - bit * size, 2 * size)

    for step in range(4):
        for at in range(len(chunks)):
            if step > 0:
                settle(at)
            lo, size = region[at]
            device, bit = links[back[at][step]]
            place_here = both.at[core, pl.ds(pl.multiple_of(lo, 16), size), :]
            copy = pltpu.make_async_remote_copy(
                src_ref=place_here,
                dst_ref=place_here,
                send_sem=gather_send.at[at, step],
                recv_sem=gather_recv.at[at, step],
                device_id=device,
                device_id_type=pl.DeviceIdType.MESH,
            )
            copy.start()
            sent.append(copy)
            waiting[at] = (copy, bit, size)
    last = []
    for at, (start, rows, order) in enumerate(chunks):
        settle(at)
        place_here = both.at[core, pl.ds(start, rows), :]
        copy = pltpu.make_async_remote_copy(
            src_ref=place_here,
            dst_ref=place_here,
            send_sem=core_send.at[at],
            recv_sem=core_recv.at[at],
            device_id=partner,
            device_id_type=pl.DeviceIdType.MESH,
        )
        copy.start()
        last.append(copy)
    token_done()
    token_ref[...] = token_in[...].astype(F32)
    result_done()
    for copy in last:
        copy.wait_recv()
    for copy in sent + last:
        copy.wait_send()


def reduce_all(final, low, grad, parts, copies, rows, collective_id):
    width = parts[0].shape[1]
    tokens = grad.shape[0]
    chunks = plan_chunks(rows)
    landing = [
        pltpu.VMEM(shape, BF)
        for _, size, order in chunks
        for shape in step_shapes(size, order, width)
    ]
    count = len(chunks)
    home = pltpu.VMEM((tokens, width // 2), BF)
    vmem = pl.BlockSpec(memory_space=pltpu.VMEM)
    return pl.pallas_call(
        functools.partial(reduce_kernel, chunks, {"inputs": len(parts), "list": copies}),
        in_specs=[vmem] * 3 + [pl.BlockSpec(memory_space=pl.ANY)] * len(parts),
        out_specs=[vmem] * 3,
        out_shape=[
            jax.ShapeDtypeStruct((2, rows, width // 2), BF),
            jax.ShapeDtypeStruct((tokens, width // 2), BF),
            jax.ShapeDtypeStruct((tokens, width // 2), F32),
        ],
        scratch_shapes=[pltpu.VMEM((rows, width), BF), home, home, home, home, pair_sems(3)]
        + landing
        + [
            pltpu.SemaphoreType.DMA((len(copies),)),
            pltpu.SemaphoreType.DMA((count, 5)),
            pltpu.SemaphoreType.DMA((count, 5)),
            pltpu.SemaphoreType.DMA((count, 4)),
            pltpu.SemaphoreType.DMA((count, 4)),
            pltpu.SemaphoreType.DMA((count,)),
            pltpu.SemaphoreType.DMA((count,)),
        ],
        compiler_params=pltpu.CompilerParams(
            collective_id=collective_id, has_side_effects=True, vmem_limit_bytes=56 * 2**20
        ),
        name="reduce_all",
    )(final, low, grad, *parts)


def finish_kernel(both_ref, up_ref, down_ref, q_ref, k_ref, v_ref, out_ref, bias_ref, *small_refs):
    layer = pl.program_id(0)
    units = down_ref.shape[1] // 2
    half = up_ref.shape[1]
    heads = out_ref.shape[1] // 2
    small_at = 2 * units + 4 * heads
    small = [both_ref[core, 0, pl.ds(small_at, 32), :].astype(F32) for core in range(2)]
    for core in range(2):
        for part in range(units // half):
            up_ref[0, :, pl.ds(core * units + part * half, half)] = both_ref[
                core, 0, pl.ds(part * half, half), :
            ].astype(F32)
            bias_ref[pl.ds(layer, 1), pl.ds(core * units + part * half, half)] = small[core][
                19 + part : 20 + part
            ]
        down_ref[0, pl.ds(core * units, units), :] = both_ref[core, 0, pl.ds(units, units), :].astype(F32)
        out_ref[0, pl.ds(core * heads, heads), :] = both_ref[
            core, 0, pl.ds(2 * units + 3 * heads, heads), :
        ].astype(F32)
    for at, ref in enumerate((q_ref, k_ref, v_ref)):
        here = pl.ds(2 * units + at * heads, heads)
        ref[0] = jnp.concatenate((both_ref[0, 0, here, :], both_ref[1, 0, here, :]), axis=0).astype(F32).T
    for row, ref in zip((0, 1, 2, 3, 16, 17, 18), small_refs):
        ref[pl.ds(layer, 1), :] = (small[0] + small[1])[row : row + 1, 0 : ref.shape[1]]


def finish(both, units, heads):
    _, layers, rows, half = both.shape
    shapes = [(half, 2 * units), (2 * units, half)] + [(half, 2 * heads)] * 3 + [(2 * heads, half)]
    small = [2 * units, half, half, HEAD_DIM, HEAD_DIM, half, half, half]

    def spec(shape):
        return pl.BlockSpec((1,) + shape, lambda l: (l,) + (0,) * len(shape))

    return pl.pallas_call(
        finish_kernel,
        grid=(layers,),
        in_specs=[pl.BlockSpec((2, 1, rows, half), lambda l: (0, l, 0, 0))],
        out_specs=[spec(shape) for shape in shapes]
        + [pl.BlockSpec((layers, size), lambda l: (0, 0)) for size in small],
        out_shape=[jax.ShapeDtypeStruct((layers,) + s, F32) for s in shapes]
        + [jax.ShapeDtypeStruct((layers, size), F32) for size in small],
        compiler_params=pltpu.CompilerParams(vmem_limit_bytes=48 * 2**20),
        name="finish",
    )(both)


LAYER_ROWS = 2432


def pack_copies(first, base, units, heads, width):
    half = width // 2
    copies = []
    for i in range(2):
        for j in range(2):
            copies.append((first, (i * half, half), (j * half, half), base + j * half, i * half))
    row = base + units
    for at, size in ((1, units), (2, 3 * heads), (3, heads), (4, 16), (5, 16)):
        copies.append((first + at, (0, size), (0, width), row, 0))
        row += size
    return copies


def shards(
    tokens, ln1_gain, ln1_shift, w_query, w_key, w_value, query_gain, key_gain, w_out,
    ln2_gain, ln2_shift, w_up, up_bias, w_down, down_bias, cotangent,
):
    heads_here = w_query.shape[2] // 2
    units_here = w_up.shape[2] // 2
    gains = jnp.stack((query_gain, key_gain), axis=2)
    resid, w_qkv, later, vectors = arrive(
        tokens, w_query, w_key, w_value, (ln1_gain, ln1_shift, ln2_gain, ln2_shift, down_bias)
    )
    width = resid.shape[1]
    caches = []
    for at in range(2):
        last = at == 1
        resid_two, seen_one, qkv, mixed, total, out_here, up_here, down_here = attend_forward(
            at, resid, w_qkv, gains[at], vectors[at], w_out, w_up, w_down
        )
        result, seen_two, active, slope, *side = feed_forward(
            at, last, resid_two, up_here, up_bias, down_here, vectors[at], cotangent if last else later
        )
        caches.append(
            (
                (resid_two, seen_two, active, slope, up_here, down_here, vectors[at]),
                (resid, seen_one, qkv, mixed, total, w_qkv, out_here, gains[at], vectors[at]),
            )
        )
        resid, w_qkv = result, side[0]
    grad, low = side
    parts, copies = [], []
    for at in (1, 0):
        grad, grad_up, grad_down, small_two = feed_backward(grad, *caches[at][0])
        grad, grad_qkv, grad_out, small_one = attend_backward(grad, *caches[at][1])
        copies += pack_copies(len(parts), at * LAYER_ROWS, units_here, heads_here, width)
        parts += [grad_up, grad_down, grad_qkv, grad_out, small_one, small_two]
    both_cores, out, grad_tokens = reduce_all(result, low, grad, parts, copies, 2 * LAYER_ROWS, 1)
    both_cores = both_cores.reshape(2, 2, LAYER_ROWS, width // 2)
    (
        grad_up, grad_down, grad_q, grad_k, grad_v, grad_out, grad_up_bias,
        grad_one_gain, grad_one_shift, grad_query_gain, grad_key_gain,
        grad_two_gain, grad_two_shift, grad_down_bias,
    ) = finish(both_cores, units_here, heads_here)
    return (
        out, grad_tokens, grad_one_gain, grad_one_shift, grad_q, grad_k, grad_v,
        grad_query_gain, grad_key_gain, grad_out, grad_two_gain, grad_two_shift,
        grad_up, grad_up_bias, grad_down, grad_down_bias,
    )


def solution(mesh):
    fine = Mesh(mesh.devices.reshape(4, 4, 2, 2, 2), ("x", "z", "core", "row", "col"))
    rows = ("x", "z", "core", "row")
    in_specs = (
        P(rows, "col"),
        P(None, "col"),
        P(None, "col"),
        P(None, "col", "row"),
        P(None, "col", "row"),
        P(None, "col", "row"),
        P(),
        P(),
        P(None, "row", "col"),
        P(None, "col"),
        P(None, "col"),
        P(None, "col", "row"),
        P(None, "row"),
        P(None, "row", "col"),
        P(None, "col"),
        P(rows, "col"),
    )
    out_specs = (P(rows, "col"),) * 2 + in_specs[1:15]
    return jax.shard_map(shards, mesh=fine, in_specs=in_specs, out_specs=out_specs, check_vma=False)
```

```python
import functools

import jax
import jax.numpy as jnp
from jax import lax
from jax.experimental import pallas as pl
from jax.experimental.pallas import tpu as pltpu
from jax.sharding import Mesh, PartitionSpec as P

HEAD_DIM = 64
EPS = 1e-06
LOG2E = 1.4426950408889634
BF = jnp.bfloat16
F32 = jnp.float32
GROUP = ("core", "row", "col")
BLOCK = 256


def dot(left, right, left_axis=1, right_axis=0):
    return lax.dot_general(
        left, right, (((left_axis,), (right_axis,)), ((), ())), preferred_element_type=F32
    )


MESH = pl.DeviceIdType.MESH
ROWS = 256
STEP = 128


def norm(resid):
    mean = jnp.mean(resid, axis=1, keepdims=True)
    centred = resid - mean
    factor = lax.rsqrt(jnp.mean(centred * centred, axis=1, keepdims=True) + EPS)
    return centred * factor, factor


def norm_back(grad, normal, factor, gain):
    scaled = grad * gain
    first = jnp.mean(scaled, axis=1, keepdims=True)
    second = jnp.mean(scaled * normal, axis=1, keepdims=True)
    return factor * (scaled - first - normal * second)


def head_norm(values):
    mean = jnp.mean(values, axis=0, keepdims=True)
    centred = values - mean
    factor = lax.rsqrt(jnp.mean(centred * centred, axis=0, keepdims=True) + EPS)
    return centred * factor, factor


def head_norm_back(grad, normal, factor, gain):
    scaled = grad * gain
    first = jnp.mean(scaled, axis=0, keepdims=True)
    second = jnp.mean(scaled * normal, axis=0, keepdims=True)
    return factor * (scaled - first - normal * second)


SCALE2 = LOG2E * HEAD_DIM ** (-0.5)


def gelu_parts(hidden):
    square = hidden * hidden
    bent = jnp.tanh(0.7978845608 * hidden * (1.0 + 0.044715 * square))
    active = 0.5 * hidden * (1.0 + bent)
    slope = 0.5 * (1.0 + bent) + 0.5 * hidden * (1.0 - bent * bent) * (
        0.7978845608 * (1.0 + 3.0 * 0.044715 * square)
    )
    return active, slope


def group_device(core_flip, row_flip, col_flip):
    device = {}
    for name, flipped in zip(GROUP, (core_flip, row_flip, col_flip)):
        if flipped:
            device[name] = 1 - lax.axis_index(name)
    return device


def partners():
    return group_device(1, 0, 0), group_device(0, 1, 1), group_device(1, 1, 1)


def whole_group():
    return [group_device(i & 1, (i >> 1) & 1, i >> 2) for i in range(1, 8)]


def plane_neighbours():
    x, z = lax.axis_index("x"), lax.axis_index("z")
    around = ({"x": (x + 1) % 4}, {"x": (x + 3) % 4}, {"z": (z + 1) % 4}, {"z": (z + 3) % 4})
    return around, (x + 2 * z) % 4


class Quarters:
    def __init__(self, pieces, sems):
        self.sems, self.pieces = sems, pieces
        self.around, self.quarter = plane_neighbours()

    def cut(self, ref):
        size = ref.shape[0] // 4
        return ref.at[pl.ds(pl.multiple_of(self.quarter * size, 16), size), :]

    def fetch(self):
        self.first = [
            send(self.cut(source), self.cut(target), self.sems, 4 * at, device)
            for at, (source, target, device) in enumerate(self.pieces)
        ]

    def share(self):
        self.second = []
        for at, (_, target, _) in enumerate(self.pieces):
            self.first[at].wait_recv()
            here = self.cut(target)
            for spot in range(3):
                self.second.append(send(here, here, self.sems, 4 * at + 1 + spot, self.around[spot]))

    def arrive(self):
        for copy in self.second:
            copy.wait_recv()

    def close(self):
        for copy in self.first + self.second:
            copy.wait_send()


def image_spots():
    core, row, col = (lax.axis_index(name) for name in GROUP)
    flip = (col + core) % 2
    own = {"core": row, "row": flip, "col": col}
    other = {"core": row, "row": 1 - flip, "col": 1 - col}
    stays = jnp.logical_and(core == row, col == 0)
    return own, other, stays


def move(source, target, sems, at, device, stays):
    def remote():
        return pltpu.make_async_remote_copy(
            src_ref=source,
            dst_ref=target,
            send_sem=sems.at[0, at],
            recv_sem=sems.at[1, at],
            device_id=device,
            device_id_type=MESH,
        )

    @pl.when(jnp.logical_not(stays))
    def _():
        remote().start()

    @pl.when(stays)
    def _():
        pltpu.make_async_copy(source, target, sems.at[0, at]).start()

    def finish():
        @pl.when(jnp.logical_not(stays))
        def _():
            remote().wait()

        @pl.when(stays)
        def _():
            pltpu.make_async_copy(source, target, sems.at[0, at]).wait()

    return finish


class Home:
    def __init__(self, sems):
        core, row, col = (lax.axis_index(name) for name in GROUP)
        self.sems = sems
        self.sends = core == row
        self.stays = jnp.logical_and(self.sends, col == 0)
        self.leaves = jnp.logical_and(self.sends, col == 1)
        self.beside = {"core": (col + row) % 2, "col": 1 - col}
        self.waits = []

    def move(self, source, target, at):
        half = target.shape[1]

        def near():
            return self.copy(source.at[:, pl.ds(0, half)], target, 2 * at, at, group_device(1, 0, 0))

        def far():
            return self.copy(source.at[:, pl.ds(half, half)], target, 2 * at + 1, at, self.beside)

        def still():
            return pltpu.make_async_copy(source.at[:, pl.ds(0, half)], target, self.sems.at[0, 2 * at])

        pl.when(self.leaves)(lambda: near().start())
        pl.when(self.stays)(lambda: still().start())
        pl.when(self.sends)(lambda: far().start())

        def finish():
            pl.when(self.leaves)(lambda: near().wait_send())
            pl.when(self.stays)(lambda: still().wait())
            pl.when(self.sends)(lambda: far().wait_send())
            pl.when(jnp.logical_not(self.stays))(lambda: near().wait_recv())

        self.waits.append(finish)

    def copy(self, source, target, send_at, recv_at, device):
        return pltpu.make_async_remote_copy(
            src_ref=source,
            dst_ref=target,
            send_sem=self.sems.at[0, send_at],
            recv_sem=self.sems.at[1, recv_at],
            device_id=device,
            device_id_type=MESH,
        )

    def close(self):
        for finish in self.waits:
            finish()


def local(source, target, sems, at):
    copy = pltpu.make_async_copy(source, target, sems.at[0, at])
    copy.start()
    return copy


def greet(devices):
    barrier = pltpu.get_barrier_semaphore()
    for device in devices:
        pl.semaphore_signal(barrier, inc=1, device_id=device, device_id_type=MESH)


def meet(devices):
    pl.semaphore_wait(pltpu.get_barrier_semaphore(), len(devices))


def send(source, target, sems, at, device):
    copy = pltpu.make_async_remote_copy(
        src_ref=source,
        dst_ref=target,
        send_sem=sems.at[0, at],
        recv_sem=sems.at[1, at],
        device_id=device,
        device_id_type=MESH,
    )
    copy.start()
    return copy


class Totals:
    def __init__(self, chip, core_out, core_in, cross_out, cross_in, sems, partner, cross):
        self.refs = (chip, core_out, core_in, cross_out, cross_in)
        self.sems, self.partner, self.cross = sems, partner, cross
        self.copies = []

    def run(self, compute, ready):
        chip, core_out, core_in, cross_out, cross_in = self.refs
        rows = chip.shape[0]
        count = rows // STEP
        core_copies, cross_copies = [], []

        def pass_on(at):
            here = pl.ds(at * STEP, STEP)
            core_copies[at].wait_recv()
            total = chip[here, :] + core_in[here, :].astype(F32)
            chip[here, :] = total
            if cross_out is not None:
                cross_out[here, :] = total.astype(BF)
                cross_copies.append(
                    send(cross_out.at[here, :], cross_in.at[here, :], self.sems, count + at, self.cross)
                )

        for at in range(count):
            here = pl.ds(at * STEP, STEP)
            chip[here, :] = compute(at * STEP)
            if at > 0:
                pass_on(at - 1)
            ready(at * STEP)
            core_out[here, :] = compute(rows + at * STEP).astype(BF)
            core_copies.append(
                send(core_out.at[here, :], core_in.at[here, :], self.sems, at, self.partner)
            )
        pass_on(count - 1)
        self.cross_copies = cross_copies
        self.copies = core_copies + cross_copies

    def chunk(self, row):
        chip, _, _, _, cross_in = self.refs
        here = pl.ds(row, STEP)
        self.cross_copies[row // STEP].wait_recv()
        half = chip.shape[1] // 2
        other = cross_in[here, :].astype(F32)
        return chip[here, :] + jnp.concatenate((other[:, half:], other[:, :half]), axis=1)

    def close(self):
        for copy in self.copies:
            copy.wait_send()


def when_starting(copies):
    return lambda row: copies[row // ROWS].wait_recv() if row % ROWS == 0 else None


def spread(fill, whole, sems, partner):
    rows = whole.shape[0] // 2
    copies = []
    for at in range(rows // ROWS):
        here = pl.ds(at * ROWS, ROWS)
        whole[here, :] = fill(at * ROWS)
        if at == 0:
            yield None
        copies.append(
            send(whole.at[here, :], whole.at[pl.ds(rows + at * ROWS, ROWS), :], sems, at, partner)
        )
    yield copies


def fill_and_send(fill, whole, sems, devices):
    steps = spread(fill, whole, sems, devices[0])
    next(steps)
    meet(devices)
    return next(steps)


def arrive_kernel(
    token_ref, wq_load, wk_load, wv_load, one_gain, one_shift, two_gain, two_shift, bias_load,
    out_ref, w_qkv_ref, later_ref, vector_ref,
    landed, sems, share_sems,
):
    around, _ = plane_neighbours()
    devices = whole_group() + list(around)
    greet(devices)
    core = lax.axis_index("core")
    own, other, stays = image_spots()
    beside = group_device(0, 0, 1)
    half = token_ref.shape[1]
    meet(devices)
    finish = move(token_ref, landed.at[:, pl.ds(0, half)], sems, 0, own, stays)
    copies = [send(token_ref, landed.at[:, pl.ds(half, half)], sems, 1, other)]
    span = w_qkv_ref.shape[0] // 3

    def turned(ref, layer):
        whole = ref[layer].astype(F32).T
        return jnp.where(core == 0, whole[:span], whole[span:]).astype(BF)

    loads = (wq_load, wk_load, wv_load)
    for at, load in enumerate(loads):
        w_qkv_ref[pl.ds(at * span, span), 0:half] = turned(load(), 0)
    shared = Quarters(
        [(w_qkv_ref.at[:, pl.ds(0, half)], w_qkv_ref.at[:, pl.ds(half, half)], beside)], share_sems
    )
    shared.fetch()
    refs = [load() for load in (one_gain, one_shift, two_gain, two_shift, bias_load)]
    for layer in range(vector_ref.shape[0]):
        rows = [ref[layer : layer + 1, :] for ref in refs]
        vector_ref[layer, :, 0:half] = jnp.concatenate(rows + [jnp.zeros((3, half), F32)], axis=0)
    copies.append(
        send(vector_ref.at[:, :, pl.ds(0, half)], vector_ref.at[:, :, pl.ds(half, half)], sems, 2, beside)
    )
    for at, load in enumerate(loads):
        later_ref[pl.ds(at * span, span), :] = turned(load(), 1)
    shared.share()
    finish()
    copies[0].wait()
    out_ref[...] = landed[...].astype(F32)
    copies[1].wait()
    shared.arrive()
    shared.close()


class Weights(Quarters):
    def __init__(self, layer, raws, targets, keep_sems, share_sems):
        raw_out, raw_up, raw_down = raws
        w_out, w_up, w_down = targets
        beside, cross, across = self.devices()
        core = lax.axis_index("core")
        units, half, span = w_up.shape[1], w_up.shape[0] // 2, w_out.shape[0] // 4
        here = pl.ds(pl.multiple_of(core * units, units), units)
        up, down = raw_up.at[layer, :, here], raw_down.at[layer, here, :]
        pieces = [
            (up, w_up.at[pl.ds(half, half), :], beside),
            (down, w_down.at[:, pl.ds(half, half)], beside),
        ]
        self.kept = []
        for at in range(2):
            source = raw_out.at[layer, pl.ds((core + at - 2 * at * core) * span, span), :]
            for device, row, col in ((beside, 0, half), (cross, half, half), (across, half, 0)):
                pieces.append((source, w_out.at[pl.ds(row + at * span, span), pl.ds(col, half)], device))
            self.kept.append(
                local(source, w_out.at[pl.ds(at * span, span), pl.ds(0, half)], keep_sems, at)
            )
        self.kept.append(local(up, w_up.at[pl.ds(0, half), :], keep_sems, 2))
        self.kept.append(local(down, w_down.at[:, pl.ds(0, half)], keep_sems, 3))
        super().__init__(pieces, share_sems)

    @staticmethod
    def devices():
        return group_device(0, 0, 1), group_device(0, 1, 1), group_device(0, 1, 0)

    def arrive(self):
        super().arrive()
        for copy in self.kept:
            copy.wait()


def attend_forward_kernel(layer, resid_load, w_qkv_load, gain_load, vector_load, *refs):
    if layer == 0:
        raws, refs = refs[:3], refs[3:]
        out_ref, seen_ref, qkv_ref, mixed_ref, total_ref, w_out_ref, w_up_ref, w_down_ref = refs[:8]
        joined, seen_sems, head_sems, keep_sems, share_sems = refs[8:]
    else:
        w_out_load, out_ref, seen_ref, qkv_ref, mixed_ref, total_ref = refs[:6]
        joined, seen_sems, head_sems = refs[6:]
    near, cross, far = partners()
    devices = (near, cross, far)
    if layer == 0:
        devices += (Weights.devices()[0], Weights.devices()[2]) + plane_neighbours()[0]
    greet(devices)
    resid_ref, vector_ref = resid_load(), vector_load()
    rows = resid_ref.shape[0]
    heads = mixed_ref.shape[0] // HEAD_DIM
    span = heads * HEAD_DIM

    def fill(row):
        normal, _ = norm(resid_ref[pl.ds(row, ROWS), :])
        return (normal * vector_ref[0:1, :] + vector_ref[1:2, :]).astype(BF)

    copies = fill_and_send(fill, seen_ref, seen_sems, devices)
    if layer == 0:
        shared = Weights(layer, raws, (w_out_ref, w_up_ref, w_down_ref), keep_sems, share_sems)
        shared.fetch()
    w_qkv_ref = w_qkv_load()
    for at in range(2 * rows // ROWS):
        if at * ROWS >= rows:
            copies[at - rows // ROWS].wait_recv()
        here = pl.ds(at * ROWS, ROWS)
        qkv_ref[:, here] = dot(w_qkv_ref[...], seen_ref[here, :], 1, 1)
    gains = gain_load()[...]
    for head in range(heads):
        if layer == 0 and head == 1:
            shared.share()
        own = pl.ds(head * HEAD_DIM, HEAD_DIM)
        query = (head_norm(qkv_ref[own, :])[0] * gains[:, 0:1]).astype(BF)
        key = head_norm(qkv_ref[pl.ds(span + head * HEAD_DIM, HEAD_DIM), :])[0] * gains[:, 1:2]
        key_rows = key.T.astype(BF)
        value = qkv_ref[pl.ds(2 * span + head * HEAD_DIM, HEAD_DIM), :].astype(BF)
        for at in range(0, 2 * rows, BLOCK):
            expo = jnp.exp2(dot(key_rows, query[:, at : at + BLOCK]) * SCALE2)
            total = jnp.sum(expo, axis=0, keepdims=True)
            mixed = (dot(value, expo.astype(BF)) * (1.0 / total)).astype(BF)
            mixed_ref[own, at : at + BLOCK] = mixed
            if at < rows:
                joined[own, at : at + BLOCK] = mixed
            total_ref[head : head + 1, at : at + BLOCK] = jnp.log2(total)
        mine, others = pl.ds(0, rows), pl.ds(rows, rows)
        for spot, (device, columns) in enumerate(((near, others), (cross, mine), (far, others))):
            copies.append(
                send(
                    mixed_ref.at[own, columns],
                    joined.at[pl.ds((spot + 1) * span + head * HEAD_DIM, HEAD_DIM), :],
                    head_sems,
                    head * 3 + spot,
                    device,
                )
            )
    if layer == 0:
        shared.arrive()
    else:
        w_out_ref = w_out_load()
    for copy in copies[-3 * heads :]:
        copy.wait_recv()
    for at in range(rows // ROWS):
        here = pl.ds(at * ROWS, ROWS)
        out_ref[here, :] = resid_ref[here, :] + dot(joined[:, here], w_out_ref[...], 0, 0)
    for copy in copies:
        copy.wait_send()
    if layer == 0:
        shared.close()


def feed_forward_kernel(layer, last, resid_load, w_up_load, bias_load, w_down_load, vector_load, side_ref, *refs):
    if last:
        out_ref, seen_ref, active_ref, slope_ref, side_out, low_ref = refs[:6]
        chip, core_out, core_in, landed, seen_sems, total_sems, side_sems = refs[6:]
        cross_out, cross_in = None, None
    else:
        raws, refs = refs[:3], refs[3:]
        out_ref, seen_ref, active_ref, slope_ref, side_out = refs[:5]
        chip, core_out, core_in, cross_out, cross_in = refs[8:13]
        seen_sems, total_sems, side_sems, keep_sems, share_sems = refs[13:]
    near, cross, _ = partners()
    beside = group_device(0, 0, 1)
    devices = whole_group() if last else (near, cross) + Weights.devices()[::2] + plane_neighbours()[0]
    greet(devices)
    core = lax.axis_index("core")
    resid_ref, vector_ref = resid_load(), vector_load()
    half = resid_ref.shape[1] // 2

    def fill(row):
        normal, _ = norm(resid_ref[pl.ds(row, ROWS), :])
        return (normal * vector_ref[2:3, :] + vector_ref[3:4, :]).astype(BF)

    if last:
        steps = spread(fill, seen_ref, seen_sems, near)
        next(steps)
        meet(devices)
        copies = next(steps)
        own, other, stays = image_spots()
        arrived = move(side_ref, landed.at[:, pl.ds(0, half)], side_sems, 0, own, stays)
        side = send(side_ref, landed.at[:, pl.ds(half, half)], side_sems, 1, other)
    else:
        copies = fill_and_send(fill, seen_ref, seen_sems, devices)
        kept = local(side_ref, side_out.at[:, pl.ds(0, half)], side_sems, 0)
        side = send(side_ref, side_out.at[:, pl.ds(half, half)], side_sems, 1, beside)
        shared = Weights(layer + 1, raws, refs[5:8], keep_sems, share_sems)
        shared.fetch()

    w_up_ref, w_down_ref, bias_ref = w_up_load(), w_down_load(), bias_load()
    units = w_up_ref.shape[1]
    bias = bias_ref[layer : layer + 1, pl.ds(pl.multiple_of(core * units, units), units)]

    def compute(row):
        here = pl.ds(row, STEP)
        hidden = dot(seen_ref[here, :], w_up_ref[...]) + bias
        active, slope = gelu_parts(hidden)
        active = active.astype(BF)
        active_ref[here, :] = active
        slope_ref[here, :] = slope.astype(BF)
        return dot(active, w_down_ref[...])

    totals = Totals(chip, core_out, core_in, cross_out, cross_in, total_sems, near, cross)
    totals.run(compute, when_starting(copies))
    if not last:
        shared.share()
    for row in range(0, resid_ref.shape[0], STEP):
        here = pl.ds(row, STEP)
        total = chip[here, :] if last else totals.chunk(row)
        out_ref[here, :] = resid_ref[here, :] + (total + vector_ref[4:5, :])
        if last:
            low_ref[here, :] = total.astype(BF)
    for copy in copies:
        copy.wait_send()
    totals.close()
    side.wait()
    if last:
        arrived()
        side_out[...] = landed[...].astype(F32)
    else:
        kept.wait()
        shared.arrive()
        shared.close()


def feed_backward_kernel(plan, *refs):
    refs = iter(refs)

    def take(count):
        return [next(refs) for _ in range(count)]

    grad_load, resid_load, seen_load, active_load, slope_load, w_up_load, w_down_load, vector_load = take(8)
    parts = take(plan["parts"])
    if parts:
        out_ref, small_ref, shard_ref, first_ref = take(4)
    else:
        out_ref, small_ref, up_ref, down_ref = take(4)
    branch, hidden, chip, core_out, core_in, cross_out, cross_in, seen_sems, total_sems = take(9)
    near, cross, _ = partners()
    devices = (near, cross)
    steps = iter(())
    if parts:
        (load_sems,) = take(1)
        beside = take_scatter(ATTEND_SMALL_CHUNKS, refs)
        feed_work, feed_landing, feed_sems = take_scatter(FEED_CHUNKS, refs, 0, 1)
        steps = loaded_scatter(ATTEND_SMALL_CHUNKS, parts, plan["copies"], load_sems, *beside)
        devices += tuple(device for device, _ in link_bits().values())
    greet(devices)
    next(steps, None)
    grad_ref = grad_load()
    width = grad_ref.shape[1]
    copies = fill_and_send(
        lambda row: grad_ref[pl.ds(row, ROWS), :].astype(BF), branch, seen_sems, devices
    )
    next(steps, None)
    w_down_ref, slope_ref, w_up_ref = w_down_load(), slope_load(), w_up_load()

    def compute(row):
        here = pl.ds(row, STEP)
        active_grad = dot(branch[here, :], w_down_ref[...], 1, 1)
        low = (active_grad * slope_ref[here, :].astype(F32)).astype(BF)
        hidden[here, :] = low
        return dot(low, w_up_ref[...], 1, 1)

    totals = Totals(chip, core_out, core_in, cross_out, cross_in, total_sems, near, cross)
    totals.run(compute, when_starting(copies))
    next(steps, None)
    rows = grad_ref.shape[0]
    active_ref, seen_ref, resid_ref, vector_ref = active_load(), seen_load(), resid_load(), vector_load()
    half = width // 2
    units = hidden.shape[1]
    for at in range(0, width, ROWS):
        down_part = dot(active_ref[:, at : at + ROWS], branch[...], 0, 0).astype(BF)
        up_part = dot(seen_ref[:, at : at + ROWS], hidden[...], 0, 0).astype(BF)
        if not parts:
            down_ref[at : at + ROWS, :] = down_part
            up_ref[at : at + ROWS, :] = up_part
            continue
        feed_work[units + at : units + at + ROWS, :] = down_part
        for row in range(at, at + ROWS, 128):
            for col in range(0, units, half):
                feed_work[col + row % half : col + row % half + 128, row // half * half : row // half * half + half] = (
                    up_part[row - at : row - at + 128, col : col + half]
                )
    if parts:
        next(steps, None)
        feed_steps = scatter(FEED_CHUNKS, feed_work, feed_landing, feed_sems, 0, 1)
        next(feed_steps)
    bias_down = jnp.sum(branch[0:rows, :].astype(F32), axis=0, keepdims=True)
    bias_up = jnp.sum(hidden[...].astype(F32), axis=0, keepdims=True)
    gain_sum = jnp.zeros((1, width), F32)
    shift_sum = jnp.zeros((1, width), F32)
    for row in range(0, rows, STEP):
        here = pl.ds(row, STEP)
        grad = totals.chunk(row)
        normal, factor = norm(resid_ref[here, :])
        gain_sum = gain_sum + jnp.sum(grad * normal, axis=0, keepdims=True)
        shift_sum = shift_sum + jnp.sum(grad, axis=0, keepdims=True)
        out_ref[here, :] = grad_ref[here, :] + norm_back(grad, normal, factor, vector_ref[2:3, :])
        if row in (STEP, 2 * STEP):
            next(steps, None)
    height = small_ref.shape[0]
    small_ref[...] = jnp.concatenate(
        [gain_sum, shift_sum, bias_down]
        + [jnp.concatenate((bias_up[:, i * half : (i + 1) * half],) * 2, axis=1) for i in range(2)]
        + [jnp.zeros((height - 5, width), F32)],
        axis=0,
    ).astype(small_ref.dtype)
    for _ in steps:
        pass
    if parts:
        keep_shards(beside[1], shard_ref)
        for _ in feed_steps:
            pass
        row = 0
        for landed in feed_landing:
            first_ref[pl.ds(row, landed.shape[0]), 0 : landed.shape[1]] = landed[...]
            row += landed.shape[0]
    for copy in copies:
        copy.wait_send()
    totals.close()


def attend_backward_kernel(plan, *refs):
    refs = iter(refs)

    def take(count):
        return [next(refs) for _ in range(count)]

    last = plan["last"]
    grad_load, resid_load, seen_load, qkv_load, mixed_load, total_load = take(6)
    w_qkv_load, w_out_load, gain_load, vector_load = take(4)
    if last:
        first_load, shard_load, other_shard_load, vec_load, final_load, low_ref = take(6)
        result_ref, token_in, layer_both, feed_both, tail_both, vec_pair = take(6)
    else:
        parts = take(2)
        out_ref, grad_qkv_ref, grad_out_ref, small_ref, shard_ref = take(5)
    proj, mixed_grad, qkv_grad, gains_own, gains_in = take(5)
    chip, core_out, core_in, cross_out, cross_in, seen_sems, total_sems, gain_sems = take(8)
    if last:
        _, feed_landing, feed_sems = take_scatter(FEED_CHUNKS, refs, 1, 5)
        feed_steps = scatter(FEED_CHUNKS, first_load.target, feed_landing, feed_sems, 1, 5)
    else:
        (load_sems,) = take(1)
        feed_beside = take_scatter(FEED_CHUNKS, refs)
        feed_steps = loaded_scatter(FEED_CHUNKS, parts, plan["copies"], load_sems, *feed_beside)
    links = link_bits()
    near, cross, _ = partners()
    devices = (near, cross) + tuple(device for device, _ in links.values())
    if last:
        low_in, result_low, token_low, home_sems = take(4)
        vec, vec_x, vec_z, vec_mid, vec_col, vec_sems = take(6)
        tail_work, tail_landing, tail_sems = take_scatter(ATTEND_CHUNKS, refs)
        layer_gather = take(2)
        feed_gather = take(2)
        tail_gather = take(2)
        x, z = lax.axis_index("x"), lax.axis_index("z")
        devices = tuple(whole_group()) + tuple(links[name][0] for name in ("x1", "x2", "z1", "z2"))
        devices += ({"x": (x + 2) % 4}, {"z": (z + 2) % 4})
    greet(devices)
    if not last:
        next(feed_steps)
    grad_ref = grad_load()
    rows, width = grad_ref.shape
    half = width // 2
    copies = fill_and_send(
        lambda row: grad_ref[pl.ds(row, ROWS), :].astype(BF), proj, seen_sems, devices
    )
    if last:
        first_load()
    next(feed_steps)
    if last:
        home = Home(home_sems)

        def low_copy():
            return home.copy(low_ref, low_in, 11, 11, cross)

        pl.when(jnp.logical_not(home.sends))(lambda: low_copy().start())
        shards = [shard_load().at[pl.ds(16 * at, 16), :] for at in range(len(FEED_CHUNKS))]
        shards += [other_shard_load().at[pl.ds(16 * at, 16), :] for at in range(len(ATTEND_SMALL_CHUNKS))]
        layer_steps = gather(LAYER_CHUNKS, shards, layer_both, *layer_gather)
        next(layer_steps)
    w_out_ref = w_out_load()
    span = mixed_grad.shape[0]
    for at in range(2 * rows // ROWS):
        if at * ROWS >= rows:
            copies[at - rows // ROWS].wait_recv()
        here = pl.ds(at * ROWS, ROWS)
        mixed_grad[:, here] = dot(w_out_ref[pl.ds(0, span), :], proj[here, :], 1, 1).astype(BF)
    gains, qkv_ref, total_ref = gain_load()[...], qkv_load(), total_load()
    scale = HEAD_DIM ** (-0.5)
    gains_sum = jnp.zeros((HEAD_DIM, 2), F32)
    slot = 0
    for head in range(span // HEAD_DIM):
        own = pl.ds(head * HEAD_DIM, HEAD_DIM)
        key_at = pl.ds(span + head * HEAD_DIM, HEAD_DIM)
        value_at = pl.ds(2 * span + head * HEAD_DIM, HEAD_DIM)
        query_normal, query_factor = head_norm(qkv_ref[own, :])
        key_normal, key_factor = head_norm(qkv_ref[key_at, :])
        query = (query_normal * gains[:, 0:1]).astype(BF)
        key_full = key_normal * gains[:, 1:2]
        key = key_full.astype(BF)
        key_rows = key_full.T.astype(BF)
        value_rows = qkv_ref[value_at, :].T.astype(BF)
        key_sum = jnp.zeros(key.shape, F32)
        value_sum = jnp.zeros(key.shape, F32)
        query_parts = []
        for at in range(0, 2 * rows, BLOCK):
            grad = mixed_grad[own, at : at + BLOCK]
            logits = dot(key_rows, query[:, at : at + BLOCK]) * SCALE2
            probs = jnp.exp2(logits - total_ref[head : head + 1, at : at + BLOCK])
            pulled = dot(value_rows, grad)
            delta = jnp.sum(probs * pulled, axis=0, keepdims=True)
            score_grad = (probs * (pulled - delta)).astype(BF)
            query_parts.append(dot(key, score_grad))
            key_sum = key_sum + dot(query[:, at : at + BLOCK], score_grad, 1, 1)
            value_sum = value_sum + dot(grad, probs.astype(BF), 1, 1)
            slot += 1
            if last and slot in (3, 6, 10):
                next(layer_steps, None)
            if slot in ((5, 9) if last else (9,)):
                next(feed_steps)
        query_sum = jnp.concatenate(query_parts, axis=1) * scale
        key_sum = key_sum * scale
        qkv_grad[own, :] = head_norm_back(query_sum, query_normal, query_factor, gains[:, 0:1]).astype(BF)
        qkv_grad[key_at, :] = head_norm_back(key_sum, key_normal, key_factor, gains[:, 1:2]).astype(BF)
        qkv_grad[value_at, :] = value_sum.astype(BF)
        gains_sum = gains_sum + jnp.concatenate(
            (
                jnp.sum(query_sum * query_normal, axis=1, keepdims=True),
                jnp.sum(key_sum * key_normal, axis=1, keepdims=True),
            ),
            axis=1,
        )
    square = jnp.concatenate((gains_sum, jnp.zeros((HEAD_DIM, 126), F32)), axis=1)
    gains_own[...] = jnp.concatenate((square, jnp.zeros((128 - HEAD_DIM, 128), F32)), axis=0).T[0:8]
    gains_copy = send(gains_own, gains_in, gain_sems, 0, cross)
    w_qkv_ref = w_qkv_load()

    def compute(row):
        return dot(qkv_grad[:, pl.ds(row, STEP)], w_qkv_ref[...], 0, 0)

    totals = Totals(chip, core_out, core_in, cross_out, cross_in, total_sems, near, cross)
    seen_ref, mixed_ref, resid_ref, vector_ref = seen_load(), mixed_load(), resid_load(), vector_load()
    if last:
        grad_qkv_ref, grad_out_ref = tail_work.at[pl.ds(0, 3 * span), :], tail_work.at[pl.ds(3 * span, span), :]

    def weight_grads():
        for at in range(0, 3 * span, span):
            here = pl.ds(at, span)
            grad_qkv_ref[here, :] = dot(qkv_grad[here, :], seen_ref[...]).astype(BF)
        grad_out_ref[...] = dot(mixed_ref[...], proj[...]).astype(BF)

    sums = [jnp.zeros((1, width), F32), jnp.zeros((1, width), F32)]

    def final_chunk(row):
        here = pl.ds(row, STEP)
        grad = totals.chunk(row)
        normal, factor = norm(resid_ref[here, :])
        sums[0] = sums[0] + jnp.sum(grad * normal, axis=0, keepdims=True)
        sums[1] = sums[1] + jnp.sum(grad, axis=0, keepdims=True)
        return grad_ref[here, :] + norm_back(grad, normal, factor, vector_ref[0:1, :])

    def small_rows(height):
        gains_copy.wait()
        shared = gains_own[0:2, :] + gains_in[0:2, :]
        blank = jnp.zeros((2, half - 128), F32)
        return jnp.concatenate(
            sums
            + [jnp.concatenate((shared, blank, shared, blank), axis=1), jnp.zeros((height - 4, width), F32)],
            axis=0,
        )

    if not last:
        totals.run(compute, lambda row: next(feed_steps) if row == 3 * STEP else None)
        weight_grads()
        next(feed_steps)
        for row in range(0, rows, STEP):
            out_ref[pl.ds(row, STEP), :] = final_chunk(row)
            if row == STEP:
                next(feed_steps)
        small_ref[...] = small_rows(16).astype(BF)
        for _ in feed_steps:
            pass
        keep_shards(feed_beside[1], shard_ref)
        for copy in copies:
            copy.wait_send()
        totals.close()
        return

    def whole(first, second):
        yield from first
        yield from second

    weight_grads()
    tail = whole(
        scatter(ATTEND_CHUNKS, tail_work, tail_landing, tail_sems),
        gather(ATTEND_CHUNKS, tail_landing[4::5], tail_both, *tail_gather),
    )
    next(tail)
    for _ in layer_steps:
        pass
    next(feed_steps)
    feed = whole(feed_steps, gather(FEED_CHUNKS, feed_landing[3::4], feed_both, *feed_gather))
    totals.run(compute, lambda row: next(feed) if row == 3 * STEP else None)
    final_ref = final_load()

    @pl.when(home.sends)
    def _():
        low_copy().wait_recv()
        other = low_in[...].astype(F32)
        other = jnp.concatenate((other[:, half:], other[:, :half]), axis=1)
        result_low[...] = (final_ref[...] + other).astype(BF)

    pl.when(jnp.logical_not(home.sends))(lambda: low_copy().wait_send())
    home.move(result_low, result_ref, 0)

    def token_chunk(row):
        here = pl.ds(row, STEP)
        token_low[here, :] = final_chunk(row).astype(BF)
        home.move(token_low.at[here, :], token_in.at[here, :], 1 + row // STEP)

    next(tail)
    next(feed)
    next(tail)
    token_chunk(0)
    token_chunk(STEP)
    next(feed)
    next(tail)
    token_chunk(2 * STEP)
    next(feed)
    next(tail)
    token_chunk(3 * STEP)
    vec[...] = jnp.concatenate((small_rows(8), vec_load()[...]), axis=0)
    vec_copies = []

    def share(source, landing, axis, place, at):
        batch = []
        for step in range(1, 4):
            batch.append(
                send(source, landing.at[step - 1], vec_sems, at + step - 1, {axis: (place + step) % 4})
            )
        vec_copies.extend(batch)
        return batch

    def collect(source, landing, batch):
        for copy in batch:
            copy.wait_recv()
        return (source[...] + landing[0]) + (landing[1] + landing[2])

    batch = share(vec, vec_x, "x", x, 0)
    next(tail)
    next(feed)
    vec_mid[0] = collect(vec, vec_x, batch)
    batch = share(vec_mid.at[0], vec_z, "z", z, 3)
    next(tail)
    vec_mid[1] = collect(vec_mid.at[0], vec_z, batch)
    vec_copies.append(send(vec_mid.at[1, :, pl.ds(half, half)], vec_col, vec_sems, 6, links["col"][0]))
    next(tail)
    vec_copies[-1].wait_recv()
    core = lax.axis_index("core")
    vec_pair[core] = vec_mid[1, :, 0:half] + vec_col[...]
    vec_copies.append(send(vec_pair.at[core], vec_pair.at[core], vec_sems, 7, near))
    next(tail)
    vec_copies[-1].wait_recv()
    for _ in feed:
        pass
    for _ in tail:
        pass
    home.close()
    for copy in copies + vec_copies:
        copy.wait_send()
    totals.close()


class Load:
    def __init__(self, source, target, sem):
        self.copy = pltpu.make_async_copy(source, target, sem)
        self.copy.start()
        self.target, self.waited = target, False

    def __call__(self):
        if not self.waited:
            self.copy.wait()
            self.waited = True
        return self.target


def call(kernel, name, collective_id, inputs, outs, scratch):
    vmem = pl.BlockSpec(memory_space=pltpu.VMEM)
    hbm = pl.BlockSpec(memory_space=pl.ANY)

    def kind(spec):
        return spec[0] if isinstance(spec, tuple) and isinstance(spec[0], str) else "block"

    def bare(spec):
        return spec if kind(spec) == "block" else spec[1]

    kinds = [kind(spec) for spec in inputs]
    values = [bare(spec) for spec in inputs]
    loaded = [at for at, k in enumerate(kinds) if k == "load"]

    def body(*refs):
        refs = list(refs)
        staged, sems = refs[-1 - len(loaded) : -1], refs[-1]
        given = refs[: len(inputs)]
        loads = [Load(given[at], staged[i], sems.at[i]) for i, at in enumerate(loaded)]
        for at, load in zip(loaded, loads):
            given[at] = load
        kernel(*given, *refs[len(inputs) : -1 - len(loaded)])
        for load in loads:
            load()

    return pl.pallas_call(
        body,
        in_specs=[vmem if k == "block" else hbm for k in kinds],
        out_specs=[vmem if kind(spec) == "block" else hbm for spec in outs],
        out_shape=[jax.ShapeDtypeStruct(*bare(spec)) for spec in outs],
        scratch_shapes=scratch
        + [pltpu.VMEM(values[at].shape, values[at].dtype) for at in loaded]
        + [pltpu.SemaphoreType.DMA((max(1, len(loaded)),))],
        compiler_params=pltpu.CompilerParams(
            collective_id=collective_id,
            has_side_effects=collective_id is not None,
            vmem_limit_bytes=58 * 2**20,
        ),
        name=name,
    )(*values)


def pair_sems(count):
    return pltpu.SemaphoreType.DMA((2, count))


def total_scratch(rows, width):
    return [pltpu.VMEM((rows, width), F32)] + [pltpu.VMEM((rows, width), BF)] * 4


def total_sems(rows):
    return [pair_sems(rows // ROWS), pair_sems(2 * rows // STEP)]


def arrive(tokens, w_query, w_key, w_value, vectors):
    rows, half = tokens.shape
    span = w_query.shape[2] // 2
    layers = w_query.shape[0]
    return call(
        arrive_kernel,
        "arrive",
        10,
        [("hbm", tokens)] + [("load", value) for value in (w_query, w_key, w_value) + vectors],
        [
            ((rows, 2 * half), F32),
            ((3 * span, 2 * half), BF),
            ((3 * span, half), BF),
            ((layers, 8, 2 * half), F32),
        ],
        [pltpu.VMEM((rows, 2 * half), BF), pair_sems(3), pair_sems(4)],
    )


def weight_shapes(width, units):
    return [((width, width), BF), ((width, units), BF), ((units, width), BF)]


def attend_forward(layer, resid, w_qkv, gains, vectors, raws, w_out):
    rows, width = resid.shape
    span = w_qkv.shape[0] // 3
    inputs = [("load", value) for value in (resid, w_qkv, gains, vectors)]
    outs = [
        ((rows, width), F32),
        ((2 * rows, width), BF),
        ((3 * span, 2 * rows), F32),
        ((span, 2 * rows), BF),
        ((span // HEAD_DIM, 2 * rows), F32),
    ]
    scratch = [pltpu.VMEM((4 * span, rows), BF), pair_sems(rows // ROWS), pair_sems(3 * span // HEAD_DIM)]
    if layer == 0:
        inputs += [("hbm", value) for value in raws]
        outs += weight_shapes(width, raws[1].shape[2] // 2)
        scratch += [pair_sems(4), pair_sems(32)]
    else:
        inputs += [("load", w_out)]
    return call(
        functools.partial(attend_forward_kernel, layer),
        "attend_forward_%d" % layer,
        8 + layer,
        inputs,
        outs,
        scratch,
    )


def feed_forward(layer, last, resid, w_up, up_bias, w_down, vectors, side, raws):
    rows, width = resid.shape
    units = w_up.shape[1]
    outs = [((rows, width), F32), ((2 * rows, width), BF)] + [((2 * rows, units), BF)] * 2
    low = pltpu.VMEM((rows, width), BF)
    if last:
        outs += [((rows, width), F32), ((rows, width), BF)]
        scratch = [pltpu.VMEM((rows, width), F32), low, low, low]
    else:
        outs += [((side.shape[0], width), BF)] + weight_shapes(width, units)
        scratch = total_scratch(rows, width)
    scratch += total_sems(rows) + [pair_sems(2)]
    return call(
        functools.partial(feed_forward_kernel, layer, last),
        "feed_forward_%d" % layer,
        4 if last else 3,
        [("load", value) for value in (resid, w_up, up_bias, w_down, vectors)]
        + [("hbm", value) for value in (side,) + (() if last else raws)],
        outs,
        scratch if last else scratch + [pair_sems(4), pair_sems(32)],
    )


def feed_backward(operands, parts):
    grad, resid, seen, active, slope, w_up, w_down, vectors = operands
    rows, width = grad.shape
    units = w_up.shape[1]
    outs = [((rows, width), F32), ((8, width), F32) if parts else ((16, width), BF)]
    weight_outs = [((width, units), BF), ((units, width), BF)]
    scratch = [pltpu.VMEM((2 * rows, width), BF), pltpu.VMEM((2 * rows, units), BF)]
    scratch += total_scratch(rows, width) + total_sems(rows)
    copies, half = [], width // 2
    if parts:
        outs.append(((16 * len(ATTEND_SMALL_CHUNKS), half), BF))
        first_shapes = landing_shapes(FEED_CHUNKS, width, 0, 1)
        outs.append(((sum(shape[0] for shape in first_shapes), width), BF))
        scratch += [pltpu.SemaphoreType.DMA((len(parts),))] + scatter_scratch(ATTEND_SMALL_CHUNKS, width)
        scratch += scatter_scratch(FEED_CHUNKS, width, 0, 1)
        row = 0
        for at, part in enumerate(parts):
            copies.append((at, (0, part.shape[0]), (0, width), row, 0))
            row += part.shape[0]
    else:
        outs += weight_outs
    return call(
        functools.partial(feed_backward_kernel, {"parts": len(parts), "copies": copies}),
        "feed_backward_and_sum" if parts else "feed_backward",
        7 if parts else 5,
        [("load", value) for value in operands] + [("hbm", value) for value in parts],
        outs,
        scratch,
    )


def link_bits():
    x, z = lax.axis_index("x"), lax.axis_index("z")
    col = lax.axis_index("col")
    return {
        "x1": ({"x": x + 1 - 2 * (x % 2)}, ((x + 1) // 2) % 2),
        "x2": ({"x": 3 - x}, x // 2),
        "z1": ({"z": z + 1 - 2 * (z % 2)}, ((z + 1) // 2) % 2),
        "z2": ({"z": 3 - z}, z // 2),
        "col": ({"col": 1 - col}, None),
    }


ORDERS = (
    ("x1", "z1", "x2", "z2", "col"),
    ("z1", "x2", "z2", "col", "x1"),
    ("x2", "z2", "col", "x1", "z1"),
    ("z2", "col", "x1", "z1", "x2"),
    ("col", "x1", "z1", "x2", "z2"),
    ("x1", "z1", "x2", "z2", "col"),
    ("z1", "x2", "z2", "col", "x1"),
    ("x2", "z2", "col", "x1", "z1"),
    ("z2", "col", "x1", "z1", "x2"),
    ("col", "x2", "z2", "x1", "z1"),
)
UNIT = 256


def plan_chunks(rows, orders):
    return [(at * UNIT, UNIT, ORDERS[orders[at]]) for at in range(rows // UNIT)]


def step_shapes(rows, order, width):
    shapes = []
    for link in order:
        if link == "col":
            width //= 2
        else:
            rows //= 2
        shapes.append((rows, width))
    return shapes


def add_into(target, other, row, col_size):
    rows = target.shape[0]
    block = min(rows, 64)

    @pl.loop(0, rows // block)
    def _(at):
        here = pl.ds(pl.multiple_of(at * block, block), block)
        there = pl.ds(pl.multiple_of(row + at * block, 16), block)
        target[here, :] = (
            target[here, :].astype(F32) + other[there, :col_size].astype(F32)
        ).astype(BF)


def scatter(chunks, work, landing, sems, first=0, stop=5):
    links = link_bits()
    count = stop - first
    state, row = [], 0
    for start, rows, order in chunks:
        if first > 0:
            rows, width = step_shapes(rows, order, work.shape[1])[first - 1]
            state.append(work.at[pl.ds(row, rows), pl.ds(0, width)])
            row += rows
        else:
            state.append(work.at[pl.ds(start, rows), :])
    flight = [None] * len(chunks)
    sent = []

    def land(at, step):
        copy, keep_row, width = flight[at]
        copy.wait_recv()
        target = landing[at * count + step - first]
        add_into(target, state[at], keep_row, width)
        state[at] = target

    for step in range(first, stop):
        for at, (start, rows, order) in enumerate(chunks):
            if step > first:
                land(at, step - 1)
            device, bit = links[order[step]]
            landed = landing[at * count + step - first]
            size, width = landed.shape
            if bit is None:
                source = state[at].at[:, pl.ds(width, width)]
                keep_row = 0
            else:
                keep_row = bit * size
                source = state[at].at[pl.ds(pl.multiple_of((1 - bit) * size, size), size), :]
            copy = send(source, landed, sems, at * count + step - first, device)
            sent.append(copy)
            flight[at] = (copy, keep_row, width)
        yield
    for at in range(len(chunks)):
        land(at, stop - 1)
    for copy in sent:
        copy.wait_send()


def gather(chunks, shards, both, sems, core_sems):
    core = lax.axis_index("core")
    links = link_bits()
    sent, region = [], []
    for at, (start, rows, order) in enumerate(chunks):
        offset, size = 0, rows
        for link in order:
            if links[link][1] is not None:
                size //= 2
                offset = offset + links[link][1] * size
        both[core, pl.ds(pl.multiple_of(start + offset, 16), size), :] = shards[at][...]
        region.append((start + offset, size))
    back = [[link for link in reversed(order) if link != "col"] for _, _, order in chunks]
    waiting = [None] * len(chunks)

    def settle(at):
        copy, bit, size = waiting[at]
        copy.wait_recv()
        lo, _ = region[at]
        region[at] = (lo - bit * size, 2 * size)

    for step in range(4):
        for at in range(len(chunks)):
            if step > 0:
                settle(at)
            lo, size = region[at]
            device, bit = links[back[at][step]]
            here = both.at[core, pl.ds(pl.multiple_of(lo, 16), size), :]
            copy = send(here, here, sems, at * 4 + step, device)
            sent.append(copy)
            waiting[at] = (copy, bit, size)
        yield
    last = []
    for at, (start, rows, order) in enumerate(chunks):
        settle(at)
        here = both.at[core, pl.ds(start, rows), :]
        last.append(send(here, here, core_sems, at, {"core": 1 - core}))
    yield
    for copy in last:
        copy.wait_recv()
    for copy in sent + last:
        copy.wait_send()


def landing_shapes(chunks, width, first=0, stop=5):
    return [shape for _, size, order in chunks for shape in step_shapes(size, order, width)[first:stop]]


def scatter_scratch(chunks, width, first=0, stop=5):
    shapes = landing_shapes(chunks, width, first, stop)
    if first == 0:
        shapes = [(sum(size for _, size, _ in chunks), width)] + shapes
    return [pltpu.VMEM(shape, BF) for shape in shapes] + [pair_sems((stop - first) * len(chunks))]


def take_scatter(chunks, refs, first=0, stop=5):
    work = next(refs) if first == 0 else None
    return work, [next(refs) for _ in range((stop - first) * len(chunks))], next(refs)


def gather_scratch(chunks):
    return [pair_sems(4 * len(chunks)), pair_sems(len(chunks))]


def loaded_scatter(chunks, parts, copies, load_sems, work, landing, sems):
    loads = []
    for at, (source, rows, cols, row, col) in enumerate(copies):
        load = pltpu.make_async_copy(
            parts[source].at[pl.ds(rows[0], rows[1]), pl.ds(cols[0], cols[1])],
            work.at[pl.ds(row, rows[1]), pl.ds(col, cols[1])],
            load_sems.at[at],
        )
        load.start()
        loads.append(load)
    yield
    for load in loads:
        load.wait()
    yield from scatter(chunks, work, landing, sems)


def keep_shards(landing, shard_ref):
    for at, landed in enumerate(landing[4::5]):
        shard_ref[pl.ds(at * 16, 16), :] = landed[...]


FEED_CHUNKS = plan_chunks(6 * UNIT, (0, 1, 2, 3, 4, 9))
ATTEND_CHUNKS = plan_chunks(3 * UNIT, (0, 1, 2))
ATTEND_SMALL_CHUNKS = plan_chunks(4 * UNIT, (0, 1, 2, 3))
LAYER_CHUNKS = FEED_CHUNKS + [(start + 6 * UNIT, rows, order) for start, rows, order in ATTEND_SMALL_CHUNKS]


def feed_copies(first, base, units, width):
    half = width // 2
    copies = []
    for i in range(2):
        for j in range(2):
            copies.append((first, (i * half, half), (j * half, half), base + j * half, i * half))
    copies.append((first + 1, (0, units), (0, width), base + units, 0))
    return copies


def attend_backward(operands, parts, extras):
    grad, resid, seen, qkv, mixed, total, w_qkv, w_out, gains, vectors = operands
    rows, width = grad.shape
    half = width // 2
    span = mixed.shape[0]
    inputs = [("load", value) for value in operands]
    scratch = [
        pltpu.VMEM((2 * rows, width), BF),
        pltpu.VMEM((span, 2 * rows), BF),
        pltpu.VMEM((3 * span, 2 * rows), BF),
        pltpu.VMEM((8, 128), F32),
        pltpu.VMEM((8, 128), F32),
    ]
    scratch += total_scratch(rows, width) + total_sems(rows) + [pair_sems(1)]
    copies = []
    if extras:
        inputs += [("load", value) for value in extras[:5]] + [("hbm", extras[5])]
        outs = [((rows, half), BF)] * 2
        for chunks in (LAYER_CHUNKS, FEED_CHUNKS, ATTEND_CHUNKS):
            outs.append(((2, len(chunks) * UNIT, half), BF))
        outs.append(((2, 16, half), F32))
        scratch += scatter_scratch(FEED_CHUNKS, width, 1, 5)
        scratch += [pltpu.VMEM((rows, width), BF)] * 3 + [pair_sems(12)]
        scratch += [pltpu.VMEM((16, width), F32)] + [pltpu.VMEM((3, 16, width), F32)] * 2
        scratch += [pltpu.VMEM((2, 16, width), F32), pltpu.VMEM((16, half), F32), pair_sems(8)]
        scratch += scatter_scratch(ATTEND_CHUNKS, width)
        scratch += gather_scratch(LAYER_CHUNKS) + gather_scratch(FEED_CHUNKS) + gather_scratch(ATTEND_CHUNKS)
    else:
        copies = feed_copies(0, 0, parts[1].shape[0], width)
        inputs += [("hbm", value) for value in parts]
        scratch += [pltpu.SemaphoreType.DMA((len(copies),))] + scatter_scratch(FEED_CHUNKS, width)
        outs = [
            ((rows, width), F32),
            ((3 * span, width), BF),
            ((span, width), BF),
            ((16, width), BF),
            ((16 * len(FEED_CHUNKS), half), BF),
        ]
    return call(
        functools.partial(attend_backward_kernel, {"last": bool(extras), "copies": copies}),
        "attend_backward_last" if extras else "attend_backward",
        1 if extras else 6,
        inputs,
        outs,
        scratch,
    )


def finish_kernel(*refs):
    layer_load, feed_load, tail_load, vec_load, token_load, result_load = refs[:6]
    token_ref, result_ref, up_out, down_out, q_out, k_out, v_out, out_out, bias_out = refs[6:15]
    one_gain_out, one_shift_out, query_out, key_out, two_gain_out, two_shift_out, down_bias_out = refs[15:22]
    up_stage, down_stage, square_stage, token_stage, store_sems = refs[22:27]
    units, half = down_out.shape[1] // 2, down_out.shape[2]
    span = q_out.shape[2] // 2
    stores = []

    def store(stage, target):
        copy = pltpu.make_async_copy(stage, target, store_sems.at[len(stores)])
        copy.start()
        stores.append(copy)

    def finish_feed(layer, both, base):
        for spot in range(2):
            for part in range(units // half):
                up_stage[layer, :, pl.ds(spot * units + part * half, half)] = both[
                    spot, pl.ds(base + part * half, half), :
                ].astype(F32)
            down_stage[layer, pl.ds(spot * units, units), :] = both[
                spot, pl.ds(base + units, units), :
            ].astype(F32)
        store(up_stage.at[layer], up_out.at[layer])
        store(down_stage.at[layer], down_out.at[layer])

    def finish_attend(layer, both, base):
        for at, target in enumerate((q_out, k_out, v_out, out_out)):
            here = pl.ds(base + at * span, span)
            value = jnp.concatenate((both[0, here, :], both[1, here, :]), axis=0).astype(F32)
            square_stage[layer, at] = value if at == 3 else value.T
            store(square_stage.at[layer, at], target.at[layer])

    layer_both = layer_load()
    finish_feed(1, layer_both, 0)
    finish_attend(1, layer_both, 2 * units)
    finish_feed(0, feed_load(), 0)
    finish_attend(0, tail_load(), 0)
    token_stage[...] = token_load()[...].astype(F32)
    store(token_stage, token_ref)
    store(result_load(), result_ref)
    small_at = 2 * units + 4 * span
    vec = vec_load()
    for layer in range(2):
        if layer == 1:
            one = [layer_both[spot, pl.ds(small_at, 16), :].astype(F32) for spot in range(2)]
            two = [layer_both[spot, pl.ds(small_at + 16, 16), :].astype(F32) for spot in range(2)]
        else:
            one = [vec[spot, 0:8, :] for spot in range(2)]
            two = [vec[spot, 8:16, :] for spot in range(2)]
        for spot in range(2):
            for part in range(units // half):
                bias_out[layer : layer + 1, pl.ds(spot * units + part * half, half)] = two[spot][
                    3 + part : 4 + part
                ]
        for row, ref in enumerate((one_gain_out, one_shift_out, query_out, key_out)):
            ref[layer : layer + 1, :] = (one[0] + one[1])[row : row + 1, 0 : ref.shape[1]]
        for row, ref in enumerate((two_gain_out, two_shift_out, down_bias_out)):
            ref[layer : layer + 1, :] = (two[0] + two[1])[row : row + 1]
    for copy in stores:
        copy.wait()


def finish(values, units, span):
    rows, half = values[4].shape
    heads = 2 * span
    shapes = [(half, 2 * units), (2 * units, half)] + [(half, heads)] * 3 + [(heads, half)]
    outs = [("hbm", ((rows, half), F32)), ("hbm", ((rows, half), BF))]
    outs += [("hbm", ((2,) + shape, F32)) for shape in shapes]
    outs += [((2, size), F32) for size in (2 * units, half, half, HEAD_DIM, HEAD_DIM, half, half, half)]
    return call(
        finish_kernel,
        "finish",
        None,
        [("load", value) for value in values],
        outs,
        [
            pltpu.VMEM((2,) + shapes[0], F32),
            pltpu.VMEM((2,) + shapes[1], F32),
            pltpu.VMEM((2, 4, heads, half), F32),
            pltpu.VMEM((rows, half), F32),
            pltpu.SemaphoreType.DMA((14,)),
        ],
    )


def shards(
    tokens, ln1_gain, ln1_shift, w_query, w_key, w_value, query_gain, key_gain, w_out,
    ln2_gain, ln2_shift, w_up, up_bias, w_down, down_bias, cotangent,
):
    gains = jnp.stack((query_gain, key_gain), axis=2)
    resid, w_qkv, later, vectors = arrive(
        tokens, w_query, w_key, w_value, (ln1_gain, ln1_shift, ln2_gain, ln2_shift, down_bias)
    )
    caches, raws = [], (w_out, w_up, w_down)
    for at in range(2):
        last = at == 1
        resid_two, seen_one, qkv, mixed, total, *fetched = attend_forward(
            at, resid, w_qkv, gains[at], vectors[at], raws, None if at == 0 else out_here
        )
        if at == 0:
            out_here, up_here, down_here = fetched
        result, seen_two, active, slope, *side = feed_forward(
            at, last, resid_two, up_here, up_bias, down_here, vectors[at], cotangent if last else later, raws
        )
        caches.append(
            (
                (resid_two, seen_two, active, slope, up_here, down_here, vectors[at]),
                (resid, seen_one, qkv, mixed, total, w_qkv, out_here, gains[at], vectors[at]),
            )
        )
        if not last:
            resid = result
            w_qkv, out_here, up_here, down_here = side
    grad, low = side
    grad, small_two, grad_up, grad_down = feed_backward((grad,) + caches[1][0], ())
    grad, grad_qkv, grad_out, small_one, shard = attend_backward(
        (grad,) + caches[1][1], (grad_up, grad_down), ()
    )
    grad, small_zero, other_shard, first = feed_backward(
        (grad,) + caches[0][0], (grad_qkv, grad_out, small_one, small_two)
    )
    out, low_grad, layer_both, feed_both, tail_both, vec = attend_backward(
        (grad,) + caches[0][1], (), (first, shard, other_shard, small_zero, result, low)
    )
    (
        grad_tokens, out, grad_up, grad_down, grad_q, grad_k, grad_v, grad_out, grad_up_bias,
        grad_one_gain, grad_one_shift, grad_query_gain, grad_key_gain,
        grad_two_gain, grad_two_shift, grad_down_bias,
    ) = finish((layer_both, feed_both, tail_both, vec, low_grad, out), w_up.shape[2] // 2, w_query.shape[2] // 2)
    return (
        out, grad_tokens, grad_one_gain, grad_one_shift, grad_q, grad_k, grad_v,
        grad_query_gain, grad_key_gain, grad_out, grad_two_gain, grad_two_shift,
        grad_up, grad_up_bias, grad_down, grad_down_bias,
    )


def solution(mesh):
    fine = Mesh(mesh.devices.reshape(4, 4, 2, 2, 2), ("x", "z", "core", "row", "col"))
    rows = ("x", "z", "core", "row")
    in_specs = (
        P(rows, "col"),
        P(None, "col"),
        P(None, "col"),
        P(None, "col", "row"),
        P(None, "col", "row"),
        P(None, "col", "row"),
        P(),
        P(),
        P(None, "row", "col"),
        P(None, "col"),
        P(None, "col"),
        P(None, "col", "row"),
        P(None, "row"),
        P(None, "row", "col"),
        P(None, "col"),
        P(rows, "col"),
    )
    out_specs = (P(rows, "col"),) * 2 + in_specs[1:15]
    return jax.shard_map(shards, mesh=fine, in_specs=in_specs, out_specs=out_specs, check_vma=False)
```

```python
import functools

import jax
import jax.numpy as jnp
from jax import lax
from jax.experimental import pallas as pl
from jax.experimental.pallas import tpu as pltpu
from jax.sharding import Mesh, PartitionSpec as P

HEAD_DIM = 64
EPS = 1e-06
LOG2E = 1.4426950408889634
BF = jnp.bfloat16
F32 = jnp.float32
GROUP = ("core", "row", "col")
BLOCK = 256


def dot(left, right, left_axis=1, right_axis=0):
    return lax.dot_general(
        left, right, (((left_axis,), (right_axis,)), ((), ())), preferred_element_type=F32
    )


MESH = pl.DeviceIdType.MESH
ROWS = 256
STEP = 128


def norm(resid):
    mean = jnp.mean(resid, axis=1, keepdims=True)
    centred = resid - mean
    factor = lax.rsqrt(jnp.mean(centred * centred, axis=1, keepdims=True) + EPS)
    return centred * factor, factor


def norm_back(grad, normal, factor, gain):
    scaled = grad * gain
    first = jnp.mean(scaled, axis=1, keepdims=True)
    second = jnp.mean(scaled * normal, axis=1, keepdims=True)
    return factor * (scaled - first - normal * second)


def head_norm(values):
    mean = jnp.mean(values, axis=0, keepdims=True)
    centred = values - mean
    factor = lax.rsqrt(jnp.mean(centred * centred, axis=0, keepdims=True) + EPS)
    return centred * factor, factor


def head_norm_back(grad, normal, factor, gain):
    scaled = grad * gain
    first = jnp.mean(scaled, axis=0, keepdims=True)
    second = jnp.mean(scaled * normal, axis=0, keepdims=True)
    return factor * (scaled - first - normal * second)


SCALE2 = LOG2E * HEAD_DIM ** (-0.5)


def gelu_parts(hidden):
    square = hidden * hidden
    bent = jnp.tanh(0.7978845608 * hidden * (1.0 + 0.044715 * square))
    active = 0.5 * hidden * (1.0 + bent)
    slope = 0.5 * (1.0 + bent) + 0.5 * hidden * (1.0 - bent * bent) * (
        0.7978845608 * (1.0 + 3.0 * 0.044715 * square)
    )
    return active, slope


def group_device(core_flip, row_flip, col_flip):
    device = {}
    for name, flipped in zip(GROUP, (core_flip, row_flip, col_flip)):
        if flipped:
            device[name] = 1 - lax.axis_index(name)
    return device


def partners():
    return group_device(1, 0, 0), group_device(0, 1, 1), group_device(1, 1, 1)


def whole_group():
    return [group_device(i & 1, (i >> 1) & 1, i >> 2) for i in range(1, 8)]


def plane_neighbours():
    x, z = lax.axis_index("x"), lax.axis_index("z")
    around = ({"x": (x + 1) % 4}, {"x": (x + 3) % 4}, {"z": (z + 1) % 4}, {"z": (z + 3) % 4})
    return around, (x + 2 * z) % 4


class Quarters:
    def __init__(self, pieces, sems):
        self.sems, self.pieces, self.second = sems, pieces, []
        self.around, self.quarter = plane_neighbours()

    def cut(self, ref):
        size = ref.shape[0] // 4
        return ref.at[pl.ds(pl.multiple_of(self.quarter * size, 16), size), :]

    def fetch(self):
        self.first = [
            send(self.cut(source), self.cut(target), self.sems, 4 * at, device)
            for at, (source, target, device) in enumerate(self.pieces)
        ]

    def share(self, count=None):
        start = len(self.second) // 3
        stop = len(self.pieces) if count is None else min(start + count, len(self.pieces))
        for at in range(start, stop):
            self.first[at].wait_recv()
            here = self.cut(self.pieces[at][1])
            for spot in range(3):
                self.second.append(send(here, here, self.sems, 4 * at + 1 + spot, self.around[spot]))

    def arrive(self):
        for copy in self.second:
            copy.wait_recv()

    def close(self):
        for copy in self.first + self.second:
            copy.wait_send()


def image_spots():
    core, row, col = (lax.axis_index(name) for name in GROUP)
    flip = (col + core) % 2
    own = {"core": row, "row": flip, "col": col}
    other = {"core": row, "row": 1 - flip, "col": 1 - col}
    stays = jnp.logical_and(core == row, col == 0)
    return own, other, stays


def move(source, target, sems, at, device, stays):
    def remote():
        return pltpu.make_async_remote_copy(
            src_ref=source,
            dst_ref=target,
            send_sem=sems.at[0, at],
            recv_sem=sems.at[1, at],
            device_id=device,
            device_id_type=MESH,
        )

    @pl.when(jnp.logical_not(stays))
    def _():
        remote().start()

    @pl.when(stays)
    def _():
        pltpu.make_async_copy(source, target, sems.at[0, at]).start()

    def finish():
        @pl.when(jnp.logical_not(stays))
        def _():
            remote().wait()

        @pl.when(stays)
        def _():
            pltpu.make_async_copy(source, target, sems.at[0, at]).wait()

    return finish


class Home:
    def __init__(self, sems):
        core, row, col = (lax.axis_index(name) for name in GROUP)
        self.sems = sems
        self.sends = core == row
        self.stays = jnp.logical_and(self.sends, col == 0)
        self.leaves = jnp.logical_and(self.sends, col == 1)
        self.beside = {"core": (col + row) % 2, "col": 1 - col}
        self.waits = []

    def move(self, source, target, at):
        half = target.shape[1]

        def near():
            return self.copy(source.at[:, pl.ds(0, half)], target, 2 * at, at, group_device(1, 0, 0))

        def far():
            return self.copy(source.at[:, pl.ds(half, half)], target, 2 * at + 1, at, self.beside)

        def still():
            return pltpu.make_async_copy(source.at[:, pl.ds(0, half)], target, self.sems.at[0, 2 * at])

        pl.when(self.leaves)(lambda: near().start())
        pl.when(self.stays)(lambda: still().start())
        pl.when(self.sends)(lambda: far().start())

        def finish():
            pl.when(self.leaves)(lambda: near().wait_send())
            pl.when(self.stays)(lambda: still().wait())
            pl.when(self.sends)(lambda: far().wait_send())
            pl.when(jnp.logical_not(self.stays))(lambda: near().wait_recv())

        self.waits.append(finish)

    def copy(self, source, target, send_at, recv_at, device):
        return pltpu.make_async_remote_copy(
            src_ref=source,
            dst_ref=target,
            send_sem=self.sems.at[0, send_at],
            recv_sem=self.sems.at[1, recv_at],
            device_id=device,
            device_id_type=MESH,
        )

    def close(self):
        for finish in self.waits:
            finish()


def local(source, target, sems, at):
    copy = pltpu.make_async_copy(source, target, sems.at[0, at])
    copy.start()
    return copy


def greet(devices):
    barrier = pltpu.get_barrier_semaphore()
    for device in devices:
        pl.semaphore_signal(barrier, inc=1, device_id=device, device_id_type=MESH)


def meet(devices):
    pl.semaphore_wait(pltpu.get_barrier_semaphore(), len(devices))


def send(source, target, sems, at, device):
    copy = pltpu.make_async_remote_copy(
        src_ref=source,
        dst_ref=target,
        send_sem=sems.at[0, at],
        recv_sem=sems.at[1, at],
        device_id=device,
        device_id_type=MESH,
    )
    copy.start()
    return copy


class Totals:
    def __init__(self, chip, core_out, core_in, cross_out, cross_in, sems, partner, cross):
        self.refs = (chip, core_out, core_in, cross_out, cross_in)
        self.sems, self.partner, self.cross = sems, partner, cross
        self.copies = []

    def run(self, compute, ready):
        chip, core_out, core_in, cross_out, cross_in = self.refs
        rows = chip.shape[0]
        count = rows // STEP
        core_copies, cross_copies = [], []

        def pass_on(at):
            here = pl.ds(at * STEP, STEP)
            core_copies[at].wait_recv()
            total = chip[here, :] + core_in[here, :].astype(F32)
            chip[here, :] = total
            if cross_out is not None:
                cross_out[here, :] = total.astype(BF)
                cross_copies.append(
                    send(cross_out.at[here, :], cross_in.at[here, :], self.sems, count + at, self.cross)
                )

        for at in range(count):
            here = pl.ds(at * STEP, STEP)
            chip[here, :] = compute(at * STEP)
            if at > 0:
                pass_on(at - 1)
            ready(at * STEP)
            core_out[here, :] = compute(rows + at * STEP).astype(BF)
            core_copies.append(
                send(core_out.at[here, :], core_in.at[here, :], self.sems, at, self.partner)
            )
        pass_on(count - 1)
        self.cross_copies = cross_copies
        self.copies = core_copies + cross_copies

    def chunk(self, row):
        chip, _, _, _, cross_in = self.refs
        here = pl.ds(row, STEP)
        self.cross_copies[row // STEP].wait_recv()
        half = chip.shape[1] // 2
        other = cross_in[here, :].astype(F32)
        return chip[here, :] + jnp.concatenate((other[:, half:], other[:, :half]), axis=1)

    def close(self):
        for copy in self.copies:
            copy.wait_send()


def when_starting(copies):
    return lambda row: copies[row // ROWS].wait_recv() if row % ROWS == 0 else None


def spread(fill, whole, sems, partner):
    rows = whole.shape[0] // 2
    copies = []
    for at in range(rows // ROWS):
        here = pl.ds(at * ROWS, ROWS)
        whole[here, :] = fill(at * ROWS)
        if at == 0:
            yield None
        copies.append(
            send(whole.at[here, :], whole.at[pl.ds(rows + at * ROWS, ROWS), :], sems, at, partner)
        )
    yield copies


def fill_and_send(fill, whole, sems, devices):
    steps = spread(fill, whole, sems, devices[0])
    next(steps)
    meet(devices)
    return next(steps)


def arrive_kernel(
    token_ref, wq_load, wk_load, wv_load, one_gain, one_shift, two_gain, two_shift, bias_load,
    out_ref, w_qkv_ref, later_ref, vector_ref,
    landed, sems, share_sems,
):
    around, _ = plane_neighbours()
    devices = whole_group() + list(around)
    greet(devices)
    core = lax.axis_index("core")
    own, other, stays = image_spots()
    beside = group_device(0, 0, 1)
    half = token_ref.shape[1]
    meet(devices)
    finish = move(token_ref, landed.at[:, pl.ds(0, half)], sems, 0, own, stays)
    copies = [send(token_ref, landed.at[:, pl.ds(half, half)], sems, 1, other)]
    span = w_qkv_ref.shape[0] // 3

    def turned(ref, layer):
        whole = ref[layer].astype(F32).T
        return jnp.where(core == 0, whole[:span], whole[span:]).astype(BF)

    loads = (wq_load, wk_load, wv_load)
    for at, load in enumerate(loads):
        w_qkv_ref[pl.ds(at * span, span), 0:half] = turned(load(), 0)
    shared = Quarters(
        [(w_qkv_ref.at[:, pl.ds(0, half)], w_qkv_ref.at[:, pl.ds(half, half)], beside)], share_sems
    )
    shared.fetch()
    refs = [load() for load in (one_gain, one_shift, two_gain, two_shift, bias_load)]
    for layer in range(vector_ref.shape[0]):
        rows = [ref[layer : layer + 1, :] for ref in refs]
        vector_ref[layer, :, 0:half] = jnp.concatenate(rows + [jnp.zeros((3, half), F32)], axis=0)
    copies.append(
        send(vector_ref.at[:, :, pl.ds(0, half)], vector_ref.at[:, :, pl.ds(half, half)], sems, 2, beside)
    )
    for at, load in enumerate(loads):
        later_ref[pl.ds(at * span, span), :] = turned(load(), 1)
    shared.share()
    finish()
    copies[0].wait()
    out_ref[...] = landed[...].astype(F32)
    copies[1].wait()
    shared.arrive()
    shared.close()


class Weights(Quarters):
    def __init__(self, pieces, kept, keep_sems, share_sems):
        self.kept = [local(source, target, keep_sems, at) for at, (source, target) in enumerate(kept)]
        super().__init__(pieces, share_sems)

    def arrive(self):
        super().arrive()
        for copy in self.kept:
            copy.wait()


def feed_weights(layer, raw_up, raw_down, w_up, w_down, keep_sems, share_sems):
    core, beside = lax.axis_index("core"), group_device(0, 0, 1)
    units, half = w_up.shape[1], w_up.shape[0] // 2
    here = pl.ds(pl.multiple_of(core * units, units), units)
    up, down = raw_up.at[layer, :, here], raw_down.at[layer, here, :]
    return Weights(
        [(up, w_up.at[pl.ds(half, half), :], beside), (down, w_down.at[:, pl.ds(half, half)], beside)],
        [(up, w_up.at[pl.ds(0, half), :]), (down, w_down.at[:, pl.ds(0, half)])],
        keep_sems,
        share_sems,
    )


def out_weights(layer, raw_out, w_out, keep_sems, share_sems):
    core = lax.axis_index("core")
    half, span = w_out.shape[1] // 2, w_out.shape[0] // 4
    beside, cross, across = group_device(0, 0, 1), group_device(0, 1, 1), group_device(0, 1, 0)
    pieces, kept = [], []
    for at in range(2):
        source = raw_out.at[layer, pl.ds((core + at - 2 * at * core) * span, span), :]
        for device, row, col in ((beside, 0, half), (cross, half, half), (across, half, 0)):
            pieces.append((source, w_out.at[pl.ds(row + at * span, span), pl.ds(col, half)], device))
        kept.append((source, w_out.at[pl.ds(at * span, span), pl.ds(0, half)]))
    return Weights(pieces, kept, keep_sems, share_sems)


def attend_forward_kernel(layer, flush, resid_load, w_qkv_load, gain_load, vector_load, raw_out_ref, *refs):
    if layer == 0:
        raw_up_ref, raw_down_ref, *refs = refs
    out_ref, seen_ref, qkv_ref, mixed_ref, total_ref, w_out_ref, *refs = refs
    if layer == 0:
        w_up_ref, w_down_ref, *refs = refs
    joined, seen_sems, head_sems, keep_sems, share_sems, *feed_sems = refs
    near, cross, far = partners()
    devices = (near, cross, far, group_device(0, 0, 1), group_device(0, 1, 0)) + plane_neighbours()[0]
    greet(devices)
    resid_ref, vector_ref = resid_load(), vector_load()
    rows = resid_ref.shape[0]
    heads = mixed_ref.shape[0] // HEAD_DIM
    span = heads * HEAD_DIM

    def fill(row):
        normal, _ = norm(resid_ref[pl.ds(row, ROWS), :])
        return (normal * vector_ref[0:1, :] + vector_ref[1:2, :]).astype(BF)

    copies = fill_and_send(fill, seen_ref, seen_sems, devices)
    fetched = []
    if layer == 0:
        fetched.append(feed_weights(layer, raw_up_ref, raw_down_ref, w_up_ref, w_down_ref, *feed_sems))
    fetched.append(out_weights(layer, raw_out_ref, w_out_ref, keep_sems, share_sems))
    for shared in fetched:
        shared.fetch()
    w_qkv_ref = w_qkv_load()
    for at in range(2 * rows // ROWS):
        if at * ROWS >= rows:
            copies[at - rows // ROWS].wait_recv()
        here = pl.ds(at * ROWS, ROWS)
        qkv_ref[:, here] = dot(w_qkv_ref[...], seen_ref[here, :], 1, 1)
    flush(seen_ref, qkv_ref)
    gains = gain_load()[...]
    for head in range(heads):
        if layer == 0 and head == 1:
            fetched[0].share(1)
        if head == 2:
            for shared in fetched:
                shared.share()
        own = pl.ds(head * HEAD_DIM, HEAD_DIM)
        query = (head_norm(qkv_ref[own, :])[0] * gains[:, 0:1]).astype(BF)
        key = head_norm(qkv_ref[pl.ds(span + head * HEAD_DIM, HEAD_DIM), :])[0] * gains[:, 1:2]
        key_rows = key.T.astype(BF)
        value = qkv_ref[pl.ds(2 * span + head * HEAD_DIM, HEAD_DIM), :].astype(BF)
        for at in range(0, 2 * rows, BLOCK):
            expo = jnp.exp2(dot(key_rows, query[:, at : at + BLOCK]) * SCALE2)
            total = jnp.sum(expo, axis=0, keepdims=True)
            mixed = (dot(value, expo.astype(BF)) * (1.0 / total)).astype(BF)
            mixed_ref[own, at : at + BLOCK] = mixed
            if at < rows:
                joined[own, at : at + BLOCK] = mixed
            total_ref[head : head + 1, at : at + BLOCK] = jnp.log2(total)
        mine, others = pl.ds(0, rows), pl.ds(rows, rows)
        for spot, (device, columns) in enumerate(((near, others), (cross, mine), (far, others))):
            copies.append(
                send(
                    mixed_ref.at[own, columns],
                    joined.at[pl.ds((spot + 1) * span + head * HEAD_DIM, HEAD_DIM), :],
                    head_sems,
                    head * 3 + spot,
                    device,
                )
            )
    flush(mixed_ref, total_ref)
    fetched[-1].arrive()
    flush(w_out_ref)
    for copy in copies[-3 * heads :]:
        copy.wait_recv()
    for at in range(rows // ROWS):
        here = pl.ds(at * ROWS, ROWS)
        out_ref[here, :] = resid_ref[here, :] + dot(joined[:, here], w_out_ref[...], 0, 0)
    if layer == 0:
        fetched[0].arrive()
    for copy in copies:
        copy.wait_send()
    for shared in fetched:
        shared.close()


def feed_forward_kernel(
    layer, last, flush, resid_load, w_up_load, bias_load, w_down_load, vector_load, side_ref, *refs
):
    if last:
        out_ref, seen_ref, active_ref, slope_ref, side_out, low_ref = refs[:6]
        chip, core_out, core_in, landed, seen_sems, total_sems, side_sems = refs[6:]
        cross_out, cross_in = None, None
    else:
        raw_up_ref, raw_down_ref, *refs = refs
        out_ref, seen_ref, active_ref, slope_ref, side_out, next_up_ref, next_down_ref = refs[:7]
        chip, core_out, core_in, cross_out, cross_in = refs[7:12]
        seen_sems, total_sems, side_sems, keep_sems, share_sems = refs[12:]
    near, cross, _ = partners()
    beside = group_device(0, 0, 1)
    devices = whole_group() if last else (near, cross, beside) + plane_neighbours()[0]
    greet(devices)
    core = lax.axis_index("core")
    resid_ref, vector_ref = resid_load(), vector_load()
    half = resid_ref.shape[1] // 2

    def fill(row):
        normal, _ = norm(resid_ref[pl.ds(row, ROWS), :])
        return (normal * vector_ref[2:3, :] + vector_ref[3:4, :]).astype(BF)

    if last:
        steps = spread(fill, seen_ref, seen_sems, near)
        next(steps)
        meet(devices)
        copies = next(steps)
        own, other, stays = image_spots()
        arrived = move(side_ref, landed.at[:, pl.ds(0, half)], side_sems, 0, own, stays)
        side = send(side_ref, landed.at[:, pl.ds(half, half)], side_sems, 1, other)
    else:
        copies = fill_and_send(fill, seen_ref, seen_sems, devices)
        kept = local(side_ref, side_out.at[:, pl.ds(0, half)], side_sems, 0)
        side = send(side_ref, side_out.at[:, pl.ds(half, half)], side_sems, 1, beside)
        shared = feed_weights(
            layer + 1, raw_up_ref, raw_down_ref, next_up_ref, next_down_ref, keep_sems, share_sems
        )
        shared.fetch()

    w_up_ref, w_down_ref, bias_ref = w_up_load(), w_down_load(), bias_load()
    units = w_up_ref.shape[1]
    bias = bias_ref[layer : layer + 1, pl.ds(pl.multiple_of(core * units, units), units)]

    def compute(row):
        here = pl.ds(row, STEP)
        hidden = dot(seen_ref[here, :], w_up_ref[...]) + bias
        active, slope = gelu_parts(hidden)
        active = active.astype(BF)
        active_ref[here, :] = active
        slope_ref[here, :] = slope.astype(BF)
        return dot(active, w_down_ref[...])

    totals = Totals(chip, core_out, core_in, cross_out, cross_in, total_sems, near, cross)
    totals.run(compute, when_starting(copies))
    flush(seen_ref, active_ref, slope_ref)
    if not last:
        shared.share()
    for row in range(0, resid_ref.shape[0], STEP):
        here = pl.ds(row, STEP)
        total = chip[here, :] if last else totals.chunk(row)
        out_ref[here, :] = resid_ref[here, :] + (total + vector_ref[4:5, :])
        if last:
            low_ref[here, :] = total.astype(BF)
    for copy in copies:
        copy.wait_send()
    totals.close()
    side.wait()
    if last:
        arrived()
        side_out[...] = landed[...].astype(F32)
    else:
        kept.wait()
        shared.arrive()
        shared.close()


def feed_backward_kernel(plan, flush, *refs):
    refs = iter(refs)

    def take(count):
        return [next(refs) for _ in range(count)]

    grad_load, resid_load, seen_load, active_load, slope_load, w_up_load, w_down_load, vector_load = take(8)
    parts = take(plan["parts"])
    out_ref, up_ref, down_ref, small_ref = take(4)
    if parts:
        (shard_ref,) = take(1)
    branch, hidden, chip, core_out, core_in, cross_out, cross_in, seen_sems, total_sems = take(9)
    near, cross, _ = partners()
    devices = (near, cross)
    steps = iter(())
    if parts:
        (load_sems,) = take(1)
        beside = take_scatter(ATTEND_SMALL_CHUNKS, refs)
        steps = loaded_scatter(ATTEND_SMALL_CHUNKS, parts, plan["copies"], load_sems, *beside)
        devices += tuple(device for device, _ in link_bits().values())
    greet(devices)
    next(steps, None)
    grad_ref = grad_load()
    width = grad_ref.shape[1]
    copies = fill_and_send(
        lambda row: grad_ref[pl.ds(row, ROWS), :].astype(BF), branch, seen_sems, devices
    )
    next(steps, None)
    w_down_ref, slope_ref, w_up_ref = w_down_load(), slope_load(), w_up_load()

    def compute(row):
        here = pl.ds(row, STEP)
        active_grad = dot(branch[here, :], w_down_ref[...], 1, 1)
        low = (active_grad * slope_ref[here, :].astype(F32)).astype(BF)
        hidden[here, :] = low
        return dot(low, w_up_ref[...], 1, 1)

    totals = Totals(chip, core_out, core_in, cross_out, cross_in, total_sems, near, cross)
    totals.run(compute, when_starting(copies))
    next(steps, None)
    rows = grad_ref.shape[0]
    active_ref, seen_ref, resid_ref, vector_ref = active_load(), seen_load(), resid_load(), vector_load()
    half = width // 2
    for at in range(0, width, ROWS):
        down_ref[at : at + ROWS, :] = dot(active_ref[:, at : at + ROWS], branch[...], 0, 0).astype(BF)
        up_ref[at : at + ROWS, :] = dot(seen_ref[:, at : at + ROWS], hidden[...], 0, 0).astype(BF)
    flush(up_ref, down_ref)
    next(steps, None)
    bias_down = jnp.sum(branch[0:rows, :].astype(F32), axis=0, keepdims=True)
    bias_up = jnp.sum(hidden[...].astype(F32), axis=0, keepdims=True)
    gain_sum = jnp.zeros((1, width), F32)
    shift_sum = jnp.zeros((1, width), F32)
    for row in range(0, rows, STEP):
        here = pl.ds(row, STEP)
        grad = totals.chunk(row)
        normal, factor = norm(resid_ref[here, :])
        gain_sum = gain_sum + jnp.sum(grad * normal, axis=0, keepdims=True)
        shift_sum = shift_sum + jnp.sum(grad, axis=0, keepdims=True)
        out_ref[here, :] = grad_ref[here, :] + norm_back(grad, normal, factor, vector_ref[2:3, :])
        if row in (0, 2 * STEP):
            next(steps, None)
    height = small_ref.shape[0]
    small_ref[...] = jnp.concatenate(
        [gain_sum, shift_sum, bias_down]
        + [jnp.concatenate((bias_up[:, i * half : (i + 1) * half],) * 2, axis=1) for i in range(2)]
        + [jnp.zeros((height - 5, width), F32)],
        axis=0,
    ).astype(small_ref.dtype)
    for _ in steps:
        pass
    if parts:
        keep_shards(beside[1], shard_ref)
    for copy in copies:
        copy.wait_send()
    totals.close()


def attend_backward_kernel(plan, *refs):
    refs = iter(refs)

    def take(count):
        return [next(refs) for _ in range(count)]

    last = plan["last"]
    grad_load, resid_load, seen_load, qkv_load, mixed_load, total_load = take(6)
    w_qkv_load, w_out_load, gain_load, vector_load = take(4)
    parts = take(2)
    if last:
        shard_load, other_shard_load, vec_load, final_load, low_ref = take(5)
        result_ref, token_in, layer_both, feed_both, tail_both, vec_pair = take(6)
    else:
        out_ref, grad_qkv_ref, grad_out_ref, small_ref, shard_ref = take(5)
    proj, mixed_grad, qkv_grad, gains_own, gains_in = take(5)
    chip, core_out, core_in, cross_out, cross_in, seen_sems, total_sems, gain_sems = take(8)
    (load_sems,) = take(1)
    feed_beside = take_scatter(FEED_CHUNKS, refs)
    feed_steps = loaded_scatter(FEED_CHUNKS, parts, plan["copies"], load_sems, *feed_beside)
    links = link_bits()
    near, cross, _ = partners()
    devices = (near, cross) + tuple(device for device, _ in links.values())
    if last:
        low_in, result_low, token_low, home_sems = take(4)
        vec, vec_x, vec_z, vec_mid, vec_col, vec_sems = take(6)
        tail_work, tail_landing, tail_sems = take_scatter(ATTEND_CHUNKS, refs)
        layer_gather = take(2)
        feed_gather = take(2)
        tail_gather = take(2)
        x, z = lax.axis_index("x"), lax.axis_index("z")
        devices = tuple(whole_group()) + tuple(links[name][0] for name in ("x1", "x2", "z1", "z2"))
        devices += ({"x": (x + 2) % 4}, {"z": (z + 2) % 4})
    greet(devices)
    next(feed_steps)
    grad_ref = grad_load()
    rows, width = grad_ref.shape
    half = width // 2
    copies = fill_and_send(
        lambda row: grad_ref[pl.ds(row, ROWS), :].astype(BF), proj, seen_sems, devices
    )
    next(feed_steps)
    if last:
        home = Home(home_sems)

        def low_copy():
            return home.copy(low_ref, low_in, 11, 11, cross)

        pl.when(jnp.logical_not(home.sends))(lambda: low_copy().start())
        shards = [shard_load().at[pl.ds(16 * at, 16), :] for at in range(len(FEED_CHUNKS))]
        shards += [other_shard_load().at[pl.ds(16 * at, 16), :] for at in range(len(ATTEND_SMALL_CHUNKS))]
        layer_steps = gather(LAYER_CHUNKS, shards, layer_both, *layer_gather)
        next(layer_steps)
    w_out_ref = w_out_load()
    span = mixed_grad.shape[0]
    for at in range(2 * rows // ROWS):
        if at * ROWS >= rows:
            copies[at - rows // ROWS].wait_recv()
        here = pl.ds(at * ROWS, ROWS)
        mixed_grad[:, here] = dot(w_out_ref[pl.ds(0, span), :], proj[here, :], 1, 1).astype(BF)
    gains, qkv_ref, total_ref = gain_load()[...], qkv_load(), total_load()
    scale = HEAD_DIM ** (-0.5)
    gains_sum = jnp.zeros((HEAD_DIM, 2), F32)
    slot = 0
    for head in range(span // HEAD_DIM):
        own = pl.ds(head * HEAD_DIM, HEAD_DIM)
        key_at = pl.ds(span + head * HEAD_DIM, HEAD_DIM)
        value_at = pl.ds(2 * span + head * HEAD_DIM, HEAD_DIM)
        query_normal, query_factor = head_norm(qkv_ref[own, :])
        key_normal, key_factor = head_norm(qkv_ref[key_at, :])
        query = (query_normal * gains[:, 0:1]).astype(BF)
        key_full = key_normal * gains[:, 1:2]
        key = key_full.astype(BF)
        key_rows = key_full.T.astype(BF)
        value_rows = qkv_ref[value_at, :].T.astype(BF)
        key_sum = jnp.zeros(key.shape, F32)
        value_sum = jnp.zeros(key.shape, F32)
        query_parts = []
        for at in range(0, 2 * rows, BLOCK):
            grad = mixed_grad[own, at : at + BLOCK]
            logits = dot(key_rows, query[:, at : at + BLOCK]) * SCALE2
            probs = jnp.exp2(logits - total_ref[head : head + 1, at : at + BLOCK])
            pulled = dot(value_rows, grad)
            delta = jnp.sum(probs * pulled, axis=0, keepdims=True)
            score_grad = (probs * (pulled - delta)).astype(BF)
            query_parts.append(dot(key, score_grad))
            key_sum = key_sum + dot(query[:, at : at + BLOCK], score_grad, 1, 1)
            value_sum = value_sum + dot(grad, probs.astype(BF), 1, 1)
            slot += 1
            if last and slot in (3, 6, 10):
                next(layer_steps, None)
            if slot == (11 if last else 9):
                next(feed_steps)
        query_sum = jnp.concatenate(query_parts, axis=1) * scale
        key_sum = key_sum * scale
        qkv_grad[own, :] = head_norm_back(query_sum, query_normal, query_factor, gains[:, 0:1]).astype(BF)
        qkv_grad[key_at, :] = head_norm_back(key_sum, key_normal, key_factor, gains[:, 1:2]).astype(BF)
        qkv_grad[value_at, :] = value_sum.astype(BF)
        gains_sum = gains_sum + jnp.concatenate(
            (
                jnp.sum(query_sum * query_normal, axis=1, keepdims=True),
                jnp.sum(key_sum * key_normal, axis=1, keepdims=True),
            ),
            axis=1,
        )
    square = jnp.concatenate((gains_sum, jnp.zeros((HEAD_DIM, 126), F32)), axis=1)
    gains_own[...] = jnp.concatenate((square, jnp.zeros((128 - HEAD_DIM, 128), F32)), axis=0).T[0:8]
    gains_copy = send(gains_own, gains_in, gain_sems, 0, cross)
    w_qkv_ref = w_qkv_load()

    def compute(row):
        return dot(qkv_grad[:, pl.ds(row, STEP)], w_qkv_ref[...], 0, 0)

    totals = Totals(chip, core_out, core_in, cross_out, cross_in, total_sems, near, cross)
    seen_ref, mixed_ref, resid_ref, vector_ref = seen_load(), mixed_load(), resid_load(), vector_load()
    if last:
        grad_qkv_ref, grad_out_ref = tail_work.at[pl.ds(0, 3 * span), :], tail_work.at[pl.ds(3 * span, span), :]

    def weight_grads():
        for at in range(0, 3 * span, span):
            here = pl.ds(at, span)
            grad_qkv_ref[here, :] = dot(qkv_grad[here, :], seen_ref[...]).astype(BF)
        grad_out_ref[...] = dot(mixed_ref[...], proj[...]).astype(BF)

    sums = [jnp.zeros((1, width), F32), jnp.zeros((1, width), F32)]

    def final_chunk(row):
        here = pl.ds(row, STEP)
        grad = totals.chunk(row)
        normal, factor = norm(resid_ref[here, :])
        sums[0] = sums[0] + jnp.sum(grad * normal, axis=0, keepdims=True)
        sums[1] = sums[1] + jnp.sum(grad, axis=0, keepdims=True)
        return grad_ref[here, :] + norm_back(grad, normal, factor, vector_ref[0:1, :])

    def small_rows(height):
        gains_copy.wait()
        shared = gains_own[0:2, :] + gains_in[0:2, :]
        blank = jnp.zeros((2, half - 128), F32)
        return jnp.concatenate(
            sums
            + [jnp.concatenate((shared, blank, shared, blank), axis=1), jnp.zeros((height - 4, width), F32)],
            axis=0,
        )

    if not last:
        totals.run(compute, lambda row: next(feed_steps) if row == 3 * STEP else None)
        weight_grads()
        next(feed_steps)
        for row in range(0, rows, STEP):
            out_ref[pl.ds(row, STEP), :] = final_chunk(row)
            if row == STEP:
                next(feed_steps)
        small_ref[...] = small_rows(16).astype(BF)
        for _ in feed_steps:
            pass
        keep_shards(feed_beside[1], shard_ref)
        for copy in copies:
            copy.wait_send()
        totals.close()
        return

    def whole(first, second):
        yield from first
        yield from second

    weight_grads()
    tail = whole(
        scatter(ATTEND_CHUNKS, tail_work, tail_landing, tail_sems),
        gather(ATTEND_CHUNKS, tail_landing[4::5], tail_both, *tail_gather),
    )
    next(tail)
    feed = whole(feed_steps, gather(FEED_CHUNKS, feed_beside[1][4::5], feed_both, *feed_gather))
    totals.run(compute, lambda row: None)
    next(feed)
    next(layer_steps)
    final_ref = final_load()

    @pl.when(home.sends)
    def _():
        low_copy().wait_recv()
        other = low_in[...].astype(F32)
        other = jnp.concatenate((other[:, half:], other[:, :half]), axis=1)
        result_low[...] = (final_ref[...] + other).astype(BF)

    pl.when(jnp.logical_not(home.sends))(lambda: low_copy().wait_send())
    home.move(result_low, result_ref, 0)

    def token_chunk(row):
        here = pl.ds(row, STEP)
        token_low[here, :] = final_chunk(row).astype(BF)
        home.move(token_low.at[here, :], token_in.at[here, :], 1 + row // STEP)

    next(tail)
    token_chunk(0)
    next(feed)
    for _ in layer_steps:
        pass
    token_chunk(STEP)
    next(tail)
    next(feed)
    next(tail)
    token_chunk(2 * STEP)
    next(feed)
    next(tail)
    next(feed)
    token_chunk(3 * STEP)
    vec[...] = jnp.concatenate((small_rows(8), vec_load()[...]), axis=0)
    vec_copies = []

    def share(source, landing, axis, place, at):
        batch = []
        for step in range(1, 4):
            batch.append(
                send(source, landing.at[step - 1], vec_sems, at + step - 1, {axis: (place + step) % 4})
            )
        vec_copies.extend(batch)
        return batch

    def collect(source, landing, batch):
        for copy in batch:
            copy.wait_recv()
        return (source[...] + landing[0]) + (landing[1] + landing[2])

    batch = share(vec, vec_x, "x", x, 0)
    next(tail)
    next(feed)
    vec_mid[0] = collect(vec, vec_x, batch)
    batch = share(vec_mid.at[0], vec_z, "z", z, 3)
    next(tail)
    next(feed)
    vec_mid[1] = collect(vec_mid.at[0], vec_z, batch)
    vec_copies.append(send(vec_mid.at[1, :, pl.ds(half, half)], vec_col, vec_sems, 6, links["col"][0]))
    next(tail)
    vec_copies[-1].wait_recv()
    core = lax.axis_index("core")
    vec_pair[core] = vec_mid[1, :, 0:half] + vec_col[...]
    vec_copies.append(send(vec_pair.at[core], vec_pair.at[core], vec_sems, 7, near))
    next(tail)
    vec_copies[-1].wait_recv()
    for _ in feed:
        pass
    for _ in tail:
        pass
    home.close()
    for copy in copies + vec_copies:
        copy.wait_send()
    totals.close()


class Load:
    def __init__(self, source, target, sem):
        self.copy = pltpu.make_async_copy(source, target, sem)
        self.copy.start()
        self.target, self.waited = target, False

    def __call__(self):
        if not self.waited:
            self.copy.wait()
            self.waited = True
        return self.target


def call(kernel, name, collective_id, inputs, outs, scratch):
    vmem = pl.BlockSpec(memory_space=pltpu.VMEM)
    hbm = pl.BlockSpec(memory_space=pl.ANY)

    def kind(spec):
        return spec[0] if isinstance(spec, tuple) and isinstance(spec[0], str) else "block"

    def bare(spec):
        return spec if kind(spec) == "block" else spec[1]

    kinds = [kind(spec) for spec in inputs]
    values = [bare(spec) for spec in inputs]
    loaded = [at for at, k in enumerate(kinds) if k == "load"]
    early = [at for at, spec in enumerate(outs) if kind(spec) == "early"]

    def body(*refs):
        refs = list(refs)
        given, refs = refs[: len(inputs)], refs[len(inputs) :]
        made, refs = refs[: len(outs)], refs[len(outs) :]
        own, refs = refs[: len(scratch)], refs[len(scratch) :]
        staged, refs = refs[: len(loaded)], refs[len(loaded) :]
        kept, (sems, out_sems) = refs[: len(early)], refs[len(early) :]
        loads = [Load(given[at], staged[i], sems.at[i]) for i, at in enumerate(loaded)]
        for at, load in zip(loaded, loads):
            given[at] = load
        copies = {}

        def flush(*flushed):
            for ref in flushed:
                i = next(i for i, one in enumerate(kept) if one is ref)
                copies[i] = pltpu.make_async_copy(ref, made[early[i]], out_sems.at[i])
                copies[i].start()

        results = list(made)
        for i, at in enumerate(early):
            results[at] = kept[i]
        if early:
            kernel(flush, *given, *results, *own)
        else:
            kernel(*given, *results, *own)
        flush(*(ref for i, ref in enumerate(kept) if i not in copies))
        for i in sorted(copies):
            copies[i].wait()
        for load in loads:
            load()

    return pl.pallas_call(
        body,
        in_specs=[vmem if k == "block" else hbm for k in kinds],
        out_specs=[vmem if kind(spec) == "block" else hbm for spec in outs],
        out_shape=[jax.ShapeDtypeStruct(*bare(spec)) for spec in outs],
        scratch_shapes=scratch
        + [pltpu.VMEM(values[at].shape, values[at].dtype) for at in loaded]
        + [pltpu.VMEM(*bare(outs[at])) for at in early]
        + [pltpu.SemaphoreType.DMA((max(1, len(loaded)),)), pltpu.SemaphoreType.DMA((max(1, len(early)),))],
        compiler_params=pltpu.CompilerParams(
            collective_id=collective_id,
            has_side_effects=collective_id is not None,
            vmem_limit_bytes=58 * 2**20,
        ),
        name=name,
    )(*values)


def pair_sems(count):
    return pltpu.SemaphoreType.DMA((2, count))


def total_scratch(rows, width):
    return [pltpu.VMEM((rows, width), F32)] + [pltpu.VMEM((rows, width), BF)] * 4


def total_sems(rows):
    return [pair_sems(rows // ROWS), pair_sems(2 * rows // STEP)]


def arrive(tokens, w_query, w_key, w_value, vectors):
    rows, half = tokens.shape
    span = w_query.shape[2] // 2
    layers = w_query.shape[0]
    return call(
        arrive_kernel,
        "arrive",
        10,
        [("hbm", tokens)] + [("load", value) for value in (w_query, w_key, w_value) + vectors],
        [
            ((rows, 2 * half), F32),
            ((3 * span, 2 * half), BF),
            ((3 * span, half), BF),
            ((layers, 8, 2 * half), F32),
        ],
        [pltpu.VMEM((rows, 2 * half), BF), pair_sems(3), pair_sems(4)],
    )


def attend_forward(layer, resid, w_qkv, gains, vectors, raws):
    rows, width = resid.shape
    span = w_qkv.shape[0] // 3
    units = raws[1].shape[2] // 2
    outs = [
        ((rows, width), F32),
        ((2 * rows, width), BF),
        ((3 * span, 2 * rows), F32),
        ((span, 2 * rows), BF),
        ((span // HEAD_DIM, 2 * rows), F32),
        ((width, width), BF),
    ]
    scratch = [pltpu.VMEM((4 * span, rows), BF), pair_sems(rows // ROWS), pair_sems(3 * span // HEAD_DIM)]
    scratch += [pair_sems(2), pair_sems(24)]
    if layer == 0:
        outs += [((width, units), BF), ((units, width), BF)]
        scratch += [pair_sems(2), pair_sems(8)]
    return call(
        functools.partial(attend_forward_kernel, layer),
        "attend_forward_%d" % layer,
        8 + layer,
        [("load", value) for value in (resid, w_qkv, gains, vectors)]
        + [("hbm", value) for value in (raws if layer == 0 else raws[:1])],
        [("early", out) for out in outs],
        scratch,
    )


def feed_forward(layer, last, resid, w_up, up_bias, w_down, vectors, side, raws):
    rows, width = resid.shape
    units = w_up.shape[1]
    outs = [((rows, width), F32), ((2 * rows, width), BF)] + [((2 * rows, units), BF)] * 2
    low = pltpu.VMEM((rows, width), BF)
    if last:
        outs += [((rows, width), F32), ((rows, width), BF)]
        scratch = [pltpu.VMEM((rows, width), F32), low, low, low]
    else:
        outs += [((side.shape[0], width), BF), ((width, units), BF), ((units, width), BF)]
        scratch = total_scratch(rows, width)
    scratch += total_sems(rows) + [pair_sems(2)]
    return call(
        functools.partial(feed_forward_kernel, layer, last),
        "feed_forward_%d" % layer,
        4 if last else 3,
        [("load", value) for value in (resid, w_up, up_bias, w_down, vectors)]
        + [("hbm", value) for value in (side,) + (() if last else raws[1:])],
        [("early", out) for out in outs],
        scratch if last else scratch + [pair_sems(2), pair_sems(8)],
    )


def feed_backward(operands, parts):
    grad, resid, seen, active, slope, w_up, w_down, vectors = operands
    rows, width = grad.shape
    units = w_up.shape[1]
    outs = [((rows, width), F32), ((width, units), BF), ((units, width), BF)]
    outs += [((8, width), F32) if parts else ((16, width), BF)]
    scratch = [pltpu.VMEM((2 * rows, width), BF), pltpu.VMEM((2 * rows, units), BF)]
    scratch += total_scratch(rows, width) + total_sems(rows)
    copies = []
    if parts:
        outs.append(((16 * len(ATTEND_SMALL_CHUNKS), width // 2), BF))
        scratch += [pltpu.SemaphoreType.DMA((len(parts),))] + scatter_scratch(ATTEND_SMALL_CHUNKS, width)
        row = 0
        for at, part in enumerate(parts):
            copies.append((at, (0, part.shape[0]), (0, width), row, 0))
            row += part.shape[0]
    return call(
        functools.partial(feed_backward_kernel, {"parts": len(parts), "copies": copies}),
        "feed_backward_and_sum" if parts else "feed_backward",
        7 if parts else 5,
        [("load", value) for value in operands] + [("hbm", value) for value in parts],
        [("early", out) for out in outs],
        scratch,
    )


def link_bits():
    x, z = lax.axis_index("x"), lax.axis_index("z")
    col = lax.axis_index("col")
    return {
        "x1": ({"x": x + 1 - 2 * (x % 2)}, ((x + 1) // 2) % 2),
        "x2": ({"x": 3 - x}, x // 2),
        "z1": ({"z": z + 1 - 2 * (z % 2)}, ((z + 1) // 2) % 2),
        "z2": ({"z": 3 - z}, z // 2),
        "col": ({"col": 1 - col}, None),
    }


ORDERS = (
    ("x1", "z1", "x2", "z2", "col"),
    ("z1", "x2", "z2", "col", "x1"),
    ("x2", "z2", "col", "x1", "z1"),
    ("z2", "col", "x1", "z1", "x2"),
    ("col", "x1", "z1", "x2", "z2"),
    ("x1", "z1", "x2", "z2", "col"),
    ("z1", "x2", "z2", "col", "x1"),
    ("x2", "z2", "col", "x1", "z1"),
    ("z2", "col", "x1", "z1", "x2"),
    ("col", "x2", "z2", "x1", "z1"),
)
UNIT = 256


def plan_chunks(rows, orders):
    return [(at * UNIT, UNIT, ORDERS[orders[at]]) for at in range(rows // UNIT)]


def step_shapes(rows, order, width):
    shapes = []
    for link in order:
        if link == "col":
            width //= 2
        else:
            rows //= 2
        shapes.append((rows, width))
    return shapes


def add_into(target, other, row, col_size):
    rows = target.shape[0]
    block = min(rows, 64)

    @pl.loop(0, rows // block)
    def _(at):
        here = pl.ds(pl.multiple_of(at * block, block), block)
        there = pl.ds(pl.multiple_of(row + at * block, 16), block)
        target[here, :] = (
            target[here, :].astype(F32) + other[there, :col_size].astype(F32)
        ).astype(BF)


def scatter(chunks, work, landing, sems):
    links = link_bits()
    state = [work.at[pl.ds(start, rows), :] for start, rows, _ in chunks]
    flight = [None] * len(chunks)
    sent = []

    def land(at, step):
        copy, keep_row, width = flight[at]
        copy.wait_recv()
        target = landing[at * 5 + step]
        add_into(target, state[at], keep_row, width)
        state[at] = target

    for step in range(5):
        for at, (start, rows, order) in enumerate(chunks):
            if step > 0:
                land(at, step - 1)
            device, bit = links[order[step]]
            landed = landing[at * 5 + step]
            size, width = landed.shape
            if bit is None:
                source = state[at].at[:, pl.ds(width, width)]
                keep_row = 0
            else:
                keep_row = bit * size
                source = state[at].at[pl.ds(pl.multiple_of((1 - bit) * size, size), size), :]
            copy = send(source, landed, sems, at * 5 + step, device)
            sent.append(copy)
            flight[at] = (copy, keep_row, width)
        yield
    for at in range(len(chunks)):
        land(at, 4)
    for copy in sent:
        copy.wait_send()


def gather(chunks, shards, both, sems, core_sems):
    core = lax.axis_index("core")
    links = link_bits()
    sent, region = [], []
    for at, (start, rows, order) in enumerate(chunks):
        offset, size = 0, rows
        for link in order:
            if links[link][1] is not None:
                size //= 2
                offset = offset + links[link][1] * size
        both[core, pl.ds(pl.multiple_of(start + offset, 16), size), :] = shards[at][...]
        region.append((start + offset, size))
    back = [[link for link in reversed(order) if link != "col"] for _, _, order in chunks]
    waiting = [None] * len(chunks)

    def settle(at):
        copy, bit, size = waiting[at]
        copy.wait_recv()
        lo, _ = region[at]
        region[at] = (lo - bit * size, 2 * size)

    for step in range(4):
        for at in range(len(chunks)):
            if step > 0:
                settle(at)
            lo, size = region[at]
            device, bit = links[back[at][step]]
            here = both.at[core, pl.ds(pl.multiple_of(lo, 16), size), :]
            copy = send(here, here, sems, at * 4 + step, device)
            sent.append(copy)
            waiting[at] = (copy, bit, size)
        yield
    last = []
    for at, (start, rows, order) in enumerate(chunks):
        settle(at)
        here = both.at[core, pl.ds(start, rows), :]
        last.append(send(here, here, core_sems, at, {"core": 1 - core}))
    yield
    for copy in last:
        copy.wait_recv()
    for copy in sent + last:
        copy.wait_send()


def scatter_scratch(chunks, width):
    shapes = [(sum(size for _, size, _ in chunks), width)]
    shapes += [shape for _, size, order in chunks for shape in step_shapes(size, order, width)]
    return [pltpu.VMEM(shape, BF) for shape in shapes] + [pair_sems(5 * len(chunks))]


def take_scatter(chunks, refs):
    return next(refs), [next(refs) for _ in range(5 * len(chunks))], next(refs)


def gather_scratch(chunks):
    return [pair_sems(4 * len(chunks)), pair_sems(len(chunks))]


def loaded_scatter(chunks, parts, copies, load_sems, work, landing, sems):
    loads = []
    for at, (source, rows, cols, row, col) in enumerate(copies):
        load = pltpu.make_async_copy(
            parts[source].at[pl.ds(rows[0], rows[1]), pl.ds(cols[0], cols[1])],
            work.at[pl.ds(row, rows[1]), pl.ds(col, cols[1])],
            load_sems.at[at],
        )
        load.start()
        loads.append(load)
    yield
    for load in loads:
        load.wait()
    yield from scatter(chunks, work, landing, sems)


def keep_shards(landing, shard_ref):
    for at, landed in enumerate(landing[4::5]):
        shard_ref[pl.ds(at * 16, 16), :] = landed[...]


FEED_CHUNKS = plan_chunks(6 * UNIT, (0, 1, 2, 3, 4, 9))
ATTEND_CHUNKS = plan_chunks(3 * UNIT, (0, 1, 2))
ATTEND_SMALL_CHUNKS = plan_chunks(4 * UNIT, (0, 1, 2, 3))
LAYER_CHUNKS = FEED_CHUNKS + [(start + 6 * UNIT, rows, order) for start, rows, order in ATTEND_SMALL_CHUNKS]


def feed_copies(first, base, units, width):
    half = width // 2
    copies = []
    for i in range(2):
        for j in range(2):
            copies.append((first, (i * half, half), (j * half, half), base + j * half, i * half))
    copies.append((first + 1, (0, units), (0, width), base + units, 0))
    return copies


def attend_backward(operands, parts, extras):
    grad, resid, seen, qkv, mixed, total, w_qkv, w_out, gains, vectors = operands
    rows, width = grad.shape
    half = width // 2
    span = mixed.shape[0]
    inputs = [("load", value) for value in operands]
    scratch = [
        pltpu.VMEM((2 * rows, width), BF),
        pltpu.VMEM((span, 2 * rows), BF),
        pltpu.VMEM((3 * span, 2 * rows), BF),
        pltpu.VMEM((8, 128), F32),
        pltpu.VMEM((8, 128), F32),
    ]
    scratch += total_scratch(rows, width) + total_sems(rows) + [pair_sems(1)]
    copies = feed_copies(0, 0, parts[1].shape[0], width)
    inputs += [("hbm", value) for value in parts]
    scratch += [pltpu.SemaphoreType.DMA((len(copies),))] + scatter_scratch(FEED_CHUNKS, width)
    if extras:
        inputs += [("load", value) for value in extras[:4]] + [("hbm", extras[4])]
        outs = [((rows, half), BF)] * 2
        for chunks in (LAYER_CHUNKS, FEED_CHUNKS, ATTEND_CHUNKS):
            outs.append(((2, len(chunks) * UNIT, half), BF))
        outs.append(((2, 16, half), F32))
        scratch += [pltpu.VMEM((rows, width), BF)] * 3 + [pair_sems(12)]
        scratch += [pltpu.VMEM((16, width), F32)] + [pltpu.VMEM((3, 16, width), F32)] * 2
        scratch += [pltpu.VMEM((2, 16, width), F32), pltpu.VMEM((16, half), F32), pair_sems(8)]
        scratch += scatter_scratch(ATTEND_CHUNKS, width)
        scratch += gather_scratch(LAYER_CHUNKS) + gather_scratch(FEED_CHUNKS) + gather_scratch(ATTEND_CHUNKS)
    else:
        outs = [
            ((rows, width), F32),
            ((3 * span, width), BF),
            ((span, width), BF),
            ((16, width), BF),
            ((16 * len(FEED_CHUNKS), half), BF),
        ]
    return call(
        functools.partial(attend_backward_kernel, {"last": bool(extras), "copies": copies}),
        "attend_backward_last" if extras else "attend_backward",
        1 if extras else 6,
        inputs,
        outs,
        scratch,
    )


def finish_kernel(*refs):
    layer_load, feed_load, tail_load, vec_load, token_load, result_load = refs[:6]
    token_ref, result_ref, up_out, down_out, q_out, k_out, v_out, out_out, bias_out = refs[6:15]
    one_gain_out, one_shift_out, query_out, key_out, two_gain_out, two_shift_out, down_bias_out = refs[15:22]
    up_stage, down_stage, square_stage, token_stage, store_sems = refs[22:27]
    units, half = down_out.shape[1] // 2, down_out.shape[2]
    span = q_out.shape[2] // 2
    stores = []

    def store(stage, target):
        copy = pltpu.make_async_copy(stage, target, store_sems.at[len(stores)])
        copy.start()
        stores.append(copy)

    def finish_feed(layer, both, base):
        for spot in range(2):
            for part in range(units // half):
                up_stage[layer, :, pl.ds(spot * units + part * half, half)] = both[
                    spot, pl.ds(base + part * half, half), :
                ].astype(F32)
            down_stage[layer, pl.ds(spot * units, units), :] = both[
                spot, pl.ds(base + units, units), :
            ].astype(F32)
        store(up_stage.at[layer], up_out.at[layer])
        store(down_stage.at[layer], down_out.at[layer])

    def finish_attend(layer, both, base):
        for at, target in enumerate((q_out, k_out, v_out, out_out)):
            here = pl.ds(base + at * span, span)
            value = jnp.concatenate((both[0, here, :], both[1, here, :]), axis=0).astype(F32)
            square_stage[layer, at] = value if at == 3 else value.T
            store(square_stage.at[layer, at], target.at[layer])

    layer_both = layer_load()
    finish_feed(1, layer_both, 0)
    finish_attend(1, layer_both, 2 * units)
    finish_feed(0, feed_load(), 0)
    finish_attend(0, tail_load(), 0)
    token_stage[...] = token_load()[...].astype(F32)
    store(token_stage, token_ref)
    store(result_load(), result_ref)
    small_at = 2 * units + 4 * span
    vec = vec_load()
    for layer in range(2):
        if layer == 1:
            one = [layer_both[spot, pl.ds(small_at, 16), :].astype(F32) for spot in range(2)]
            two = [layer_both[spot, pl.ds(small_at + 16, 16), :].astype(F32) for spot in range(2)]
        else:
            one = [vec[spot, 0:8, :] for spot in range(2)]
            two = [vec[spot, 8:16, :] for spot in range(2)]
        for spot in range(2):
            for part in range(units // half):
                bias_out[layer : layer + 1, pl.ds(spot * units + part * half, half)] = two[spot][
                    3 + part : 4 + part
                ]
        for row, ref in enumerate((one_gain_out, one_shift_out, query_out, key_out)):
            ref[layer : layer + 1, :] = (one[0] + one[1])[row : row + 1, 0 : ref.shape[1]]
        for row, ref in enumerate((two_gain_out, two_shift_out, down_bias_out)):
            ref[layer : layer + 1, :] = (two[0] + two[1])[row : row + 1]
    for copy in stores:
        copy.wait()


def finish(values, units, span):
    rows, half = values[4].shape
    heads = 2 * span
    shapes = [(half, 2 * units), (2 * units, half)] + [(half, heads)] * 3 + [(heads, half)]
    outs = [("hbm", ((rows, half), F32)), ("hbm", ((rows, half), BF))]
    outs += [("hbm", ((2,) + shape, F32)) for shape in shapes]
    outs += [((2, size), F32) for size in (2 * units, half, half, HEAD_DIM, HEAD_DIM, half, half, half)]
    return call(
        finish_kernel,
        "finish",
        None,
        [("load", value) for value in values],
        outs,
        [
            pltpu.VMEM((2,) + shapes[0], F32),
            pltpu.VMEM((2,) + shapes[1], F32),
            pltpu.VMEM((2, 4, heads, half), F32),
            pltpu.VMEM((rows, half), F32),
            pltpu.SemaphoreType.DMA((14,)),
        ],
    )


def shards(
    tokens, ln1_gain, ln1_shift, w_query, w_key, w_value, query_gain, key_gain, w_out,
    ln2_gain, ln2_shift, w_up, up_bias, w_down, down_bias, cotangent,
):
    gains = jnp.stack((query_gain, key_gain), axis=2)
    resid, w_qkv, later, vectors = arrive(
        tokens, w_query, w_key, w_value, (ln1_gain, ln1_shift, ln2_gain, ln2_shift, down_bias)
    )
    caches, raws = [], (w_out, w_up, w_down)
    for at in range(2):
        last = at == 1
        resid_two, seen_one, qkv, mixed, total, *fetched = attend_forward(
            at, resid, w_qkv, gains[at], vectors[at], raws
        )
        out_here = fetched[0]
        if at == 0:
            up_here, down_here = fetched[1:]
        result, seen_two, active, slope, *side = feed_forward(
            at, last, resid_two, up_here, up_bias, down_here, vectors[at], cotangent if last else later, raws
        )
        caches.append(
            (
                (resid_two, seen_two, active, slope, up_here, down_here, vectors[at]),
                (resid, seen_one, qkv, mixed, total, w_qkv, out_here, gains[at], vectors[at]),
            )
        )
        if not last:
            resid = result
            w_qkv, up_here, down_here = side
    grad, low = side
    grad, grad_up, grad_down, small_two = feed_backward((grad,) + caches[1][0], ())
    grad, grad_qkv, grad_out, small_one, shard = attend_backward(
        (grad,) + caches[1][1], (grad_up, grad_down), ()
    )
    grad, grad_up, grad_down, small_zero, other_shard = feed_backward(
        (grad,) + caches[0][0], (grad_qkv, grad_out, small_one, small_two)
    )
    out, low_grad, layer_both, feed_both, tail_both, vec = attend_backward(
        (grad,) + caches[0][1], (grad_up, grad_down), (shard, other_shard, small_zero, result, low)
    )
    (
        grad_tokens, out, grad_up, grad_down, grad_q, grad_k, grad_v, grad_out, grad_up_bias,
        grad_one_gain, grad_one_shift, grad_query_gain, grad_key_gain,
        grad_two_gain, grad_two_shift, grad_down_bias,
    ) = finish((layer_both, feed_both, tail_both, vec, low_grad, out), w_up.shape[2] // 2, w_query.shape[2] // 2)
    return (
        out, grad_tokens, grad_one_gain, grad_one_shift, grad_q, grad_k, grad_v,
        grad_query_gain, grad_key_gain, grad_out, grad_two_gain, grad_two_shift,
        grad_up, grad_up_bias, grad_down, grad_down_bias,
    )


def solution(mesh):
    fine = Mesh(mesh.devices.reshape(4, 4, 2, 2, 2), ("x", "z", "core", "row", "col"))
    rows = ("x", "z", "core", "row")
    in_specs = (
        P(rows, "col"),
        P(None, "col"),
        P(None, "col"),
        P(None, "col", "row"),
        P(None, "col", "row"),
        P(None, "col", "row"),
        P(),
        P(),
        P(None, "row", "col"),
        P(None, "col"),
        P(None, "col"),
        P(None, "col", "row"),
        P(None, "row"),
        P(None, "row", "col"),
        P(None, "col"),
        P(rows, "col"),
    )
    out_specs = (P(rows, "col"),) * 2 + in_specs[1:15]
    return jax.shard_map(shards, mesh=fine, in_specs=in_specs, out_specs=out_specs, check_vma=False)
```

```python
import functools

import jax
import jax.numpy as jnp
from jax import lax
from jax.experimental import pallas as pl
from jax.experimental.pallas import tpu as pltpu
from jax.sharding import Mesh, PartitionSpec as P

HEAD_DIM = 64
EPS = 1e-06
LOG2E = 1.4426950408889634
BF = jnp.bfloat16
F32 = jnp.float32
GROUP = ("core", "row", "col")
BLOCK = 256


def dot(left, right, left_axis=1, right_axis=0):
    return lax.dot_general(
        left, right, (((left_axis,), (right_axis,)), ((), ())), preferred_element_type=F32
    )


MESH = pl.DeviceIdType.MESH
ROWS = 256
STEP = 128


def norm(resid):
    mean = jnp.mean(resid, axis=1, keepdims=True)
    centred = resid - mean
    factor = lax.rsqrt(jnp.mean(centred * centred, axis=1, keepdims=True) + EPS)
    return centred * factor, factor


def norm_back(grad, normal, factor, gain):
    scaled = grad * gain
    first = jnp.mean(scaled, axis=1, keepdims=True)
    second = jnp.mean(scaled * normal, axis=1, keepdims=True)
    return factor * (scaled - first - normal * second)


def head_norm(values):
    mean = jnp.mean(values, axis=0, keepdims=True)
    centred = values - mean
    factor = lax.rsqrt(jnp.mean(centred * centred, axis=0, keepdims=True) + EPS)
    return centred * factor, factor


def head_norm_back(grad, normal, factor, gain):
    scaled = grad * gain
    first = jnp.mean(scaled, axis=0, keepdims=True)
    second = jnp.mean(scaled * normal, axis=0, keepdims=True)
    return factor * (scaled - first - normal * second)


SCALE2 = LOG2E * HEAD_DIM ** (-0.5)


def gelu_parts(hidden):
    square = hidden * hidden
    bent = jnp.tanh(0.7978845608 * hidden * (1.0 + 0.044715 * square))
    active = 0.5 * hidden * (1.0 + bent)
    slope = 0.5 * (1.0 + bent) + 0.5 * hidden * (1.0 - bent * bent) * (
        0.7978845608 * (1.0 + 3.0 * 0.044715 * square)
    )
    return active, slope


def group_device(core_flip, row_flip, col_flip):
    device = {}
    for name, flipped in zip(GROUP, (core_flip, row_flip, col_flip)):
        if flipped:
            device[name] = 1 - lax.axis_index(name)
    return device


def partners():
    return group_device(1, 0, 0), group_device(0, 1, 1), group_device(1, 1, 1)


def whole_group():
    return [group_device(i & 1, (i >> 1) & 1, i >> 2) for i in range(1, 8)]


def plane_neighbours():
    x, z = lax.axis_index("x"), lax.axis_index("z")
    around = ({"x": (x + 1) % 4}, {"x": (x + 3) % 4}, {"z": (z + 1) % 4}, {"z": (z + 3) % 4})
    return around, (x + 2 * z) % 4


class Quarters:
    def __init__(self, pieces, sems):
        self.sems, self.pieces, self.second = sems, pieces, []
        self.around, self.quarter = plane_neighbours()

    def cut(self, ref):
        size = ref.shape[0] // 4
        return ref.at[pl.ds(pl.multiple_of(self.quarter * size, 16), size), :]

    def fetch(self):
        self.first = [
            send(self.cut(source), self.cut(target), self.sems, 4 * at, device)
            for at, (source, target, device) in enumerate(self.pieces)
        ]

    def share(self, count=None):
        start = len(self.second) // 3
        stop = len(self.pieces) if count is None else min(start + count, len(self.pieces))
        for at in range(start, stop):
            self.first[at].wait_recv()
            here = self.cut(self.pieces[at][1])
            for spot in range(3):
                self.second.append(send(here, here, self.sems, 4 * at + 1 + spot, self.around[spot]))

    def arrive(self):
        for copy in self.second:
            copy.wait_recv()

    def close(self):
        for copy in self.first + self.second:
            copy.wait_send()


def image_spots():
    core, row, col = (lax.axis_index(name) for name in GROUP)
    flip = (col + core) % 2
    own = {"core": row, "row": flip, "col": col}
    other = {"core": row, "row": 1 - flip, "col": 1 - col}
    stays = jnp.logical_and(core == row, col == 0)
    return own, other, stays


def move(source, target, sems, at, device, stays):
    def remote():
        return pltpu.make_async_remote_copy(
            src_ref=source,
            dst_ref=target,
            send_sem=sems.at[0, at],
            recv_sem=sems.at[1, at],
            device_id=device,
            device_id_type=MESH,
        )

    @pl.when(jnp.logical_not(stays))
    def _():
        remote().start()

    @pl.when(stays)
    def _():
        pltpu.make_async_copy(source, target, sems.at[0, at]).start()

    def finish():
        @pl.when(jnp.logical_not(stays))
        def _():
            remote().wait()

        @pl.when(stays)
        def _():
            pltpu.make_async_copy(source, target, sems.at[0, at]).wait()

    return finish


class Home:
    def __init__(self, sems):
        core, row, col = (lax.axis_index(name) for name in GROUP)
        self.sems = sems
        self.sends = core == row
        self.stays = jnp.logical_and(self.sends, col == 0)
        self.leaves = jnp.logical_and(self.sends, col == 1)
        self.beside = {"core": (col + row) % 2, "col": 1 - col}
        self.waits = []

    def move(self, source, target, at):
        half = target.shape[1]

        def near():
            return self.copy(source.at[:, pl.ds(0, half)], target, 2 * at, at, group_device(1, 0, 0))

        def far():
            return self.copy(source.at[:, pl.ds(half, half)], target, 2 * at + 1, at, self.beside)

        def still():
            return pltpu.make_async_copy(source.at[:, pl.ds(0, half)], target, self.sems.at[0, 2 * at])

        pl.when(self.leaves)(lambda: near().start())
        pl.when(self.stays)(lambda: still().start())
        pl.when(self.sends)(lambda: far().start())

        def finish():
            pl.when(self.leaves)(lambda: near().wait_send())
            pl.when(self.stays)(lambda: still().wait())
            pl.when(self.sends)(lambda: far().wait_send())
            pl.when(jnp.logical_not(self.stays))(lambda: near().wait_recv())

        self.waits.append(finish)

    def copy(self, source, target, send_at, recv_at, device):
        return pltpu.make_async_remote_copy(
            src_ref=source,
            dst_ref=target,
            send_sem=self.sems.at[0, send_at],
            recv_sem=self.sems.at[1, recv_at],
            device_id=device,
            device_id_type=MESH,
        )

    def close(self):
        for finish in self.waits:
            finish()


def local(source, target, sems, at):
    copy = pltpu.make_async_copy(source, target, sems.at[0, at])
    copy.start()
    return copy


def greet(devices):
    barrier = pltpu.get_barrier_semaphore()
    for device in devices:
        pl.semaphore_signal(barrier, inc=1, device_id=device, device_id_type=MESH)


def meet(devices):
    pl.semaphore_wait(pltpu.get_barrier_semaphore(), len(devices))


def send(source, target, sems, at, device):
    copy = pltpu.make_async_remote_copy(
        src_ref=source,
        dst_ref=target,
        send_sem=sems.at[0, at],
        recv_sem=sems.at[1, at],
        device_id=device,
        device_id_type=MESH,
    )
    copy.start()
    return copy


class Totals:
    def __init__(self, chip, core_out, core_in, cross_out, cross_in, sems, partner, cross):
        self.refs = (chip, core_out, core_in, cross_out, cross_in)
        self.sems, self.partner, self.cross = sems, partner, cross
        self.copies = []

    def run(self, compute, ready):
        chip, core_out, core_in, cross_out, cross_in = self.refs
        rows = chip.shape[0]
        count = rows // STEP
        core_copies, cross_copies = [], []

        def pass_on(at):
            here = pl.ds(at * STEP, STEP)
            core_copies[at].wait_recv()
            total = chip[here, :] + core_in[here, :].astype(F32)
            chip[here, :] = total
            if cross_out is not None:
                cross_out[here, :] = total.astype(BF)
                cross_copies.append(
                    send(cross_out.at[here, :], cross_in.at[here, :], self.sems, count + at, self.cross)
                )

        for at in range(count):
            here = pl.ds(at * STEP, STEP)
            chip[here, :] = compute(at * STEP)
            if at > 0:
                pass_on(at - 1)
            ready(at * STEP)
            core_out[here, :] = compute(rows + at * STEP).astype(BF)
            core_copies.append(
                send(core_out.at[here, :], core_in.at[here, :], self.sems, at, self.partner)
            )
        pass_on(count - 1)
        self.cross_copies = cross_copies
        self.copies = core_copies + cross_copies

    def chunk(self, row):
        chip, _, _, _, cross_in = self.refs
        here = pl.ds(row, STEP)
        self.cross_copies[row // STEP].wait_recv()
        half = chip.shape[1] // 2
        other = cross_in[here, :].astype(F32)
        return chip[here, :] + jnp.concatenate((other[:, half:], other[:, :half]), axis=1)

    def close(self):
        for copy in self.copies:
            copy.wait_send()


def when_starting(copies):
    return lambda row: copies[row // ROWS].wait_recv() if row % ROWS == 0 else None


def spread(fill, whole, sems, partner):
    rows = whole.shape[0] // 2
    copies = []
    for at in range(rows // ROWS):
        here = pl.ds(at * ROWS, ROWS)
        whole[here, :] = fill(at * ROWS)
        if at == 0:
            yield None
        copies.append(
            send(whole.at[here, :], whole.at[pl.ds(rows + at * ROWS, ROWS), :], sems, at, partner)
        )
    yield copies


def fill_and_send(fill, whole, sems, devices):
    steps = spread(fill, whole, sems, devices[0])
    next(steps)
    meet(devices)
    return next(steps)


def arrive_kernel(
    token_ref, wq_load, wk_load, wv_load, one_gain, one_shift, two_gain, two_shift, bias_load,
    query_load, key_load, out_ref, w_qkv_ref, later_ref, vector_ref, gain_ref,
    landed, sems, share_sems,
):
    around, _ = plane_neighbours()
    devices = whole_group() + list(around)
    greet(devices)
    core = lax.axis_index("core")
    own, other, stays = image_spots()
    beside = group_device(0, 0, 1)
    half = token_ref.shape[1]
    meet(devices)
    finish = move(token_ref, landed.at[:, pl.ds(0, half)], sems, 0, own, stays)
    copies = [send(token_ref, landed.at[:, pl.ds(half, half)], sems, 1, other)]
    span = w_qkv_ref.shape[0] // 3

    def turned(ref, layer):
        whole = ref[layer].astype(F32).T
        return jnp.where(core == 0, whole[:span], whole[span:]).astype(BF)

    loads = (wq_load, wk_load, wv_load)
    for at, load in enumerate(loads):
        w_qkv_ref[pl.ds(at * span, span), 0:half] = turned(load(), 0)
    shared = Quarters(
        [(w_qkv_ref.at[:, pl.ds(0, half)], w_qkv_ref.at[:, pl.ds(half, half)], beside)], share_sems
    )
    shared.fetch()
    refs = [load() for load in (one_gain, one_shift, two_gain, two_shift, bias_load)]
    for layer in range(vector_ref.shape[0]):
        rows = [ref[layer : layer + 1, :] for ref in refs]
        vector_ref[layer, :, 0:half] = jnp.concatenate(rows + [jnp.zeros((3, half), F32)], axis=0)
    copies.append(
        send(vector_ref.at[:, :, pl.ds(0, half)], vector_ref.at[:, :, pl.ds(half, half)], sems, 2, beside)
    )
    for at, load in enumerate(loads):
        later_ref[pl.ds(at * span, span), :] = turned(load(), 1)
    rows = [load()[layer : layer + 1, :] for layer in range(2) for load in (query_load, key_load)]
    rows.append(jnp.zeros((128 - len(rows), HEAD_DIM), F32))
    square = jnp.concatenate((jnp.concatenate(rows, axis=0), jnp.zeros((128, 128 - HEAD_DIM), F32)), axis=1).T
    for layer in range(2):
        gain_ref[layer] = square[0:HEAD_DIM, 2 * layer : 2 * layer + 2]
    shared.share()
    finish()
    copies[0].wait()
    out_ref[...] = landed[...].astype(F32)
    copies[1].wait()
    shared.arrive()
    shared.close()


class Weights(Quarters):
    def __init__(self, pieces, kept, keep_sems, share_sems):
        self.kept = [local(source, target, keep_sems, at) for at, (source, target) in enumerate(kept)]
        super().__init__(pieces, share_sems)

    def arrive(self):
        super().arrive()
        for copy in self.kept:
            copy.wait()


def feed_weights(layer, raw_up, raw_down, w_up, w_down, keep_sems, share_sems):
    core, beside = lax.axis_index("core"), group_device(0, 0, 1)
    units, half = w_up.shape[1], w_up.shape[0] // 2
    here = pl.ds(pl.multiple_of(core * units, units), units)
    up, down = raw_up.at[layer, :, here], raw_down.at[layer, here, :]
    return Weights(
        [(up, w_up.at[pl.ds(half, half), :], beside), (down, w_down.at[:, pl.ds(half, half)], beside)],
        [(up, w_up.at[pl.ds(0, half), :]), (down, w_down.at[:, pl.ds(0, half)])],
        keep_sems,
        share_sems,
    )


def out_weights(layer, raw_out, w_out, keep_sems, share_sems):
    core = lax.axis_index("core")
    half, span = w_out.shape[1] // 2, w_out.shape[0] // 4
    beside, cross, across = group_device(0, 0, 1), group_device(0, 1, 1), group_device(0, 1, 0)
    pieces, kept = [], []
    for at in range(2):
        source = raw_out.at[layer, pl.ds((core + at - 2 * at * core) * span, span), :]
        for device, row, col in ((beside, 0, half), (cross, half, half), (across, half, 0)):
            pieces.append((source, w_out.at[pl.ds(row + at * span, span), pl.ds(col, half)], device))
        kept.append((source, w_out.at[pl.ds(at * span, span), pl.ds(0, half)]))
    return Weights(pieces, kept, keep_sems, share_sems)


def attend_forward_kernel(layer, flush, resid_load, w_qkv_load, gain_load, vector_load, raw_out_ref, *refs):
    if layer == 0:
        raw_up_ref, raw_down_ref, *refs = refs
    out_ref, seen_ref, qkv_ref, mixed_ref, total_ref, w_out_ref, *refs = refs
    if layer == 0:
        w_up_ref, w_down_ref, *refs = refs
    joined, seen_sems, head_sems, keep_sems, share_sems, *feed_sems = refs
    near, cross, far = partners()
    devices = (near, cross, far, group_device(0, 0, 1), group_device(0, 1, 0)) + plane_neighbours()[0]
    greet(devices)
    resid_ref, vector_ref = resid_load(), vector_load().at[layer]
    rows = resid_ref.shape[0]
    heads = mixed_ref.shape[0] // HEAD_DIM
    span = heads * HEAD_DIM

    def fill(row):
        normal, _ = norm(resid_ref[pl.ds(row, ROWS), :])
        return (normal * vector_ref[0:1, :] + vector_ref[1:2, :]).astype(BF)

    copies = fill_and_send(fill, seen_ref, seen_sems, devices)
    fetched = []
    if layer == 0:
        fetched.append(feed_weights(layer, raw_up_ref, raw_down_ref, w_up_ref, w_down_ref, *feed_sems))
    fetched.append(out_weights(layer, raw_out_ref, w_out_ref, keep_sems, share_sems))
    for shared in fetched:
        shared.fetch()
    w_qkv_ref = w_qkv_load()
    for at in range(2 * rows // ROWS):
        if at * ROWS >= rows:
            copies[at - rows // ROWS].wait_recv()
        here = pl.ds(at * ROWS, ROWS)
        qkv_ref[:, here] = dot(w_qkv_ref[...], seen_ref[here, :], 1, 1)
    flush(seen_ref, qkv_ref)
    gains = gain_load()[layer]
    for head in range(heads):
        if layer == 0 and head == 1:
            fetched[0].share(1)
        if head == 2:
            for shared in fetched:
                shared.share()
        own = pl.ds(head * HEAD_DIM, HEAD_DIM)
        query = (head_norm(qkv_ref[own, :])[0] * gains[:, 0:1]).astype(BF)
        key = head_norm(qkv_ref[pl.ds(span + head * HEAD_DIM, HEAD_DIM), :])[0] * gains[:, 1:2]
        key_rows = key.T.astype(BF)
        value = qkv_ref[pl.ds(2 * span + head * HEAD_DIM, HEAD_DIM), :].astype(BF)
        for at in range(0, 2 * rows, BLOCK):
            expo = jnp.exp2(dot(key_rows, query[:, at : at + BLOCK]) * SCALE2)
            total = jnp.sum(expo, axis=0, keepdims=True)
            mixed = (dot(value, expo.astype(BF)) * (1.0 / total)).astype(BF)
            mixed_ref[own, at : at + BLOCK] = mixed
            if at < rows:
                joined[own, at : at + BLOCK] = mixed
            total_ref[head : head + 1, at : at + BLOCK] = jnp.log2(total)
        mine, others = pl.ds(0, rows), pl.ds(rows, rows)
        for spot, (device, columns) in enumerate(((near, others), (cross, mine), (far, others))):
            copies.append(
                send(
                    mixed_ref.at[own, columns],
                    joined.at[pl.ds((spot + 1) * span + head * HEAD_DIM, HEAD_DIM), :],
                    head_sems,
                    head * 3 + spot,
                    device,
                )
            )
    flush(mixed_ref, total_ref)
    fetched[-1].arrive()
    flush(w_out_ref)
    for copy in copies[-3 * heads :]:
        copy.wait_recv()
    for at in range(rows // ROWS):
        here = pl.ds(at * ROWS, ROWS)
        out_ref[here, :] = resid_ref[here, :] + dot(joined[:, here], w_out_ref[...], 0, 0)
    if layer == 0:
        fetched[0].arrive()
    for copy in copies:
        copy.wait_send()
    for shared in fetched:
        shared.close()


def feed_forward_kernel(
    layer, last, flush, resid_load, w_up_load, bias_load, w_down_load, vector_load, side_ref, *refs
):
    if last:
        out_ref, seen_ref, active_ref, slope_ref, side_out, low_ref = refs[:6]
        chip, core_out, core_in, landed, seen_sems, total_sems, side_sems = refs[6:]
        cross_out, cross_in = None, None
    else:
        raw_up_ref, raw_down_ref, *refs = refs
        out_ref, seen_ref, active_ref, slope_ref, side_out, next_up_ref, next_down_ref = refs[:7]
        chip, core_out, core_in, cross_out, cross_in = refs[7:12]
        seen_sems, total_sems, side_sems, keep_sems, share_sems = refs[12:]
    near, cross, _ = partners()
    beside = group_device(0, 0, 1)
    devices = whole_group() if last else (near, cross, beside) + plane_neighbours()[0]
    greet(devices)
    core = lax.axis_index("core")
    resid_ref, vector_ref = resid_load(), vector_load().at[layer]
    half = resid_ref.shape[1] // 2

    def fill(row):
        normal, _ = norm(resid_ref[pl.ds(row, ROWS), :])
        return (normal * vector_ref[2:3, :] + vector_ref[3:4, :]).astype(BF)

    if last:
        steps = spread(fill, seen_ref, seen_sems, near)
        next(steps)
        meet(devices)
        copies = next(steps)
        own, other, stays = image_spots()
        arrived = move(side_ref, landed.at[:, pl.ds(0, half)], side_sems, 0, own, stays)
        side = send(side_ref, landed.at[:, pl.ds(half, half)], side_sems, 1, other)
    else:
        copies = fill_and_send(fill, seen_ref, seen_sems, devices)
        kept = local(side_ref, side_out.at[:, pl.ds(0, half)], side_sems, 0)
        side = send(side_ref, side_out.at[:, pl.ds(half, half)], side_sems, 1, beside)
        shared = feed_weights(
            layer + 1, raw_up_ref, raw_down_ref, next_up_ref, next_down_ref, keep_sems, share_sems
        )
        shared.fetch()

    w_up_ref, w_down_ref, bias_ref = w_up_load(), w_down_load(), bias_load()
    units = w_up_ref.shape[1]
    bias = bias_ref[layer : layer + 1, pl.ds(pl.multiple_of(core * units, units), units)]

    def compute(row):
        here = pl.ds(row, STEP)
        hidden = dot(seen_ref[here, :], w_up_ref[...]) + bias
        active, slope = gelu_parts(hidden)
        active = active.astype(BF)
        active_ref[here, :] = active
        slope_ref[here, :] = slope.astype(BF)
        return dot(active, w_down_ref[...])

    totals = Totals(chip, core_out, core_in, cross_out, cross_in, total_sems, near, cross)
    totals.run(compute, when_starting(copies))
    flush(seen_ref, active_ref, slope_ref)
    if not last:
        shared.share()
    for row in range(0, resid_ref.shape[0], STEP):
        here = pl.ds(row, STEP)
        total = chip[here, :] if last else totals.chunk(row)
        out_ref[here, :] = resid_ref[here, :] + (total + vector_ref[4:5, :])
        if last:
            low_ref[here, :] = total.astype(BF)
    for copy in copies:
        copy.wait_send()
    totals.close()
    side.wait()
    if last:
        arrived()
        side_out[...] = landed[...].astype(F32)
    else:
        kept.wait()
        shared.arrive()
        shared.close()


def feed_backward_kernel(plan, flush, *refs):
    refs = iter(refs)

    def take(count):
        return [next(refs) for _ in range(count)]

    grad_load, resid_load, seen_load, active_load, slope_load, w_up_load, w_down_load, vector_load = take(8)
    parts = take(plan["parts"])
    out_ref, up_ref, down_ref, small_ref = take(4)
    if parts:
        (shard_ref,) = take(1)
    branch, hidden, chip, core_out, core_in, cross_out, cross_in, seen_sems, total_sems = take(9)
    near, cross, _ = partners()
    devices = (near, cross)
    steps = iter(())
    if parts:
        (load_sems,) = take(1)
        beside = take_scatter(ATTEND_SMALL_CHUNKS, refs)
        steps = loaded_scatter(ATTEND_SMALL_CHUNKS, parts, plan["copies"], load_sems, *beside)
        devices += tuple(device for device, _ in link_bits().values())
    greet(devices)
    next(steps, None)
    grad_ref = grad_load()
    width = grad_ref.shape[1]
    copies = fill_and_send(
        lambda row: grad_ref[pl.ds(row, ROWS), :].astype(BF), branch, seen_sems, devices
    )
    next(steps, None)
    w_down_ref, slope_ref, w_up_ref = w_down_load(), slope_load(), w_up_load()

    def compute(row):
        here = pl.ds(row, STEP)
        active_grad = dot(branch[here, :], w_down_ref[...], 1, 1)
        low = (active_grad * slope_ref[here, :].astype(F32)).astype(BF)
        hidden[here, :] = low
        return dot(low, w_up_ref[...], 1, 1)

    totals = Totals(chip, core_out, core_in, cross_out, cross_in, total_sems, near, cross)
    totals.run(compute, when_starting(copies))
    next(steps, None)
    rows = grad_ref.shape[0]
    active_ref, seen_ref, resid_ref = active_load(), seen_load(), resid_load()
    vector_ref = vector_load().at[0 if parts else 1]
    half = width // 2
    for at in range(0, width, ROWS):
        down_ref[at : at + ROWS, :] = dot(active_ref[:, at : at + ROWS], branch[...], 0, 0).astype(BF)
        up_ref[at : at + ROWS, :] = dot(seen_ref[:, at : at + ROWS], hidden[...], 0, 0).astype(BF)
    flush(up_ref, down_ref)
    next(steps, None)
    bias_down = jnp.sum(branch[0:rows, :].astype(F32), axis=0, keepdims=True)
    bias_up = jnp.sum(hidden[...].astype(F32), axis=0, keepdims=True)
    gain_sum = jnp.zeros((1, width), F32)
    shift_sum = jnp.zeros((1, width), F32)
    for row in range(0, rows, STEP):
        here = pl.ds(row, STEP)
        grad = totals.chunk(row)
        normal, factor = norm(resid_ref[here, :])
        gain_sum = gain_sum + jnp.sum(grad * normal, axis=0, keepdims=True)
        shift_sum = shift_sum + jnp.sum(grad, axis=0, keepdims=True)
        out_ref[here, :] = grad_ref[here, :] + norm_back(grad, normal, factor, vector_ref[2:3, :])
        if row in (0, 2 * STEP):
            next(steps, None)
    height = small_ref.shape[0]
    small_ref[...] = jnp.concatenate(
        [gain_sum, shift_sum, bias_down]
        + [jnp.concatenate((bias_up[:, i * half : (i + 1) * half],) * 2, axis=1) for i in range(2)]
        + [jnp.zeros((height - 5, width), F32)],
        axis=0,
    ).astype(small_ref.dtype)
    for _ in steps:
        pass
    if parts:
        keep_shards(beside[1], shard_ref)
    for copy in copies:
        copy.wait_send()
    totals.close()


def attend_backward_kernel(plan, flush, *refs):
    refs = iter(refs)

    def take(count):
        return [next(refs) for _ in range(count)]

    last = plan["last"]
    grad_load, resid_load, seen_load, qkv_load, mixed_load, total_load = take(6)
    w_qkv_load, w_out_load, gain_load, vector_load = take(4)
    parts = take(2)
    if last:
        shard_load, other_shard_load, vec_load, final_load, low_ref = take(5)
        result_ref, token_in, layer_both, feed_both, tail_both, vec_pair = take(6)
    else:
        out_ref, grad_qkv_ref, grad_out_ref, small_ref, shard_ref = take(5)
    proj, mixed_grad, qkv_grad, gains_own, gains_in = take(5)
    chip, core_out, core_in, cross_out, cross_in, seen_sems, total_sems, gain_sems = take(8)
    (load_sems,) = take(1)
    feed_beside = take_scatter(FEED_CHUNKS, refs)
    feed_steps = loaded_scatter(FEED_CHUNKS, parts, plan["copies"], load_sems, *feed_beside)
    links = link_bits()
    near, cross, _ = partners()
    devices = (near, cross) + tuple(device for device, _ in links.values())
    if last:
        low_in, result_low, token_low, home_sems = take(4)
        vec, vec_x, vec_z, vec_mid, vec_col, vec_sems = take(6)
        tail_work, tail_landing, tail_sems = take_scatter(ATTEND_CHUNKS, refs)
        layer_gather = take(2)
        feed_gather = take(2)
        tail_gather = take(2)
        x, z = lax.axis_index("x"), lax.axis_index("z")
        devices = tuple(whole_group()) + tuple(links[name][0] for name in ("x1", "x2", "z1", "z2"))
        devices += ({"x": (x + 2) % 4}, {"z": (z + 2) % 4})
    greet(devices)
    next(feed_steps)
    grad_ref = grad_load()
    rows, width = grad_ref.shape
    half = width // 2
    copies = fill_and_send(
        lambda row: grad_ref[pl.ds(row, ROWS), :].astype(BF), proj, seen_sems, devices
    )
    next(feed_steps)
    if last:
        home = Home(home_sems)

        def low_copy():
            return home.copy(low_ref, low_in, 11, 11, cross)

        pl.when(jnp.logical_not(home.sends))(lambda: low_copy().start())
        shards = [shard_load().at[pl.ds(16 * at, 16), :] for at in range(len(FEED_CHUNKS))]
        shards += [other_shard_load().at[pl.ds(16 * at, 16), :] for at in range(len(ATTEND_SMALL_CHUNKS))]
        layer_steps = gather(LAYER_CHUNKS, shards, layer_both, *layer_gather)
        next(layer_steps)
    w_out_ref = w_out_load()
    span = mixed_grad.shape[0]
    for at in range(2 * rows // ROWS):
        if at * ROWS >= rows:
            copies[at - rows // ROWS].wait_recv()
        here = pl.ds(at * ROWS, ROWS)
        mixed_grad[:, here] = dot(w_out_ref[pl.ds(0, span), :], proj[here, :], 1, 1).astype(BF)
    gains, qkv_ref, total_ref = gain_load()[0 if last else 1], qkv_load(), total_load()
    scale = HEAD_DIM ** (-0.5)
    gains_sum = jnp.zeros((HEAD_DIM, 2), F32)
    slot = 0
    for head in range(span // HEAD_DIM):
        own = pl.ds(head * HEAD_DIM, HEAD_DIM)
        key_at = pl.ds(span + head * HEAD_DIM, HEAD_DIM)
        value_at = pl.ds(2 * span + head * HEAD_DIM, HEAD_DIM)
        query_normal, query_factor = head_norm(qkv_ref[own, :])
        key_normal, key_factor = head_norm(qkv_ref[key_at, :])
        query = (query_normal * gains[:, 0:1]).astype(BF)
        key_full = key_normal * gains[:, 1:2]
        key = key_full.astype(BF)
        key_rows = key_full.T.astype(BF)
        value_rows = qkv_ref[value_at, :].T.astype(BF)
        key_sum = jnp.zeros(key.shape, F32)
        value_sum = jnp.zeros(key.shape, F32)
        query_parts = []
        for at in range(0, 2 * rows, BLOCK):
            grad = mixed_grad[own, at : at + BLOCK]
            logits = dot(key_rows, query[:, at : at + BLOCK]) * SCALE2
            probs = jnp.exp2(logits - total_ref[head : head + 1, at : at + BLOCK])
            pulled = dot(value_rows, grad)
            delta = jnp.sum(probs * pulled, axis=0, keepdims=True)
            score_grad = (probs * (pulled - delta)).astype(BF)
            query_parts.append(dot(key, score_grad))
            key_sum = key_sum + dot(query[:, at : at + BLOCK], score_grad, 1, 1)
            value_sum = value_sum + dot(grad, probs.astype(BF), 1, 1)
            slot += 1
            if last and slot in (5, 10):
                next(layer_steps, None)
            if slot == (12 if last else 9):
                next(feed_steps)
        query_sum = jnp.concatenate(query_parts, axis=1) * scale
        key_sum = key_sum * scale
        qkv_grad[own, :] = head_norm_back(query_sum, query_normal, query_factor, gains[:, 0:1]).astype(BF)
        qkv_grad[key_at, :] = head_norm_back(key_sum, key_normal, key_factor, gains[:, 1:2]).astype(BF)
        qkv_grad[value_at, :] = value_sum.astype(BF)
        gains_sum = gains_sum + jnp.concatenate(
            (
                jnp.sum(query_sum * query_normal, axis=1, keepdims=True),
                jnp.sum(key_sum * key_normal, axis=1, keepdims=True),
            ),
            axis=1,
        )
    square = jnp.concatenate((gains_sum, jnp.zeros((HEAD_DIM, 126), F32)), axis=1)
    gains_own[...] = jnp.concatenate((square, jnp.zeros((128 - HEAD_DIM, 128), F32)), axis=0).T[0:8]
    gains_copy = send(gains_own, gains_in, gain_sems, 0, cross)
    w_qkv_ref = w_qkv_load()

    def compute(row):
        return dot(qkv_grad[:, pl.ds(row, STEP)], w_qkv_ref[...], 0, 0)

    totals = Totals(chip, core_out, core_in, cross_out, cross_in, total_sems, near, cross)
    seen_ref, mixed_ref, resid_ref = seen_load(), mixed_load(), resid_load()
    vector_ref = vector_load().at[0 if last else 1]
    if last:
        grad_qkv_ref, grad_out_ref = tail_work.at[pl.ds(0, 3 * span), :], tail_work.at[pl.ds(3 * span, span), :]

    def weight_grads():
        for at in range(0, 3 * span, span):
            here = pl.ds(at, span)
            grad_qkv_ref[here, :] = dot(qkv_grad[here, :], seen_ref[...]).astype(BF)
        grad_out_ref[...] = dot(mixed_ref[...], proj[...]).astype(BF)

    sums = [jnp.zeros((1, width), F32), jnp.zeros((1, width), F32)]

    def final_chunk(row):
        here = pl.ds(row, STEP)
        grad = totals.chunk(row)
        normal, factor = norm(resid_ref[here, :])
        sums[0] = sums[0] + jnp.sum(grad * normal, axis=0, keepdims=True)
        sums[1] = sums[1] + jnp.sum(grad, axis=0, keepdims=True)
        return grad_ref[here, :] + norm_back(grad, normal, factor, vector_ref[0:1, :])

    def small_rows(height):
        gains_copy.wait()
        shared = gains_own[0:2, :] + gains_in[0:2, :]
        blank = jnp.zeros((2, half - 128), F32)
        return jnp.concatenate(
            sums
            + [jnp.concatenate((shared, blank, shared, blank), axis=1), jnp.zeros((height - 4, width), F32)],
            axis=0,
        )

    if not last:
        totals.run(compute, lambda row: next(feed_steps) if row == 3 * STEP else None)
        weight_grads()
        flush(grad_qkv_ref, grad_out_ref)
        next(feed_steps)
        for row in range(0, rows, STEP):
            out_ref[pl.ds(row, STEP), :] = final_chunk(row)
            if row == STEP:
                next(feed_steps)
        small_ref[...] = small_rows(16).astype(BF)
        for _ in feed_steps:
            pass
        keep_shards(feed_beside[1], shard_ref)
        for copy in copies:
            copy.wait_send()
        totals.close()
        return

    def whole(first, second):
        yield from first
        yield from second

    weight_grads()
    tail = whole(
        scatter(ATTEND_CHUNKS, tail_work, tail_landing, tail_sems),
        gather(ATTEND_CHUNKS, tail_landing[4::5], tail_both, *tail_gather),
    )
    next(tail)
    feed = whole(feed_steps, gather(FEED_CHUNKS, feed_beside[1][4::5], feed_both, *feed_gather))
    totals.run(compute, lambda row: None)
    next(feed)
    next(layer_steps)
    final_ref = final_load()

    @pl.when(home.sends)
    def _():
        low_copy().wait_recv()
        other = low_in[...].astype(F32)
        other = jnp.concatenate((other[:, half:], other[:, :half]), axis=1)
        result_low[...] = (final_ref[...] + other).astype(BF)

    pl.when(jnp.logical_not(home.sends))(lambda: low_copy().wait_send())
    home.move(result_low, result_ref, 0)

    def token_chunk(row):
        here = pl.ds(row, STEP)
        token_low[here, :] = final_chunk(row).astype(BF)
        home.move(token_low.at[here, :], token_in.at[here, :], 1 + row // STEP)

    next(tail)
    token_chunk(0)
    next(feed)
    token_chunk(STEP)
    next(layer_steps)
    next(tail)
    next(feed)
    next(tail)
    token_chunk(2 * STEP)
    for _ in layer_steps:
        pass
    flush(layer_both)
    next(feed)
    next(tail)
    next(feed)
    token_chunk(3 * STEP)
    vec[...] = jnp.concatenate((small_rows(8), vec_load()[...]), axis=0)
    vec_copies = []

    def share(source, landing, axis, place, at):
        batch = []
        for step in range(1, 4):
            batch.append(
                send(source, landing.at[step - 1], vec_sems, at + step - 1, {axis: (place + step) % 4})
            )
        vec_copies.extend(batch)
        return batch

    def collect(source, landing, batch):
        for copy in batch:
            copy.wait_recv()
        return (source[...] + landing[0]) + (landing[1] + landing[2])

    batch = share(vec, vec_x, "x", x, 0)
    next(tail)
    next(feed)
    vec_mid[0] = collect(vec, vec_x, batch)
    batch = share(vec_mid.at[0], vec_z, "z", z, 3)
    next(tail)
    next(feed)
    vec_mid[1] = collect(vec_mid.at[0], vec_z, batch)
    vec_copies.append(send(vec_mid.at[1, :, pl.ds(half, half)], vec_col, vec_sems, 6, links["col"][0]))
    next(tail)
    vec_copies[-1].wait_recv()
    core = lax.axis_index("core")
    vec_pair[core] = vec_mid[1, :, 0:half] + vec_col[...]
    vec_copies.append(send(vec_pair.at[core], vec_pair.at[core], vec_sems, 7, near))
    next(tail)
    vec_copies[-1].wait_recv()
    for _ in feed:
        pass
    flush(feed_both)
    for _ in tail:
        pass
    home.close()
    for copy in copies + vec_copies:
        copy.wait_send()
    totals.close()


class Load:
    def __init__(self, source, target, sem):
        self.copy = pltpu.make_async_copy(source, target, sem)
        self.copy.start()
        self.target, self.waited = target, False

    def __call__(self):
        if not self.waited:
            self.copy.wait()
            self.waited = True
        return self.target


def call(kernel, name, collective_id, inputs, outs, scratch):
    vmem = pl.BlockSpec(memory_space=pltpu.VMEM)
    hbm = pl.BlockSpec(memory_space=pl.ANY)

    def kind(spec):
        return spec[0] if isinstance(spec, tuple) and isinstance(spec[0], str) else "block"

    def bare(spec):
        return spec if kind(spec) == "block" else spec[1]

    kinds = [kind(spec) for spec in inputs]
    values = [bare(spec) for spec in inputs]
    loaded = [at for at, k in enumerate(kinds) if k == "load"]
    early = [at for at, spec in enumerate(outs) if kind(spec) == "early"]

    def body(*refs):
        refs = list(refs)
        given, refs = refs[: len(inputs)], refs[len(inputs) :]
        made, refs = refs[: len(outs)], refs[len(outs) :]
        own, refs = refs[: len(scratch)], refs[len(scratch) :]
        staged, refs = refs[: len(loaded)], refs[len(loaded) :]
        kept, (sems, out_sems) = refs[: len(early)], refs[len(early) :]
        loads = [Load(given[at], staged[i], sems.at[i]) for i, at in enumerate(loaded)]
        for at, load in zip(loaded, loads):
            given[at] = load
        copies = {}

        def flush(*flushed):
            for ref in flushed:
                i = next(i for i, one in enumerate(kept) if one is ref)
                copies[i] = pltpu.make_async_copy(ref, made[early[i]], out_sems.at[i])
                copies[i].start()

        results = list(made)
        for i, at in enumerate(early):
            results[at] = kept[i]
        if early:
            kernel(flush, *given, *results, *own)
        else:
            kernel(*given, *results, *own)
        flush(*(ref for i, ref in enumerate(kept) if i not in copies))
        for i in sorted(copies):
            copies[i].wait()
        for load in loads:
            load()

    return pl.pallas_call(
        body,
        in_specs=[vmem if k == "block" else hbm for k in kinds],
        out_specs=[vmem if kind(spec) == "block" else hbm for spec in outs],
        out_shape=[jax.ShapeDtypeStruct(*bare(spec)) for spec in outs],
        scratch_shapes=scratch
        + [pltpu.VMEM(values[at].shape, values[at].dtype) for at in loaded]
        + [pltpu.VMEM(*bare(outs[at])) for at in early]
        + [pltpu.SemaphoreType.DMA((max(1, len(loaded)),)), pltpu.SemaphoreType.DMA((max(1, len(early)),))],
        compiler_params=pltpu.CompilerParams(
            collective_id=collective_id,
            has_side_effects=collective_id is not None,
            vmem_limit_bytes=58 * 2**20,
        ),
        name=name,
    )(*values)


def pair_sems(count):
    return pltpu.SemaphoreType.DMA((2, count))


def total_scratch(rows, width):
    return [pltpu.VMEM((rows, width), F32)] + [pltpu.VMEM((rows, width), BF)] * 4


def total_sems(rows):
    return [pair_sems(rows // ROWS), pair_sems(2 * rows // STEP)]


def arrive(tokens, w_query, w_key, w_value, vectors):
    rows, half = tokens.shape
    span = w_query.shape[2] // 2
    layers = w_query.shape[0]
    return call(
        arrive_kernel,
        "arrive",
        10,
        [("hbm", tokens)] + [("load", value) for value in (w_query, w_key, w_value) + vectors],
        [
            ((rows, 2 * half), F32),
            ((3 * span, 2 * half), BF),
            ((3 * span, half), BF),
            ((layers, 8, 2 * half), F32),
            ((layers, HEAD_DIM, 2), F32),
        ],
        [pltpu.VMEM((rows, 2 * half), BF), pair_sems(3), pair_sems(4)],
    )


def attend_forward(layer, resid, w_qkv, gains, vectors, raws):
    rows, width = resid.shape
    span = w_qkv.shape[0] // 3
    units = raws[1].shape[2] // 2
    outs = [
        ((rows, width), F32),
        ((2 * rows, width), BF),
        ((3 * span, 2 * rows), F32),
        ((span, 2 * rows), BF),
        ((span // HEAD_DIM, 2 * rows), F32),
        ((width, width), BF),
    ]
    scratch = [pltpu.VMEM((4 * span, rows), BF), pair_sems(rows // ROWS), pair_sems(3 * span // HEAD_DIM)]
    scratch += [pair_sems(2), pair_sems(24)]
    if layer == 0:
        outs += [((width, units), BF), ((units, width), BF)]
        scratch += [pair_sems(2), pair_sems(8)]
    return call(
        functools.partial(attend_forward_kernel, layer),
        "attend_forward_%d" % layer,
        8 + layer,
        [("load", value) for value in (resid, w_qkv, gains, vectors)]
        + [("hbm", value) for value in (raws if layer == 0 else raws[:1])],
        [("early", out) for out in outs],
        scratch,
    )


def feed_forward(layer, last, resid, w_up, up_bias, w_down, vectors, side, raws):
    rows, width = resid.shape
    units = w_up.shape[1]
    outs = [((rows, width), F32), ((2 * rows, width), BF)] + [((2 * rows, units), BF)] * 2
    low = pltpu.VMEM((rows, width), BF)
    if last:
        outs += [((rows, width), F32), ((rows, width), BF)]
        scratch = [pltpu.VMEM((rows, width), F32), low, low, low]
    else:
        outs += [((side.shape[0], width), BF), ((width, units), BF), ((units, width), BF)]
        scratch = total_scratch(rows, width)
    scratch += total_sems(rows) + [pair_sems(2)]
    return call(
        functools.partial(feed_forward_kernel, layer, last),
        "feed_forward_%d" % layer,
        4 if last else 3,
        [("load", value) for value in (resid, w_up, up_bias, w_down, vectors)]
        + [("hbm", value) for value in (side,) + (() if last else raws[1:])],
        [("early", out) for out in outs],
        scratch if last else scratch + [pair_sems(2), pair_sems(8)],
    )


def feed_backward(operands, parts):
    grad, resid, seen, active, slope, w_up, w_down, vectors = operands
    rows, width = grad.shape
    units = w_up.shape[1]
    outs = [((rows, width), F32), ((width, units), BF), ((units, width), BF)]
    outs += [((8, width), F32) if parts else ((16, width), BF)]
    scratch = [pltpu.VMEM((2 * rows, width), BF), pltpu.VMEM((2 * rows, units), BF)]
    scratch += total_scratch(rows, width) + total_sems(rows)
    copies = []
    if parts:
        outs.append(((16 * len(ATTEND_SMALL_CHUNKS), width // 2), BF))
        scratch += [pltpu.SemaphoreType.DMA((len(parts),))] + scatter_scratch(ATTEND_SMALL_CHUNKS, width)
        row = 0
        for at, part in enumerate(parts):
            copies.append((at, (0, part.shape[0]), (0, width), row, 0))
            row += part.shape[0]
    return call(
        functools.partial(feed_backward_kernel, {"parts": len(parts), "copies": copies}),
        "feed_backward_and_sum" if parts else "feed_backward",
        7 if parts else 5,
        [("load", value) for value in operands] + [("hbm", value) for value in parts],
        [("early", out) for out in outs],
        scratch,
    )


def link_bits():
    x, z = lax.axis_index("x"), lax.axis_index("z")
    col = lax.axis_index("col")
    return {
        "x1": ({"x": x + 1 - 2 * (x % 2)}, ((x + 1) // 2) % 2),
        "x2": ({"x": 3 - x}, x // 2),
        "z1": ({"z": z + 1 - 2 * (z % 2)}, ((z + 1) // 2) % 2),
        "z2": ({"z": 3 - z}, z // 2),
        "col": ({"col": 1 - col}, None),
    }


ORDERS = (
    ("x1", "z1", "x2", "z2", "col"),
    ("z1", "x2", "z2", "col", "x1"),
    ("x2", "z2", "col", "x1", "z1"),
    ("z2", "col", "x1", "z1", "x2"),
    ("col", "x1", "z1", "x2", "z2"),
    ("x1", "z1", "x2", "z2", "col"),
    ("z1", "x2", "z2", "col", "x1"),
    ("x2", "z2", "col", "x1", "z1"),
    ("z2", "col", "x1", "z1", "x2"),
    ("col", "x2", "z2", "x1", "z1"),
)
UNIT = 256


def plan_chunks(rows, orders):
    return [(at * UNIT, UNIT, ORDERS[orders[at]]) for at in range(rows // UNIT)]


def step_shapes(rows, order, width):
    shapes = []
    for link in order:
        if link == "col":
            width //= 2
        else:
            rows //= 2
        shapes.append((rows, width))
    return shapes


def add_into(target, other, row, col_size):
    rows = target.shape[0]
    block = min(rows, 64)

    @pl.loop(0, rows // block)
    def _(at):
        here = pl.ds(pl.multiple_of(at * block, block), block)
        there = pl.ds(pl.multiple_of(row + at * block, 16), block)
        target[here, :] = (
            target[here, :].astype(F32) + other[there, :col_size].astype(F32)
        ).astype(BF)


def scatter(chunks, work, landing, sems):
    links = link_bits()
    state = [work.at[pl.ds(start, rows), :] for start, rows, _ in chunks]
    flight = [None] * len(chunks)
    sent = []

    def land(at, step):
        copy, keep_row, width = flight[at]
        copy.wait_recv()
        target = landing[at * 5 + step]
        add_into(target, state[at], keep_row, width)
        state[at] = target

    for step in range(5):
        for at, (start, rows, order) in enumerate(chunks):
            if step > 0:
                land(at, step - 1)
            device, bit = links[order[step]]
            landed = landing[at * 5 + step]
            size, width = landed.shape
            if bit is None:
                source = state[at].at[:, pl.ds(width, width)]
                keep_row = 0
            else:
                keep_row = bit * size
                source = state[at].at[pl.ds(pl.multiple_of((1 - bit) * size, size), size), :]
            copy = send(source, landed, sems, at * 5 + step, device)
            sent.append(copy)
            flight[at] = (copy, keep_row, width)
        yield
    for at in range(len(chunks)):
        land(at, 4)
    for copy in sent:
        copy.wait_send()


def gather(chunks, shards, both, sems, core_sems):
    core = lax.axis_index("core")
    links = link_bits()
    sent, region = [], []
    for at, (start, rows, order) in enumerate(chunks):
        offset, size = 0, rows
        for link in order:
            if links[link][1] is not None:
                size //= 2
                offset = offset + links[link][1] * size
        both[core, pl.ds(pl.multiple_of(start + offset, 16), size), :] = shards[at][...]
        region.append((start + offset, size))
    back = [[link for link in reversed(order) if link != "col"] for _, _, order in chunks]
    waiting = [None] * len(chunks)

    def settle(at):
        copy, bit, size = waiting[at]
        copy.wait_recv()
        lo, _ = region[at]
        region[at] = (lo - bit * size, 2 * size)

    for step in range(4):
        for at in range(len(chunks)):
            if step > 0:
                settle(at)
            lo, size = region[at]
            device, bit = links[back[at][step]]
            here = both.at[core, pl.ds(pl.multiple_of(lo, 16), size), :]
            copy = send(here, here, sems, at * 4 + step, device)
            sent.append(copy)
            waiting[at] = (copy, bit, size)
        yield
    last = []
    for at, (start, rows, order) in enumerate(chunks):
        settle(at)
        here = both.at[core, pl.ds(start, rows), :]
        last.append(send(here, here, core_sems, at, {"core": 1 - core}))
    yield
    for copy in last:
        copy.wait_recv()
    for copy in sent + last:
        copy.wait_send()


def scatter_scratch(chunks, width):
    shapes = [(sum(size for _, size, _ in chunks), width)]
    shapes += [shape for _, size, order in chunks for shape in step_shapes(size, order, width)]
    return [pltpu.VMEM(shape, BF) for shape in shapes] + [pair_sems(5 * len(chunks))]


def take_scatter(chunks, refs):
    return next(refs), [next(refs) for _ in range(5 * len(chunks))], next(refs)


def gather_scratch(chunks):
    return [pair_sems(4 * len(chunks)), pair_sems(len(chunks))]


def loaded_scatter(chunks, parts, copies, load_sems, work, landing, sems):
    loads = []
    for at, (source, rows, cols, row, col) in enumerate(copies):
        load = pltpu.make_async_copy(
            parts[source].at[pl.ds(rows[0], rows[1]), pl.ds(cols[0], cols[1])],
            work.at[pl.ds(row, rows[1]), pl.ds(col, cols[1])],
            load_sems.at[at],
        )
        load.start()
        loads.append(load)
    yield
    for load in loads:
        load.wait()
    yield from scatter(chunks, work, landing, sems)


def keep_shards(landing, shard_ref):
    for at, landed in enumerate(landing[4::5]):
        shard_ref[pl.ds(at * 16, 16), :] = landed[...]


FEED_CHUNKS = plan_chunks(6 * UNIT, (0, 1, 2, 3, 4, 9))
ATTEND_CHUNKS = plan_chunks(3 * UNIT, (0, 1, 2))
ATTEND_SMALL_CHUNKS = plan_chunks(4 * UNIT, (0, 1, 2, 3))
LAYER_CHUNKS = FEED_CHUNKS + [(start + 6 * UNIT, rows, order) for start, rows, order in ATTEND_SMALL_CHUNKS]


def feed_copies(first, base, units, width):
    half = width // 2
    copies = []
    for i in range(2):
        for j in range(2):
            copies.append((first, (i * half, half), (j * half, half), base + j * half, i * half))
    copies.append((first + 1, (0, units), (0, width), base + units, 0))
    return copies


def attend_backward(operands, parts, extras):
    grad, resid, seen, qkv, mixed, total, w_qkv, w_out, gains, vectors = operands
    rows, width = grad.shape
    half = width // 2
    span = mixed.shape[0]
    inputs = [("load", value) for value in operands]
    scratch = [
        pltpu.VMEM((2 * rows, width), BF),
        pltpu.VMEM((span, 2 * rows), BF),
        pltpu.VMEM((3 * span, 2 * rows), BF),
        pltpu.VMEM((8, 128), F32),
        pltpu.VMEM((8, 128), F32),
    ]
    scratch += total_scratch(rows, width) + total_sems(rows) + [pair_sems(1)]
    copies = feed_copies(0, 0, parts[1].shape[0], width)
    inputs += [("hbm", value) for value in parts]
    scratch += [pltpu.SemaphoreType.DMA((len(copies),))] + scatter_scratch(FEED_CHUNKS, width)
    if extras:
        inputs += [("load", value) for value in extras[:4]] + [("hbm", extras[4])]
        outs = [((rows, half), BF)] * 2
        for chunks in (LAYER_CHUNKS, FEED_CHUNKS, ATTEND_CHUNKS):
            outs.append(((2, len(chunks) * UNIT, half), BF))
        outs.append(((2, 16, half), F32))
        scratch += [pltpu.VMEM((rows, width), BF)] * 3 + [pair_sems(12)]
        scratch += [pltpu.VMEM((16, width), F32)] + [pltpu.VMEM((3, 16, width), F32)] * 2
        scratch += [pltpu.VMEM((2, 16, width), F32), pltpu.VMEM((16, half), F32), pair_sems(8)]
        scratch += scatter_scratch(ATTEND_CHUNKS, width)
        scratch += gather_scratch(LAYER_CHUNKS) + gather_scratch(FEED_CHUNKS) + gather_scratch(ATTEND_CHUNKS)
    else:
        outs = [
            ((rows, width), F32),
            ((3 * span, width), BF),
            ((span, width), BF),
            ((16, width), BF),
            ((16 * len(FEED_CHUNKS), half), BF),
        ]
    return call(
        functools.partial(attend_backward_kernel, {"last": bool(extras), "copies": copies}),
        "attend_backward_last" if extras else "attend_backward",
        1 if extras else 6,
        inputs,
        [("early", out) for out in outs],
        scratch,
    )


def finish_kernel(*refs):
    layer_load, feed_load, tail_load, vec_load, token_load, result_load = refs[:6]
    token_ref, result_ref, up_out, down_out, q_out, k_out, v_out, out_out, bias_out = refs[6:15]
    one_gain_out, one_shift_out, query_out, key_out, two_gain_out, two_shift_out, down_bias_out = refs[15:22]
    up_stage, down_stage, square_stage, token_stage, store_sems = refs[22:27]
    units, half = down_out.shape[1] // 2, down_out.shape[2]
    span = q_out.shape[2] // 2
    stores = []

    def store(stage, target):
        copy = pltpu.make_async_copy(stage, target, store_sems.at[len(stores)])
        copy.start()
        stores.append(copy)

    def finish_feed(layer, both, base):
        for spot in range(2):
            for part in range(units // half):
                up_stage[layer, :, pl.ds(spot * units + part * half, half)] = both[
                    spot, pl.ds(base + part * half, half), :
                ].astype(F32)
            down_stage[layer, pl.ds(spot * units, units), :] = both[
                spot, pl.ds(base + units, units), :
            ].astype(F32)
        store(up_stage.at[layer], up_out.at[layer])
        store(down_stage.at[layer], down_out.at[layer])

    def finish_attend(layer, both, base):
        for at, target in enumerate((q_out, k_out, v_out, out_out)):
            here = pl.ds(base + at * span, span)
            value = jnp.concatenate((both[0, here, :], both[1, here, :]), axis=0).astype(F32)
            square_stage[layer, at] = value if at == 3 else value.T
            store(square_stage.at[layer, at], target.at[layer])

    layer_both = layer_load()
    finish_feed(1, layer_both, 0)
    finish_attend(1, layer_both, 2 * units)
    finish_feed(0, feed_load(), 0)
    finish_attend(0, tail_load(), 0)
    token_stage[...] = token_load()[...].astype(F32)
    store(token_stage, token_ref)
    store(result_load(), result_ref)
    small_at = 2 * units + 4 * span
    vec = vec_load()
    for layer in range(2):
        if layer == 1:
            one = [layer_both[spot, pl.ds(small_at, 16), :].astype(F32) for spot in range(2)]
            two = [layer_both[spot, pl.ds(small_at + 16, 16), :].astype(F32) for spot in range(2)]
        else:
            one = [vec[spot, 0:8, :] for spot in range(2)]
            two = [vec[spot, 8:16, :] for spot in range(2)]
        for spot in range(2):
            for part in range(units // half):
                bias_out[layer : layer + 1, pl.ds(spot * units + part * half, half)] = two[spot][
                    3 + part : 4 + part
                ]
        for row, ref in enumerate((one_gain_out, one_shift_out, query_out, key_out)):
            ref[layer : layer + 1, :] = (one[0] + one[1])[row : row + 1, 0 : ref.shape[1]]
        for row, ref in enumerate((two_gain_out, two_shift_out, down_bias_out)):
            ref[layer : layer + 1, :] = (two[0] + two[1])[row : row + 1]
    for copy in stores:
        copy.wait()


def finish(values, units, span):
    rows, half = values[4].shape
    heads = 2 * span
    shapes = [(half, 2 * units), (2 * units, half)] + [(half, heads)] * 3 + [(heads, half)]
    outs = [("hbm", ((rows, half), F32)), ("hbm", ((rows, half), BF))]
    outs += [("hbm", ((2,) + shape, F32)) for shape in shapes]
    outs += [((2, size), F32) for size in (2 * units, half, half, HEAD_DIM, HEAD_DIM, half, half, half)]
    return call(
        finish_kernel,
        "finish",
        None,
        [("load", value) for value in values],
        outs,
        [
            pltpu.VMEM((2,) + shapes[0], F32),
            pltpu.VMEM((2,) + shapes[1], F32),
            pltpu.VMEM((2, 4, heads, half), F32),
            pltpu.VMEM((rows, half), F32),
            pltpu.SemaphoreType.DMA((14,)),
        ],
    )


def shards(
    tokens, ln1_gain, ln1_shift, w_query, w_key, w_value, query_gain, key_gain, w_out,
    ln2_gain, ln2_shift, w_up, up_bias, w_down, down_bias, cotangent,
):
    resid, w_qkv, later, vectors, gains = arrive(
        tokens, w_query, w_key, w_value,
        (ln1_gain, ln1_shift, ln2_gain, ln2_shift, down_bias, query_gain, key_gain),
    )
    caches, raws = [], (w_out, w_up, w_down)
    for at in range(2):
        last = at == 1
        resid_two, seen_one, qkv, mixed, total, *fetched = attend_forward(
            at, resid, w_qkv, gains, vectors, raws
        )
        out_here = fetched[0]
        if at == 0:
            up_here, down_here = fetched[1:]
        result, seen_two, active, slope, *side = feed_forward(
            at, last, resid_two, up_here, up_bias, down_here, vectors, cotangent if last else later, raws
        )
        caches.append(
            (
                (resid_two, seen_two, active, slope, up_here, down_here, vectors),
                (resid, seen_one, qkv, mixed, total, w_qkv, out_here, gains, vectors),
            )
        )
        if not last:
            resid = result
            w_qkv, up_here, down_here = side
    grad, low = side
    grad, grad_up, grad_down, small_two = feed_backward((grad,) + caches[1][0], ())
    grad, grad_qkv, grad_out, small_one, shard = attend_backward(
        (grad,) + caches[1][1], (grad_up, grad_down), ()
    )
    grad, grad_up, grad_down, small_zero, other_shard = feed_backward(
        (grad,) + caches[0][0], (grad_qkv, grad_out, small_one, small_two)
    )
    out, low_grad, layer_both, feed_both, tail_both, vec = attend_backward(
        (grad,) + caches[0][1], (grad_up, grad_down), (shard, other_shard, small_zero, result, low)
    )
    (
        grad_tokens, out, grad_up, grad_down, grad_q, grad_k, grad_v, grad_out, grad_up_bias,
        grad_one_gain, grad_one_shift, grad_query_gain, grad_key_gain,
        grad_two_gain, grad_two_shift, grad_down_bias,
    ) = finish((layer_both, feed_both, tail_both, vec, low_grad, out), w_up.shape[2] // 2, w_query.shape[2] // 2)
    return (
        out, grad_tokens, grad_one_gain, grad_one_shift, grad_q, grad_k, grad_v,
        grad_query_gain, grad_key_gain, grad_out, grad_two_gain, grad_two_shift,
        grad_up, grad_up_bias, grad_down, grad_down_bias,
    )


def solution(mesh):
    fine = Mesh(mesh.devices.reshape(4, 4, 2, 2, 2), ("x", "z", "core", "row", "col"))
    rows = ("x", "z", "core", "row")
    in_specs = (
        P(rows, "col"),
        P(None, "col"),
        P(None, "col"),
        P(None, "col", "row"),
        P(None, "col", "row"),
        P(None, "col", "row"),
        P(),
        P(),
        P(None, "row", "col"),
        P(None, "col"),
        P(None, "col"),
        P(None, "col", "row"),
        P(None, "row"),
        P(None, "row", "col"),
        P(None, "col"),
        P(rows, "col"),
    )
    out_specs = (P(rows, "col"),) * 2 + in_specs[1:15]
    return jax.shard_map(shards, mesh=fine, in_specs=in_specs, out_specs=out_specs, check_vma=False)
```

```python
import functools

import jax
import jax.numpy as jnp
from jax import lax
from jax.experimental import pallas as pl
from jax.experimental.pallas import tpu as pltpu
from jax.sharding import Mesh, PartitionSpec as P

HEAD_DIM = 64
EPS = 1e-06
LOG2E = 1.4426950408889634
BF = jnp.bfloat16
F32 = jnp.float32
GROUP = ("core", "row", "col")
BLOCK = 256


def dot(left, right, left_axis=1, right_axis=0):
    return lax.dot_general(
        left, right, (((left_axis,), (right_axis,)), ((), ())), preferred_element_type=F32
    )


MESH = pl.DeviceIdType.MESH
ROWS = 256
STEP = 128


def norm(resid):
    mean = jnp.mean(resid, axis=1, keepdims=True)
    centred = resid - mean
    factor = lax.rsqrt(jnp.mean(centred * centred, axis=1, keepdims=True) + EPS)
    return centred * factor, factor


def norm_back(grad, normal, factor, gain):
    scaled = grad * gain
    first = jnp.mean(scaled, axis=1, keepdims=True)
    second = jnp.mean(scaled * normal, axis=1, keepdims=True)
    return factor * (scaled - first - normal * second)


def head_norm(values):
    mean = jnp.mean(values, axis=0, keepdims=True)
    centred = values - mean
    factor = lax.rsqrt(jnp.mean(centred * centred, axis=0, keepdims=True) + EPS)
    return centred * factor, factor


def head_norm_back(grad, normal, factor, gain):
    scaled = grad * gain
    first = jnp.mean(scaled, axis=0, keepdims=True)
    second = jnp.mean(scaled * normal, axis=0, keepdims=True)
    return factor * (scaled - first - normal * second)


SCALE2 = LOG2E * HEAD_DIM ** (-0.5)


def gelu_parts(hidden):
    square = hidden * hidden
    bent = jnp.tanh(0.7978845608 * hidden * (1.0 + 0.044715 * square))
    active = 0.5 * hidden * (1.0 + bent)
    slope = 0.5 * (1.0 + bent) + 0.5 * hidden * (1.0 - bent * bent) * (
        0.7978845608 * (1.0 + 3.0 * 0.044715 * square)
    )
    return active, slope


def group_device(core_flip, row_flip, col_flip):
    device = {}
    for name, flipped in zip(GROUP, (core_flip, row_flip, col_flip)):
        if flipped:
            device[name] = 1 - lax.axis_index(name)
    return device


def partners():
    return group_device(1, 0, 0), group_device(0, 1, 1), group_device(1, 1, 1)


def whole_group():
    return [group_device(i & 1, (i >> 1) & 1, i >> 2) for i in range(1, 8)]


def plane_neighbours():
    x, z = lax.axis_index("x"), lax.axis_index("z")
    around = ({"x": (x + 1) % 4}, {"x": (x + 3) % 4}, {"z": (z + 1) % 4}, {"z": (z + 3) % 4})
    return around, (x + 2 * z) % 4


class Quarters:
    def __init__(self, pieces, sems):
        self.sems, self.pieces, self.second = sems, pieces, []
        self.around, self.quarter = plane_neighbours()

    def cut(self, ref):
        size = ref.shape[0] // 4
        return ref.at[pl.ds(pl.multiple_of(self.quarter * size, 16), size), :]

    def fetch(self):
        self.first = [
            send(self.cut(source), self.cut(target), self.sems, 4 * at, device)
            for at, (source, target, device) in enumerate(self.pieces)
        ]

    def share(self, count=None):
        start = len(self.second) // 3
        stop = len(self.pieces) if count is None else min(start + count, len(self.pieces))
        for at in range(start, stop):
            self.first[at].wait_recv()
            here = self.cut(self.pieces[at][1])
            for spot in range(3):
                self.second.append(send(here, here, self.sems, 4 * at + 1 + spot, self.around[spot]))

    def arrive(self):
        for copy in self.second:
            copy.wait_recv()

    def close(self):
        for copy in self.first + self.second:
            copy.wait_send()


def image_spots():
    core, row, col = (lax.axis_index(name) for name in GROUP)
    flip = (col + core) % 2
    own = {"core": row, "row": flip, "col": col}
    other = {"core": row, "row": 1 - flip, "col": 1 - col}
    stays = jnp.logical_and(core == row, col == 0)
    return own, other, stays


def move(source, target, sems, at, device, stays):
    def remote():
        return pltpu.make_async_remote_copy(
            src_ref=source,
            dst_ref=target,
            send_sem=sems.at[0, at],
            recv_sem=sems.at[1, at],
            device_id=device,
            device_id_type=MESH,
        )

    @pl.when(jnp.logical_not(stays))
    def _():
        remote().start()

    @pl.when(stays)
    def _():
        pltpu.make_async_copy(source, target, sems.at[0, at]).start()

    def finish():
        @pl.when(jnp.logical_not(stays))
        def _():
            remote().wait()

        @pl.when(stays)
        def _():
            pltpu.make_async_copy(source, target, sems.at[0, at]).wait()

    return finish


class Home:
    def __init__(self, sems):
        core, row, col = (lax.axis_index(name) for name in GROUP)
        self.sems = sems
        self.sends = core == row
        self.stays = jnp.logical_and(self.sends, col == 0)
        self.leaves = jnp.logical_and(self.sends, col == 1)
        self.beside = {"core": (col + row) % 2, "col": 1 - col}
        self.waits = []

    def move(self, source, target, at):
        half = target.shape[1]

        def near():
            return self.copy(source.at[:, pl.ds(0, half)], target, 2 * at, at, group_device(1, 0, 0))

        def far():
            return self.copy(source.at[:, pl.ds(half, half)], target, 2 * at + 1, at, self.beside)

        def still():
            return pltpu.make_async_copy(source.at[:, pl.ds(0, half)], target, self.sems.at[0, 2 * at])

        pl.when(self.leaves)(lambda: near().start())
        pl.when(self.stays)(lambda: still().start())
        pl.when(self.sends)(lambda: far().start())

        def finish():
            pl.when(self.leaves)(lambda: near().wait_send())
            pl.when(self.stays)(lambda: still().wait())
            pl.when(self.sends)(lambda: far().wait_send())
            pl.when(jnp.logical_not(self.stays))(lambda: near().wait_recv())

        self.waits.append(finish)

    def copy(self, source, target, send_at, recv_at, device):
        return pltpu.make_async_remote_copy(
            src_ref=source,
            dst_ref=target,
            send_sem=self.sems.at[0, send_at],
            recv_sem=self.sems.at[1, recv_at],
            device_id=device,
            device_id_type=MESH,
        )

    def close(self):
        for finish in self.waits:
            finish()


def local(source, target, sems, at):
    copy = pltpu.make_async_copy(source, target, sems.at[0, at])
    copy.start()
    return copy


def greet(devices):
    barrier = pltpu.get_barrier_semaphore()
    for device in devices:
        pl.semaphore_signal(barrier, inc=1, device_id=device, device_id_type=MESH)


def meet(devices):
    pl.semaphore_wait(pltpu.get_barrier_semaphore(), len(devices))


def send(source, target, sems, at, device):
    copy = pltpu.make_async_remote_copy(
        src_ref=source,
        dst_ref=target,
        send_sem=sems.at[0, at],
        recv_sem=sems.at[1, at],
        device_id=device,
        device_id_type=MESH,
    )
    copy.start()
    return copy


class Totals:
    def __init__(self, chip, core_out, core_in, cross_out, cross_in, sems, partner, cross):
        self.refs = (chip, core_out, core_in, cross_out, cross_in)
        self.sems, self.partner, self.cross = sems, partner, cross
        self.copies = []

    def run(self, compute, ready):
        chip, core_out, core_in, cross_out, cross_in = self.refs
        rows = chip.shape[0]
        count = rows // STEP
        core_copies, cross_copies = [], []

        def pass_on(at):
            here = pl.ds(at * STEP, STEP)
            core_copies[at].wait_recv()
            total = chip[here, :] + core_in[here, :].astype(F32)
            chip[here, :] = total
            if cross_out is not None:
                cross_out[here, :] = total.astype(BF)
                cross_copies.append(
                    send(cross_out.at[here, :], cross_in.at[here, :], self.sems, count + at, self.cross)
                )

        for at in range(count):
            here = pl.ds(at * STEP, STEP)
            chip[here, :] = compute(at * STEP)
            if at > 0:
                pass_on(at - 1)
            ready(at * STEP)
            core_out[here, :] = compute(rows + at * STEP).astype(BF)
            core_copies.append(
                send(core_out.at[here, :], core_in.at[here, :], self.sems, at, self.partner)
            )
        pass_on(count - 1)
        self.cross_copies = cross_copies
        self.copies = core_copies + cross_copies

    def chunk(self, row):
        chip, _, _, _, cross_in = self.refs
        here = pl.ds(row, STEP)
        self.cross_copies[row // STEP].wait_recv()
        half = chip.shape[1] // 2
        other = cross_in[here, :].astype(F32)
        return chip[here, :] + jnp.concatenate((other[:, half:], other[:, :half]), axis=1)

    def close(self):
        for copy in self.copies:
            copy.wait_send()


def when_starting(copies):
    return lambda row: copies[row // STEP].wait_recv()


def spread(fill, whole, sems, partner):
    rows = whole.shape[0] // 2
    copies = []
    for at in range(rows // STEP):
        here = pl.ds(at * STEP, STEP)
        whole[here, :] = fill(at * STEP)
        if at == 0:
            yield None
        copies.append(
            send(whole.at[here, :], whole.at[pl.ds(rows + at * STEP, STEP), :], sems, at, partner)
        )
    yield copies


def fill_and_send(fill, whole, sems, devices):
    steps = spread(fill, whole, sems, devices[0])
    next(steps)
    meet(devices)
    return next(steps)


def arrive_kernel(
    token_ref, wq_load, wk_load, wv_load, one_gain, one_shift, two_gain, two_shift, bias_load,
    query_load, key_load, out_ref, w_qkv_ref, later_ref, vector_ref, gain_ref,
    landed, sems, share_sems,
):
    around, _ = plane_neighbours()
    devices = whole_group() + list(around)
    greet(devices)
    core = lax.axis_index("core")
    own, other, stays = image_spots()
    beside = group_device(0, 0, 1)
    half = token_ref.shape[1]
    meet(devices)
    finish = move(token_ref, landed.at[:, pl.ds(0, half)], sems, 0, own, stays)
    copies = [send(token_ref, landed.at[:, pl.ds(half, half)], sems, 1, other)]
    span = w_qkv_ref.shape[0] // 3

    def turned(ref, layer):
        whole = ref[layer].astype(F32).T
        return jnp.where(core == 0, whole[:span], whole[span:]).astype(BF)

    loads = (wq_load, wk_load, wv_load)
    for at, load in enumerate(loads):
        w_qkv_ref[pl.ds(at * span, span), 0:half] = turned(load(), 0)
    shared = Quarters(
        [(w_qkv_ref.at[:, pl.ds(0, half)], w_qkv_ref.at[:, pl.ds(half, half)], beside)], share_sems
    )
    shared.fetch()
    refs = [load() for load in (one_gain, one_shift, two_gain, two_shift, bias_load)]
    for layer in range(vector_ref.shape[0]):
        rows = [ref[layer : layer + 1, :] for ref in refs]
        vector_ref[layer, :, 0:half] = jnp.concatenate(rows + [jnp.zeros((3, half), F32)], axis=0)
    copies.append(
        send(vector_ref.at[:, :, pl.ds(0, half)], vector_ref.at[:, :, pl.ds(half, half)], sems, 2, beside)
    )
    for at, load in enumerate(loads):
        later_ref[pl.ds(at * span, span), :] = turned(load(), 1)
    rows = [load()[layer : layer + 1, :] for layer in range(2) for load in (query_load, key_load)]
    rows.append(jnp.zeros((128 - len(rows), HEAD_DIM), F32))
    square = jnp.concatenate((jnp.concatenate(rows, axis=0), jnp.zeros((128, 128 - HEAD_DIM), F32)), axis=1).T
    for layer in range(2):
        gain_ref[layer] = square[0:HEAD_DIM, 2 * layer : 2 * layer + 2]
    shared.share()
    finish()
    copies[0].wait()
    out_ref[...] = landed[...].astype(F32)
    copies[1].wait()
    shared.arrive()
    shared.close()


class Weights(Quarters):
    def __init__(self, pieces, kept, keep_sems, share_sems):
        self.kept = [local(source, target, keep_sems, at) for at, (source, target) in enumerate(kept)]
        super().__init__(pieces, share_sems)

    def arrive(self):
        super().arrive()
        for copy in self.kept:
            copy.wait()


def feed_weights(layer, raw_up, raw_down, w_up, w_down, keep_sems, share_sems):
    core, beside = lax.axis_index("core"), group_device(0, 0, 1)
    units, half = w_up.shape[1], w_up.shape[0] // 2
    here = pl.ds(pl.multiple_of(core * units, units), units)
    up, down = raw_up.at[layer, :, here], raw_down.at[layer, here, :]
    return Weights(
        [(up, w_up.at[pl.ds(half, half), :], beside), (down, w_down.at[:, pl.ds(half, half)], beside)],
        [(up, w_up.at[pl.ds(0, half), :]), (down, w_down.at[:, pl.ds(0, half)])],
        keep_sems,
        share_sems,
    )


def out_weights(layer, raw_out, w_out, keep_sems, share_sems):
    core = lax.axis_index("core")
    half, span = w_out.shape[1] // 2, w_out.shape[0] // 4
    beside, cross, across = group_device(0, 0, 1), group_device(0, 1, 1), group_device(0, 1, 0)
    pieces, kept = [], []
    for at in range(2):
        source = raw_out.at[layer, pl.ds((core + at - 2 * at * core) * span, span), :]
        for device, row, col in ((beside, 0, half), (cross, half, half), (across, half, 0)):
            pieces.append((source, w_out.at[pl.ds(row + at * span, span), pl.ds(col, half)], device))
        kept.append((source, w_out.at[pl.ds(at * span, span), pl.ds(0, half)]))
    return Weights(pieces, kept, keep_sems, share_sems)


def attend_forward_kernel(layer, flush, resid_load, w_qkv_load, gain_load, vector_load, raw_out_ref, *refs):
    if layer == 0:
        raw_up_ref, raw_down_ref, *refs = refs
    out_ref, seen_ref, qkv_ref, mixed_ref, total_ref, w_out_ref, *refs = refs
    if layer == 0:
        w_up_ref, w_down_ref, *refs = refs
    joined, seen_sems, head_sems, keep_sems, share_sems, *feed_sems = refs
    near, cross, far = partners()
    devices = (near, cross, far, group_device(0, 0, 1), group_device(0, 1, 0)) + plane_neighbours()[0]
    greet(devices)
    resid_ref, vector_ref = resid_load(), vector_load().at[layer]
    rows = resid_ref.shape[0]
    heads = mixed_ref.shape[0] // HEAD_DIM
    span = heads * HEAD_DIM

    def fill(row):
        normal, _ = norm(resid_ref[pl.ds(row, STEP), :])
        return (normal * vector_ref[0:1, :] + vector_ref[1:2, :]).astype(BF)

    copies = fill_and_send(fill, seen_ref, seen_sems, devices)
    fetched = []
    if layer == 0:
        fetched.append(feed_weights(layer, raw_up_ref, raw_down_ref, w_up_ref, w_down_ref, *feed_sems))
    fetched.append(out_weights(layer, raw_out_ref, w_out_ref, keep_sems, share_sems))
    for shared in fetched:
        shared.fetch()
    w_qkv_ref = w_qkv_load()
    for at in range(2 * rows // ROWS):
        if at * ROWS >= rows:
            for part in range(ROWS // STEP):
                copies[(at * ROWS - rows) // STEP + part].wait_recv()
        here = pl.ds(at * ROWS, ROWS)
        qkv_ref[:, here] = dot(w_qkv_ref[...], seen_ref[here, :], 1, 1)
    flush(seen_ref, qkv_ref)
    gains = gain_load()[layer]
    for head in range(heads):
        if layer == 0 and head == 1:
            fetched[0].share(1)
        if head == 2:
            for shared in fetched:
                shared.share()
        own = pl.ds(head * HEAD_DIM, HEAD_DIM)
        query = (head_norm(qkv_ref[own, :])[0] * gains[:, 0:1]).astype(BF)
        key = head_norm(qkv_ref[pl.ds(span + head * HEAD_DIM, HEAD_DIM), :])[0] * gains[:, 1:2]
        key_rows = key.T.astype(BF)
        value = qkv_ref[pl.ds(2 * span + head * HEAD_DIM, HEAD_DIM), :].astype(BF)
        for at in range(0, 2 * rows, BLOCK):
            expo = jnp.exp2(dot(key_rows, query[:, at : at + BLOCK]) * SCALE2)
            total = jnp.sum(expo, axis=0, keepdims=True)
            mixed = (dot(value, expo.astype(BF)) * (1.0 / total)).astype(BF)
            mixed_ref[own, at : at + BLOCK] = mixed
            if at < rows:
                joined[own, at : at + BLOCK] = mixed
            total_ref[head : head + 1, at : at + BLOCK] = jnp.log2(total)
        mine, others = pl.ds(0, rows), pl.ds(rows, rows)
        for spot, (device, columns) in enumerate(((near, others), (cross, mine), (far, others))):
            copies.append(
                send(
                    mixed_ref.at[own, columns],
                    joined.at[pl.ds((spot + 1) * span + head * HEAD_DIM, HEAD_DIM), :],
                    head_sems,
                    head * 3 + spot,
                    device,
                )
            )
    flush(mixed_ref, total_ref)
    fetched[-1].arrive()
    flush(w_out_ref)
    for copy in copies[-3 * heads :]:
        copy.wait_recv()
    for at in range(rows // ROWS):
        here = pl.ds(at * ROWS, ROWS)
        out_ref[here, :] = resid_ref[here, :] + dot(joined[:, here], w_out_ref[...], 0, 0)
    if layer == 0:
        fetched[0].arrive()
    for copy in copies:
        copy.wait_send()
    for shared in fetched:
        shared.close()


def feed_forward_kernel(
    layer, last, flush, resid_load, w_up_load, bias_load, w_down_load, vector_load, side_ref, *refs
):
    if last:
        out_ref, seen_ref, active_ref, slope_ref, side_out, low_ref = refs[:6]
        chip, core_out, core_in, landed, seen_sems, total_sems, side_sems = refs[6:]
        cross_out, cross_in = None, None
    else:
        raw_up_ref, raw_down_ref, *refs = refs
        out_ref, seen_ref, active_ref, slope_ref, side_out, next_up_ref, next_down_ref = refs[:7]
        chip, core_out, core_in, cross_out, cross_in = refs[7:12]
        seen_sems, total_sems, side_sems, keep_sems, share_sems = refs[12:]
    near, cross, _ = partners()
    beside = group_device(0, 0, 1)
    devices = whole_group() if last else (near, cross, beside) + plane_neighbours()[0]
    greet(devices)
    core = lax.axis_index("core")
    resid_ref, vector_ref = resid_load(), vector_load().at[layer]
    half = resid_ref.shape[1] // 2

    def fill(row):
        normal, _ = norm(resid_ref[pl.ds(row, STEP), :])
        return (normal * vector_ref[2:3, :] + vector_ref[3:4, :]).astype(BF)

    if last:
        steps = spread(fill, seen_ref, seen_sems, near)
        next(steps)
        meet(devices)
        copies = next(steps)
        own, other, stays = image_spots()
        arrived = move(side_ref, landed.at[:, pl.ds(0, half)], side_sems, 0, own, stays)
        side = send(side_ref, landed.at[:, pl.ds(half, half)], side_sems, 1, other)
    else:
        copies = fill_and_send(fill, seen_ref, seen_sems, devices)
        kept = local(side_ref, side_out.at[:, pl.ds(0, half)], side_sems, 0)
        side = send(side_ref, side_out.at[:, pl.ds(half, half)], side_sems, 1, beside)
        shared = feed_weights(
            layer + 1, raw_up_ref, raw_down_ref, next_up_ref, next_down_ref, keep_sems, share_sems
        )
        shared.fetch()

    w_up_ref, w_down_ref, bias_ref = w_up_load(), w_down_load(), bias_load()
    units = w_up_ref.shape[1]
    bias = bias_ref[layer : layer + 1, pl.ds(pl.multiple_of(core * units, units), units)]

    def compute(row):
        here = pl.ds(row, STEP)
        hidden = dot(seen_ref[here, :], w_up_ref[...]) + bias
        active, slope = gelu_parts(hidden)
        active = active.astype(BF)
        active_ref[here, :] = active
        slope_ref[here, :] = slope.astype(BF)
        return dot(active, w_down_ref[...])

    totals = Totals(chip, core_out, core_in, cross_out, cross_in, total_sems, near, cross)
    totals.run(compute, when_starting(copies))
    flush(seen_ref, active_ref, slope_ref)
    if not last:
        shared.share()
    for row in range(0, resid_ref.shape[0], STEP):
        here = pl.ds(row, STEP)
        total = chip[here, :] if last else totals.chunk(row)
        out_ref[here, :] = resid_ref[here, :] + (total + vector_ref[4:5, :])
        if last:
            low_ref[here, :] = total.astype(BF)
    for copy in copies:
        copy.wait_send()
    totals.close()
    side.wait()
    if last:
        arrived()
        side_out[...] = landed[...].astype(F32)
    else:
        kept.wait()
        shared.arrive()
        shared.close()


def feed_backward_kernel(plan, flush, *refs):
    refs = iter(refs)

    def take(count):
        return [next(refs) for _ in range(count)]

    grad_load, resid_load, seen_load, active_load, slope_load, w_up_load, w_down_load, vector_load = take(8)
    parts = take(plan["parts"])
    out_ref, up_ref, down_ref, small_ref = take(4)
    if parts:
        (shard_ref,) = take(1)
    branch, hidden, chip, core_out, core_in, cross_out, cross_in, seen_sems, total_sems = take(9)
    near, cross, _ = partners()
    devices = (near, cross)
    steps = iter(())
    if parts:
        (load_sems,) = take(1)
        beside = take_scatter(ATTEND_SMALL_CHUNKS, refs)
        steps = loaded_scatter(ATTEND_SMALL_CHUNKS, parts, plan["copies"], load_sems, *beside)
        devices += tuple(device for device, _ in link_bits().values())
    greet(devices)
    next(steps, None)
    grad_ref = grad_load()
    width = grad_ref.shape[1]
    copies = fill_and_send(
        lambda row: grad_ref[pl.ds(row, STEP), :].astype(BF), branch, seen_sems, devices
    )
    next(steps, None)
    w_down_ref, slope_ref, w_up_ref = w_down_load(), slope_load(), w_up_load()

    def compute(row):
        here = pl.ds(row, STEP)
        active_grad = dot(branch[here, :], w_down_ref[...], 1, 1)
        low = (active_grad * slope_ref[here, :].astype(F32)).astype(BF)
        hidden[here, :] = low
        return dot(low, w_up_ref[...], 1, 1)

    totals = Totals(chip, core_out, core_in, cross_out, cross_in, total_sems, near, cross)
    totals.run(compute, when_starting(copies))
    next(steps, None)
    rows = grad_ref.shape[0]
    active_ref, seen_ref, resid_ref = active_load(), seen_load(), resid_load()
    vector_ref = vector_load().at[0 if parts else 1]
    half = width // 2
    for at in range(0, width, ROWS):
        down_ref[at : at + ROWS, :] = dot(active_ref[:, at : at + ROWS], branch[...], 0, 0).astype(BF)
        up_ref[at : at + ROWS, :] = dot(seen_ref[:, at : at + ROWS], hidden[...], 0, 0).astype(BF)
    flush(up_ref, down_ref)
    next(steps, None)
    bias_down = jnp.sum(branch[0:rows, :].astype(F32), axis=0, keepdims=True)
    bias_up = jnp.sum(hidden[...].astype(F32), axis=0, keepdims=True)
    gain_sum = jnp.zeros((1, width), F32)
    shift_sum = jnp.zeros((1, width), F32)
    for row in range(0, rows, STEP):
        here = pl.ds(row, STEP)
        grad = totals.chunk(row)
        normal, factor = norm(resid_ref[here, :])
        gain_sum = gain_sum + jnp.sum(grad * normal, axis=0, keepdims=True)
        shift_sum = shift_sum + jnp.sum(grad, axis=0, keepdims=True)
        out_ref[here, :] = grad_ref[here, :] + norm_back(grad, normal, factor, vector_ref[2:3, :])
        if row in (0, 2 * STEP):
            next(steps, None)
    height = small_ref.shape[0]
    small_ref[...] = jnp.concatenate(
        [gain_sum, shift_sum, bias_down]
        + [jnp.concatenate((bias_up[:, i * half : (i + 1) * half],) * 2, axis=1) for i in range(2)]
        + [jnp.zeros((height - 5, width), F32)],
        axis=0,
    ).astype(small_ref.dtype)
    for _ in steps:
        pass
    if parts:
        keep_shards(beside[1], shard_ref)
    for copy in copies:
        copy.wait_send()
    totals.close()


def attend_backward_kernel(plan, flush, *refs):
    refs = iter(refs)

    def take(count):
        return [next(refs) for _ in range(count)]

    last = plan["last"]
    grad_load, resid_load, seen_load, qkv_load, mixed_load, total_load = take(6)
    w_qkv_load, w_out_load, gain_load, vector_load = take(4)
    parts = take(2)
    if last:
        shard_load, other_shard_load, vec_load, final_load, low_ref = take(5)
        result_ref, token_in, layer_both, feed_both, tail_both, vec_pair = take(6)
    else:
        out_ref, grad_qkv_ref, grad_out_ref, small_ref, shard_ref = take(5)
    proj, mixed_grad, qkv_grad, gains_own, gains_in = take(5)
    chip, core_out, core_in, cross_out, cross_in, seen_sems, total_sems, gain_sems = take(8)
    (load_sems,) = take(1)
    feed_beside = take_scatter(FEED_CHUNKS, refs)
    feed_steps = loaded_scatter(FEED_CHUNKS, parts, plan["copies"], load_sems, *feed_beside)
    links = link_bits()
    near, cross, _ = partners()
    devices = (near, cross) + tuple(device for device, _ in links.values())
    if last:
        low_in, result_low, token_low, home_sems = take(4)
        vec, vec_x, vec_z, vec_mid, vec_col, vec_sems = take(6)
        tail_work, tail_landing, tail_sems = take_scatter(ATTEND_CHUNKS, refs)
        layer_gather = take(2)
        feed_gather = take(2)
        tail_gather = take(2)
        x, z = lax.axis_index("x"), lax.axis_index("z")
        devices = tuple(whole_group()) + tuple(links[name][0] for name in ("x1", "x2", "z1", "z2"))
        devices += ({"x": (x + 2) % 4}, {"z": (z + 2) % 4})
    greet(devices)
    next(feed_steps)
    grad_ref = grad_load()
    rows, width = grad_ref.shape
    half = width // 2
    copies = fill_and_send(
        lambda row: grad_ref[pl.ds(row, STEP), :].astype(BF), proj, seen_sems, devices
    )
    next(feed_steps)
    if last:
        home = Home(home_sems)

        def low_copy():
            return home.copy(low_ref, low_in, 11, 11, cross)

        pl.when(jnp.logical_not(home.sends))(lambda: low_copy().start())
        shards = [shard_load().at[pl.ds(16 * at, 16), :] for at in range(len(FEED_CHUNKS))]
        shards += [other_shard_load().at[pl.ds(16 * at, 16), :] for at in range(len(ATTEND_SMALL_CHUNKS))]
        layer_steps = gather(LAYER_CHUNKS, shards, layer_both, *layer_gather)
        next(layer_steps)
    w_out_ref = w_out_load()
    span = mixed_grad.shape[0]
    for at in range(2 * rows // ROWS):
        if at * ROWS >= rows:
            for part in range(ROWS // STEP):
                copies[(at * ROWS - rows) // STEP + part].wait_recv()
        here = pl.ds(at * ROWS, ROWS)
        mixed_grad[:, here] = dot(w_out_ref[pl.ds(0, span), :], proj[here, :], 1, 1).astype(BF)
    gains, qkv_ref, total_ref = gain_load()[0 if last else 1], qkv_load(), total_load()
    scale = HEAD_DIM ** (-0.5)
    gains_sum = jnp.zeros((HEAD_DIM, 2), F32)
    slot = 0
    for head in range(span // HEAD_DIM):
        own = pl.ds(head * HEAD_DIM, HEAD_DIM)
        key_at = pl.ds(span + head * HEAD_DIM, HEAD_DIM)
        value_at = pl.ds(2 * span + head * HEAD_DIM, HEAD_DIM)
        query_normal, query_factor = head_norm(qkv_ref[own, :])
        key_normal, key_factor = head_norm(qkv_ref[key_at, :])
        query = (query_normal * gains[:, 0:1]).astype(BF)
        key_full = key_normal * gains[:, 1:2]
        key = key_full.astype(BF)
        key_rows = key_full.T.astype(BF)
        value_rows = qkv_ref[value_at, :].T.astype(BF)
        key_sum = jnp.zeros(key.shape, F32)
        value_sum = jnp.zeros(key.shape, F32)
        query_parts = []
        for at in range(0, 2 * rows, BLOCK):
            grad = mixed_grad[own, at : at + BLOCK]
            logits = dot(key_rows, query[:, at : at + BLOCK]) * SCALE2
            probs = jnp.exp2(logits - total_ref[head : head + 1, at : at + BLOCK])
            pulled = dot(value_rows, grad)
            delta = jnp.sum(probs * pulled, axis=0, keepdims=True)
            score_grad = (probs * (pulled - delta)).astype(BF)
            query_parts.append(dot(key, score_grad))
            key_sum = key_sum + dot(query[:, at : at + BLOCK], score_grad, 1, 1)
            value_sum = value_sum + dot(grad, probs.astype(BF), 1, 1)
            slot += 1
            if last and slot in (5, 10):
                next(layer_steps, None)
            if slot == (12 if last else 9):
                next(feed_steps)
        query_sum = jnp.concatenate(query_parts, axis=1) * scale
        key_sum = key_sum * scale
        qkv_grad[own, :] = head_norm_back(query_sum, query_normal, query_factor, gains[:, 0:1]).astype(BF)
        qkv_grad[key_at, :] = head_norm_back(key_sum, key_normal, key_factor, gains[:, 1:2]).astype(BF)
        qkv_grad[value_at, :] = value_sum.astype(BF)
        gains_sum = gains_sum + jnp.concatenate(
            (
                jnp.sum(query_sum * query_normal, axis=1, keepdims=True),
                jnp.sum(key_sum * key_normal, axis=1, keepdims=True),
            ),
            axis=1,
        )
    square = jnp.concatenate((gains_sum, jnp.zeros((HEAD_DIM, 126), F32)), axis=1)
    gains_own[...] = jnp.concatenate((square, jnp.zeros((128 - HEAD_DIM, 128), F32)), axis=0).T[0:8]
    gains_copy = send(gains_own, gains_in, gain_sems, 0, cross)
    w_qkv_ref = w_qkv_load()

    def compute(row):
        return dot(qkv_grad[:, pl.ds(row, STEP)], w_qkv_ref[...], 0, 0)

    totals = Totals(chip, core_out, core_in, cross_out, cross_in, total_sems, near, cross)
    seen_ref, mixed_ref, resid_ref = seen_load(), mixed_load(), resid_load()
    vector_ref = vector_load().at[0 if last else 1]
    if last:
        grad_qkv_ref, grad_out_ref = tail_work.at[pl.ds(0, 3 * span), :], tail_work.at[pl.ds(3 * span, span), :]

    def weight_grads():
        for at in range(0, 3 * span, span):
            here = pl.ds(at, span)
            grad_qkv_ref[here, :] = dot(qkv_grad[here, :], seen_ref[...]).astype(BF)
        grad_out_ref[...] = dot(mixed_ref[...], proj[...]).astype(BF)

    sums = [jnp.zeros((1, width), F32), jnp.zeros((1, width), F32)]

    def final_chunk(row):
        here = pl.ds(row, STEP)
        grad = totals.chunk(row)
        normal, factor = norm(resid_ref[here, :])
        sums[0] = sums[0] + jnp.sum(grad * normal, axis=0, keepdims=True)
        sums[1] = sums[1] + jnp.sum(grad, axis=0, keepdims=True)
        return grad_ref[here, :] + norm_back(grad, normal, factor, vector_ref[0:1, :])

    def small_rows(height):
        gains_copy.wait()
        shared = gains_own[0:2, :] + gains_in[0:2, :]
        blank = jnp.zeros((2, half - 128), F32)
        return jnp.concatenate(
            sums
            + [jnp.concatenate((shared, blank, shared, blank), axis=1), jnp.zeros((height - 4, width), F32)],
            axis=0,
        )

    if not last:
        totals.run(compute, lambda row: next(feed_steps) if row == 3 * STEP else None)
        weight_grads()
        flush(grad_qkv_ref, grad_out_ref)
        next(feed_steps)
        for row in range(0, rows, STEP):
            out_ref[pl.ds(row, STEP), :] = final_chunk(row)
            if row == STEP:
                next(feed_steps)
        small_ref[...] = small_rows(16).astype(BF)
        for _ in feed_steps:
            pass
        keep_shards(feed_beside[1], shard_ref)
        for copy in copies:
            copy.wait_send()
        totals.close()
        return

    def whole(first, second):
        yield from first
        yield from second

    weight_grads()
    tail = whole(
        scatter(ATTEND_CHUNKS, tail_work, tail_landing, tail_sems),
        gather(ATTEND_CHUNKS, tail_landing[4::5], tail_both, *tail_gather),
    )
    next(tail)
    feed = whole(feed_steps, gather(FEED_CHUNKS, feed_beside[1][4::5], feed_both, *feed_gather))
    totals.run(compute, lambda row: None)
    next(feed)
    next(layer_steps)
    final_ref = final_load()

    @pl.when(home.sends)
    def _():
        low_copy().wait_recv()
        other = low_in[...].astype(F32)
        other = jnp.concatenate((other[:, half:], other[:, :half]), axis=1)
        result_low[...] = (final_ref[...] + other).astype(BF)

    pl.when(jnp.logical_not(home.sends))(lambda: low_copy().wait_send())
    home.move(result_low, result_ref, 0)

    def token_chunk(row):
        here = pl.ds(row, STEP)
        token_low[here, :] = final_chunk(row).astype(BF)
        home.move(token_low.at[here, :], token_in.at[here, :], 1 + row // STEP)

    next(tail)
    token_chunk(0)
    next(feed)
    token_chunk(STEP)
    next(layer_steps)
    next(tail)
    next(feed)
    next(tail)
    token_chunk(2 * STEP)
    for _ in layer_steps:
        pass
    flush(layer_both)
    next(feed)
    next(tail)
    next(feed)
    token_chunk(3 * STEP)
    vec[...] = jnp.concatenate((small_rows(8), vec_load()[...]), axis=0)
    vec_copies = []

    def share(source, landing, axis, place, at):
        batch = []
        for step in range(1, 4):
            batch.append(
                send(source, landing.at[step - 1], vec_sems, at + step - 1, {axis: (place + step) % 4})
            )
        vec_copies.extend(batch)
        return batch

    def collect(source, landing, batch):
        for copy in batch:
            copy.wait_recv()
        return (source[...] + landing[0]) + (landing[1] + landing[2])

    batch = share(vec, vec_x, "x", x, 0)
    next(tail)
    next(feed)
    vec_mid[0] = collect(vec, vec_x, batch)
    batch = share(vec_mid.at[0], vec_z, "z", z, 3)
    next(tail)
    next(feed)
    vec_mid[1] = collect(vec_mid.at[0], vec_z, batch)
    vec_copies.append(send(vec_mid.at[1, :, pl.ds(half, half)], vec_col, vec_sems, 6, links["col"][0]))
    next(tail)
    vec_copies[-1].wait_recv()
    core = lax.axis_index("core")
    vec_pair[core] = vec_mid[1, :, 0:half] + vec_col[...]
    vec_copies.append(send(vec_pair.at[core], vec_pair.at[core], vec_sems, 7, near))
    next(tail)
    vec_copies[-1].wait_recv()
    for _ in feed:
        pass
    flush(feed_both)
    for _ in tail:
        pass
    home.close()
    for copy in copies + vec_copies:
        copy.wait_send()
    totals.close()


class Load:
    def __init__(self, source, target, sem):
        self.copy = pltpu.make_async_copy(source, target, sem)
        self.copy.start()
        self.target, self.waited = target, False

    def __call__(self):
        if not self.waited:
            self.copy.wait()
            self.waited = True
        return self.target


def call(kernel, name, collective_id, inputs, outs, scratch):
    vmem = pl.BlockSpec(memory_space=pltpu.VMEM)
    hbm = pl.BlockSpec(memory_space=pl.ANY)

    def kind(spec):
        return spec[0] if isinstance(spec, tuple) and isinstance(spec[0], str) else "block"

    def bare(spec):
        return spec if kind(spec) == "block" else spec[1]

    kinds = [kind(spec) for spec in inputs]
    values = [bare(spec) for spec in inputs]
    loaded = [at for at, k in enumerate(kinds) if k == "load"]
    early = [at for at, spec in enumerate(outs) if kind(spec) == "early"]

    def body(*refs):
        refs = list(refs)
        given, refs = refs[: len(inputs)], refs[len(inputs) :]
        made, refs = refs[: len(outs)], refs[len(outs) :]
        own, refs = refs[: len(scratch)], refs[len(scratch) :]
        staged, refs = refs[: len(loaded)], refs[len(loaded) :]
        kept, (sems, out_sems) = refs[: len(early)], refs[len(early) :]
        loads = [Load(given[at], staged[i], sems.at[i]) for i, at in enumerate(loaded)]
        for at, load in zip(loaded, loads):
            given[at] = load
        copies = {}

        def flush(*flushed):
            for ref in flushed:
                i = next(i for i, one in enumerate(kept) if one is ref)
                copies[i] = pltpu.make_async_copy(ref, made[early[i]], out_sems.at[i])
                copies[i].start()

        results = list(made)
        for i, at in enumerate(early):
            results[at] = kept[i]
        if early:
            kernel(flush, *given, *results, *own)
        else:
            kernel(*given, *results, *own)
        flush(*(ref for i, ref in enumerate(kept) if i not in copies))
        for i in sorted(copies):
            copies[i].wait()
        for load in loads:
            load()

    return pl.pallas_call(
        body,
        in_specs=[vmem if k == "block" else hbm for k in kinds],
        out_specs=[vmem if kind(spec) == "block" else hbm for spec in outs],
        out_shape=[jax.ShapeDtypeStruct(*bare(spec)) for spec in outs],
        scratch_shapes=scratch
        + [pltpu.VMEM(values[at].shape, values[at].dtype) for at in loaded]
        + [pltpu.VMEM(*bare(outs[at])) for at in early]
        + [pltpu.SemaphoreType.DMA((max(1, len(loaded)),)), pltpu.SemaphoreType.DMA((max(1, len(early)),))],
        compiler_params=pltpu.CompilerParams(
            collective_id=collective_id,
            has_side_effects=collective_id is not None,
            vmem_limit_bytes=58 * 2**20,
        ),
        name=name,
    )(*values)


def pair_sems(count):
    return pltpu.SemaphoreType.DMA((2, count))


def total_scratch(rows, width):
    return [pltpu.VMEM((rows, width), F32)] + [pltpu.VMEM((rows, width), BF)] * 4


def total_sems(rows):
    return [pair_sems(rows // STEP), pair_sems(2 * rows // STEP)]


def arrive(tokens, w_query, w_key, w_value, vectors):
    rows, half = tokens.shape
    span = w_query.shape[2] // 2
    layers = w_query.shape[0]
    return call(
        arrive_kernel,
        "arrive",
        10,
        [("hbm", tokens)] + [("load", value) for value in (w_query, w_key, w_value) + vectors],
        [
            ((rows, 2 * half), F32),
            ((3 * span, 2 * half), BF),
            ((3 * span, half), BF),
            ((layers, 8, 2 * half), F32),
            ((layers, HEAD_DIM, 2), F32),
        ],
        [pltpu.VMEM((rows, 2 * half), BF), pair_sems(3), pair_sems(4)],
    )


def attend_forward(layer, resid, w_qkv, gains, vectors, raws):
    rows, width = resid.shape
    span = w_qkv.shape[0] // 3
    units = raws[1].shape[2] // 2
    outs = [
        ((rows, width), F32),
        ((2 * rows, width), BF),
        ((3 * span, 2 * rows), F32),
        ((span, 2 * rows), BF),
        ((span // HEAD_DIM, 2 * rows), F32),
        ((width, width), BF),
    ]
    scratch = [pltpu.VMEM((4 * span, rows), BF), pair_sems(rows // STEP), pair_sems(3 * span // HEAD_DIM)]
    scratch += [pair_sems(2), pair_sems(24)]
    if layer == 0:
        outs += [((width, units), BF), ((units, width), BF)]
        scratch += [pair_sems(2), pair_sems(8)]
    return call(
        functools.partial(attend_forward_kernel, layer),
        "attend_forward_%d" % layer,
        8 + layer,
        [("load", value) for value in (resid, w_qkv, gains, vectors)]
        + [("hbm", value) for value in (raws if layer == 0 else raws[:1])],
        [("early", out) for out in outs],
        scratch,
    )


def feed_forward(layer, last, resid, w_up, up_bias, w_down, vectors, side, raws):
    rows, width = resid.shape
    units = w_up.shape[1]
    outs = [((rows, width), F32), ((2 * rows, width), BF)] + [((2 * rows, units), BF)] * 2
    low = pltpu.VMEM((rows, width), BF)
    if last:
        outs += [((rows, width), F32), ((rows, width), BF)]
        scratch = [pltpu.VMEM((rows, width), F32), low, low, low]
    else:
        outs += [((side.shape[0], width), BF), ((width, units), BF), ((units, width), BF)]
        scratch = total_scratch(rows, width)
    scratch += total_sems(rows) + [pair_sems(2)]
    return call(
        functools.partial(feed_forward_kernel, layer, last),
        "feed_forward_%d" % layer,
        4 if last else 3,
        [("load", value) for value in (resid, w_up, up_bias, w_down, vectors)]
        + [("hbm", value) for value in (side,) + (() if last else raws[1:])],
        [("early", out) for out in outs],
        scratch if last else scratch + [pair_sems(2), pair_sems(8)],
    )


def feed_backward(operands, parts):
    grad, resid, seen, active, slope, w_up, w_down, vectors = operands
    rows, width = grad.shape
    units = w_up.shape[1]
    outs = [((rows, width), F32), ((width, units), BF), ((units, width), BF)]
    outs += [((8, width), F32) if parts else ((16, width), BF)]
    scratch = [pltpu.VMEM((2 * rows, width), BF), pltpu.VMEM((2 * rows, units), BF)]
    scratch += total_scratch(rows, width) + total_sems(rows)
    copies = []
    if parts:
        outs.append(((16 * len(ATTEND_SMALL_CHUNKS), width // 2), BF))
        scratch += [pltpu.SemaphoreType.DMA((len(parts),))] + scatter_scratch(ATTEND_SMALL_CHUNKS, width)
        row = 0
        for at, part in enumerate(parts):
            copies.append((at, (0, part.shape[0]), (0, width), row, 0))
            row += part.shape[0]
    return call(
        functools.partial(feed_backward_kernel, {"parts": len(parts), "copies": copies}),
        "feed_backward_and_sum" if parts else "feed_backward",
        7 if parts else 5,
        [("load", value) for value in operands] + [("hbm", value) for value in parts],
        [("early", out) for out in outs],
        scratch,
    )


def link_bits():
    x, z = lax.axis_index("x"), lax.axis_index("z")
    col = lax.axis_index("col")
    return {
        "x1": ({"x": x + 1 - 2 * (x % 2)}, ((x + 1) // 2) % 2),
        "x2": ({"x": 3 - x}, x // 2),
        "z1": ({"z": z + 1 - 2 * (z % 2)}, ((z + 1) // 2) % 2),
        "z2": ({"z": 3 - z}, z // 2),
        "col": ({"col": 1 - col}, None),
    }


ORDERS = (
    ("x1", "z1", "x2", "z2", "col"),
    ("z1", "x2", "z2", "col", "x1"),
    ("x2", "z2", "col", "x1", "z1"),
    ("z2", "col", "x1", "z1", "x2"),
    ("col", "x1", "z1", "x2", "z2"),
    ("x1", "z1", "x2", "z2", "col"),
    ("z1", "x2", "z2", "col", "x1"),
    ("x2", "z2", "col", "x1", "z1"),
    ("z2", "col", "x1", "z1", "x2"),
    ("col", "x2", "z2", "x1", "z1"),
)
UNIT = 256


def plan_chunks(rows, orders):
    return [(at * UNIT, UNIT, ORDERS[orders[at]]) for at in range(rows // UNIT)]


def step_shapes(rows, order, width):
    shapes = []
    for link in order:
        if link == "col":
            width //= 2
        else:
            rows //= 2
        shapes.append((rows, width))
    return shapes


def add_into(target, other, row, col_size):
    rows = target.shape[0]
    block = min(rows, 64)

    @pl.loop(0, rows // block)
    def _(at):
        here = pl.ds(pl.multiple_of(at * block, block), block)
        there = pl.ds(pl.multiple_of(row + at * block, 16), block)
        target[here, :] = (
            target[here, :].astype(F32) + other[there, :col_size].astype(F32)
        ).astype(BF)


def scatter(chunks, work, landing, sems):
    links = link_bits()
    state = [work.at[pl.ds(start, rows), :] for start, rows, _ in chunks]
    flight = [None] * len(chunks)
    sent = []

    def land(at, step):
        copy, keep_row, width = flight[at]
        copy.wait_recv()
        target = landing[at * 5 + step]
        add_into(target, state[at], keep_row, width)
        state[at] = target

    for step in range(5):
        for at, (start, rows, order) in enumerate(chunks):
            if step > 0:
                land(at, step - 1)
            device, bit = links[order[step]]
            landed = landing[at * 5 + step]
            size, width = landed.shape
            if bit is None:
                source = state[at].at[:, pl.ds(width, width)]
                keep_row = 0
            else:
                keep_row = bit * size
                source = state[at].at[pl.ds(pl.multiple_of((1 - bit) * size, size), size), :]
            copy = send(source, landed, sems, at * 5 + step, device)
            sent.append(copy)
            flight[at] = (copy, keep_row, width)
        yield
    for at in range(len(chunks)):
        land(at, 4)
    for copy in sent:
        copy.wait_send()


def gather(chunks, shards, both, sems, core_sems):
    core = lax.axis_index("core")
    links = link_bits()
    sent, region = [], []
    for at, (start, rows, order) in enumerate(chunks):
        offset, size = 0, rows
        for link in order:
            if links[link][1] is not None:
                size //= 2
                offset = offset + links[link][1] * size
        both[core, pl.ds(pl.multiple_of(start + offset, 16), size), :] = shards[at][...]
        region.append((start + offset, size))
    back = [[link for link in reversed(order) if link != "col"] for _, _, order in chunks]
    waiting = [None] * len(chunks)

    def settle(at):
        copy, bit, size = waiting[at]
        copy.wait_recv()
        lo, _ = region[at]
        region[at] = (lo - bit * size, 2 * size)

    for step in range(4):
        for at in range(len(chunks)):
            if step > 0:
                settle(at)
            lo, size = region[at]
            device, bit = links[back[at][step]]
            here = both.at[core, pl.ds(pl.multiple_of(lo, 16), size), :]
            copy = send(here, here, sems, at * 4 + step, device)
            sent.append(copy)
            waiting[at] = (copy, bit, size)
        yield
    last = []
    for at, (start, rows, order) in enumerate(chunks):
        settle(at)
        here = both.at[core, pl.ds(start, rows), :]
        last.append(send(here, here, core_sems, at, {"core": 1 - core}))
    yield
    for copy in last:
        copy.wait_recv()
    for copy in sent + last:
        copy.wait_send()


def scatter_scratch(chunks, width):
    shapes = [(sum(size for _, size, _ in chunks), width)]
    shapes += [shape for _, size, order in chunks for shape in step_shapes(size, order, width)]
    return [pltpu.VMEM(shape, BF) for shape in shapes] + [pair_sems(5 * len(chunks))]


def take_scatter(chunks, refs):
    return next(refs), [next(refs) for _ in range(5 * len(chunks))], next(refs)


def gather_scratch(chunks):
    return [pair_sems(4 * len(chunks)), pair_sems(len(chunks))]


def loaded_scatter(chunks, parts, copies, load_sems, work, landing, sems):
    loads = []
    for at, (source, rows, cols, row, col) in enumerate(copies):
        load = pltpu.make_async_copy(
            parts[source].at[pl.ds(rows[0], rows[1]), pl.ds(cols[0], cols[1])],
            work.at[pl.ds(row, rows[1]), pl.ds(col, cols[1])],
            load_sems.at[at],
        )
        load.start()
        loads.append(load)
    yield
    for load in loads:
        load.wait()
    yield from scatter(chunks, work, landing, sems)


def keep_shards(landing, shard_ref):
    for at, landed in enumerate(landing[4::5]):
        shard_ref[pl.ds(at * 16, 16), :] = landed[...]


FEED_CHUNKS = plan_chunks(6 * UNIT, (0, 1, 2, 3, 4, 9))
ATTEND_CHUNKS = plan_chunks(3 * UNIT, (0, 1, 2))
ATTEND_SMALL_CHUNKS = plan_chunks(4 * UNIT, (0, 1, 2, 3))
LAYER_CHUNKS = FEED_CHUNKS + [(start + 6 * UNIT, rows, order) for start, rows, order in ATTEND_SMALL_CHUNKS]


def feed_copies(first, base, units, width):
    half = width // 2
    copies = []
    for i in range(2):
        for j in range(2):
            copies.append((first, (i * half, half), (j * half, half), base + j * half, i * half))
    copies.append((first + 1, (0, units), (0, width), base + units, 0))
    return copies


def attend_backward(operands, parts, extras):
    grad, resid, seen, qkv, mixed, total, w_qkv, w_out, gains, vectors = operands
    rows, width = grad.shape
    half = width // 2
    span = mixed.shape[0]
    inputs = [("load", value) for value in operands]
    scratch = [
        pltpu.VMEM((2 * rows, width), BF),
        pltpu.VMEM((span, 2 * rows), BF),
        pltpu.VMEM((3 * span, 2 * rows), BF),
        pltpu.VMEM((8, 128), F32),
        pltpu.VMEM((8, 128), F32),
    ]
    scratch += total_scratch(rows, width) + total_sems(rows) + [pair_sems(1)]
    copies = feed_copies(0, 0, parts[1].shape[0], width)
    inputs += [("hbm", value) for value in parts]
    scratch += [pltpu.SemaphoreType.DMA((len(copies),))] + scatter_scratch(FEED_CHUNKS, width)
    if extras:
        inputs += [("load", value) for value in extras[:4]] + [("hbm", extras[4])]
        outs = [((rows, half), BF)] * 2
        for chunks in (LAYER_CHUNKS, FEED_CHUNKS, ATTEND_CHUNKS):
            outs.append(((2, len(chunks) * UNIT, half), BF))
        outs.append(((2, 16, half), F32))
        scratch += [pltpu.VMEM((rows, width), BF)] * 3 + [pair_sems(12)]
        scratch += [pltpu.VMEM((16, width), F32)] + [pltpu.VMEM((3, 16, width), F32)] * 2
        scratch += [pltpu.VMEM((2, 16, width), F32), pltpu.VMEM((16, half), F32), pair_sems(8)]
        scratch += scatter_scratch(ATTEND_CHUNKS, width)
        scratch += gather_scratch(LAYER_CHUNKS) + gather_scratch(FEED_CHUNKS) + gather_scratch(ATTEND_CHUNKS)
    else:
        outs = [
            ((rows, width), F32),
            ((3 * span, width), BF),
            ((span, width), BF),
            ((16, width), BF),
            ((16 * len(FEED_CHUNKS), half), BF),
        ]
    return call(
        functools.partial(attend_backward_kernel, {"last": bool(extras), "copies": copies}),
        "attend_backward_last" if extras else "attend_backward",
        1 if extras else 6,
        inputs,
        [("early", out) for out in outs],
        scratch,
    )


def finish_kernel(*refs):
    layer_load, feed_load, tail_load, vec_load, token_load, result_load = refs[:6]
    token_ref, result_ref, up_out, down_out, q_out, k_out, v_out, out_out, bias_out = refs[6:15]
    one_gain_out, one_shift_out, query_out, key_out, two_gain_out, two_shift_out, down_bias_out = refs[15:22]
    up_stage, down_stage, square_stage, token_stage, store_sems = refs[22:27]
    units, half = down_out.shape[1] // 2, down_out.shape[2]
    span = q_out.shape[2] // 2
    stores = []

    def store(stage, target):
        copy = pltpu.make_async_copy(stage, target, store_sems.at[len(stores)])
        copy.start()
        stores.append(copy)

    def finish_feed(layer, both, base):
        for spot in range(2):
            for part in range(units // half):
                up_stage[layer, :, pl.ds(spot * units + part * half, half)] = both[
                    spot, pl.ds(base + part * half, half), :
                ].astype(F32)
            down_stage[layer, pl.ds(spot * units, units), :] = both[
                spot, pl.ds(base + units, units), :
            ].astype(F32)
        store(up_stage.at[layer], up_out.at[layer])
        store(down_stage.at[layer], down_out.at[layer])

    def finish_attend(layer, both, base):
        for at, target in enumerate((q_out, k_out, v_out, out_out)):
            here = pl.ds(base + at * span, span)
            value = jnp.concatenate((both[0, here, :], both[1, here, :]), axis=0).astype(F32)
            square_stage[layer, at] = value if at == 3 else value.T
            store(square_stage.at[layer, at], target.at[layer])

    layer_both = layer_load()
    finish_feed(1, layer_both, 0)
    finish_attend(1, layer_both, 2 * units)
    finish_feed(0, feed_load(), 0)
    finish_attend(0, tail_load(), 0)
    token_stage[...] = token_load()[...].astype(F32)
    store(token_stage, token_ref)
    store(result_load(), result_ref)
    small_at = 2 * units + 4 * span
    vec = vec_load()
    for layer in range(2):
        if layer == 1:
            one = [layer_both[spot, pl.ds(small_at, 16), :].astype(F32) for spot in range(2)]
            two = [layer_both[spot, pl.ds(small_at + 16, 16), :].astype(F32) for spot in range(2)]
        else:
            one = [vec[spot, 0:8, :] for spot in range(2)]
            two = [vec[spot, 8:16, :] for spot in range(2)]
        for spot in range(2):
            for part in range(units // half):
                bias_out[layer : layer + 1, pl.ds(spot * units + part * half, half)] = two[spot][
                    3 + part : 4 + part
                ]
        for row, ref in enumerate((one_gain_out, one_shift_out, query_out, key_out)):
            ref[layer : layer + 1, :] = (one[0] + one[1])[row : row + 1, 0 : ref.shape[1]]
        for row, ref in enumerate((two_gain_out, two_shift_out, down_bias_out)):
            ref[layer : layer + 1, :] = (two[0] + two[1])[row : row + 1]
    for copy in stores:
        copy.wait()


def finish(values, units, span):
    rows, half = values[4].shape
    heads = 2 * span
    shapes = [(half, 2 * units), (2 * units, half)] + [(half, heads)] * 3 + [(heads, half)]
    outs = [("hbm", ((rows, half), F32)), ("hbm", ((rows, half), BF))]
    outs += [("hbm", ((2,) + shape, F32)) for shape in shapes]
    outs += [((2, size), F32) for size in (2 * units, half, half, HEAD_DIM, HEAD_DIM, half, half, half)]
    return call(
        finish_kernel,
        "finish",
        None,
        [("load", value) for value in values],
        outs,
        [
            pltpu.VMEM((2,) + shapes[0], F32),
            pltpu.VMEM((2,) + shapes[1], F32),
            pltpu.VMEM((2, 4, heads, half), F32),
            pltpu.VMEM((rows, half), F32),
            pltpu.SemaphoreType.DMA((14,)),
        ],
    )


def shards(
    tokens, ln1_gain, ln1_shift, w_query, w_key, w_value, query_gain, key_gain, w_out,
    ln2_gain, ln2_shift, w_up, up_bias, w_down, down_bias, cotangent,
):
    resid, w_qkv, later, vectors, gains = arrive(
        tokens, w_query, w_key, w_value,
        (ln1_gain, ln1_shift, ln2_gain, ln2_shift, down_bias, query_gain, key_gain),
    )
    caches, raws = [], (w_out, w_up, w_down)
    for at in range(2):
        last = at == 1
        resid_two, seen_one, qkv, mixed, total, *fetched = attend_forward(
            at, resid, w_qkv, gains, vectors, raws
        )
        out_here = fetched[0]
        if at == 0:
            up_here, down_here = fetched[1:]
        result, seen_two, active, slope, *side = feed_forward(
            at, last, resid_two, up_here, up_bias, down_here, vectors, cotangent if last else later, raws
        )
        caches.append(
            (
                (resid_two, seen_two, active, slope, up_here, down_here, vectors),
                (resid, seen_one, qkv, mixed, total, w_qkv, out_here, gains, vectors),
            )
        )
        if not last:
            resid = result
            w_qkv, up_here, down_here = side
    grad, low = side
    grad, grad_up, grad_down, small_two = feed_backward((grad,) + caches[1][0], ())
    grad, grad_qkv, grad_out, small_one, shard = attend_backward(
        (grad,) + caches[1][1], (grad_up, grad_down), ()
    )
    grad, grad_up, grad_down, small_zero, other_shard = feed_backward(
        (grad,) + caches[0][0], (grad_qkv, grad_out, small_one, small_two)
    )
    out, low_grad, layer_both, feed_both, tail_both, vec = attend_backward(
        (grad,) + caches[0][1], (grad_up, grad_down), (shard, other_shard, small_zero, result, low)
    )
    (
        grad_tokens, out, grad_up, grad_down, grad_q, grad_k, grad_v, grad_out, grad_up_bias,
        grad_one_gain, grad_one_shift, grad_query_gain, grad_key_gain,
        grad_two_gain, grad_two_shift, grad_down_bias,
    ) = finish((layer_both, feed_both, tail_both, vec, low_grad, out), w_up.shape[2] // 2, w_query.shape[2] // 2)
    return (
        out, grad_tokens, grad_one_gain, grad_one_shift, grad_q, grad_k, grad_v,
        grad_query_gain, grad_key_gain, grad_out, grad_two_gain, grad_two_shift,
        grad_up, grad_up_bias, grad_down, grad_down_bias,
    )


def solution(mesh):
    fine = Mesh(mesh.devices.reshape(4, 4, 2, 2, 2), ("x", "z", "core", "row", "col"))
    rows = ("x", "z", "core", "row")
    in_specs = (
        P(rows, "col"),
        P(None, "col"),
        P(None, "col"),
        P(None, "col", "row"),
        P(None, "col", "row"),
        P(None, "col", "row"),
        P(),
        P(),
        P(None, "row", "col"),
        P(None, "col"),
        P(None, "col"),
        P(None, "col", "row"),
        P(None, "row"),
        P(None, "row", "col"),
        P(None, "col"),
        P(rows, "col"),
    )
    out_specs = (P(rows, "col"),) * 2 + in_specs[1:15]
    return jax.shard_map(shards, mesh=fine, in_specs=in_specs, out_specs=out_specs, check_vma=False)
```
